128 devices in a mesh: bx: 16 (over x, y), by: 8 (over z, core).
Axes of the slice: x: 4, y: 4, z: 4, core: 2. Of those that a mesh axis runs over, the one named last changes fastest.
Arguments:
- tracers: float32 [4, 12, 2048, 2048], P(None, None, 'bx', 'by'), may hold values from -6 to 6
- velocity: float32 [2, 12, 2048, 2048], P(None, None, 'bx', 'by'), may hold values from -0.2 to 0.2
- ocean: int32 [2048, 2048], P('bx', 'by'), may hold values 0 or 1
- thickness: float32 [12], replicated, may hold values from 0.5 to 2
- depth: float32 [2048, 2048], P('bx', 'by'), may hold values from 0.25 to 10, as said below
Outputs:
- new_tracers: float32 [4, 12, 2048, 2048], P(None, None, 'bx', 'by')
- surface_pressure: float32 [2048, 2048], P(('bx', 'by'))
The draws below stay inside these ranges and needn't reach their ends.
Inputs may be any that keep to these rules, and one draw needn't show every extreme that they name: depth is positive.
All inputs are finite; a program needn't handle non-finite values. No bound on the sum of `ocean` on one device may be relied on, other than what follows from the above.
Results may differ from the reference program's by a relative error of at most 0.00002.
Values sent between devices are 32-bit elements; how exact they have to be, the bound alone decides.
No kernel may reach another device: no remote copies, remote signals or barrier semaphores. Data moves between devices by JAX's collectives and lax.ppermute only.
A program may use at most 128 MiB of HBM per device.

```python
import math
import jax
import jax.numpy as jnp
from jax import lax

TRACERS = 4
LEVELS = 12
ITERS = 3
NX = 2048
NY = 2048


def draw_depth(key, part):
    key = jax.random.fold_in(key, 11)
    key_base = jax.random.fold_in(key, 1)
    key_row = jax.random.fold_in(key, 2)
    key_col = jax.random.fold_in(key, 3)
    center_row = jax.random.uniform(key_row, (), jnp.float32, 0.0, 1.0)
    center_col = jax.random.uniform(key_col, (), jnp.float32, 0.0, 1.0)
    rows = (jnp.arange(NX, dtype=jnp.float32)[:, None] + 0.5) / NX
    cols = (jnp.arange(NY, dtype=jnp.float32)[None, :] + 0.5) / NY
    spread = 0.25
    reach = ((rows - center_row) / spread) ** 2 + ((cols - center_col) / spread) ** 2
    bump = 1.0 + 3.0 * jnp.exp(-0.5 * reach)
    base = jnp.exp(jax.random.uniform(key_base, (NX, NY), jnp.float32, math.log(0.5), math.log(2.0)))
    return (base * bump).astype(jnp.float32)


def with_ends(array, rng, least, largest):
    longest = array.shape.index(max(array.shape))
    spots = []
    for shift in (0, 1):
        where = [jax.random.randint(jax.random.fold_in(rng, axis), (), 0, length) for axis, length in enumerate(array.shape)]
        where[longest] = (where[longest] + shift) % array.shape[longest]
        spots.append(tuple(where))
    return array.at[spots[0]].set(least).at[spots[1]].set(largest)


def block_scale(rng, extent, shards, low, high):
    loudness = 1.0
    for axis_at, blocks in shards:
        steps = jax.random.uniform(jax.random.fold_in(jax.random.fold_in(rng, 6), axis_at), (blocks,), jnp.float32, low / len(shards), high / len(shards))
        loudness = loudness * jnp.repeat(jnp.exp(steps), extent[axis_at] // blocks).reshape((-1,) + (1,) * (len(extent) - 1 - axis_at))
    return loudness


def gaussian(key, shape, deviation, most, shards=(), held_as=jnp.bfloat16):
    entries = deviation * jax.random.normal(key, shape, jnp.float32)
    if shards:
        entries = entries * block_scale(key, shape, shards, -0.22, 0.18)
    return jnp.clip(entries, -most, most).astype(held_as)


def setup_inputs(seed: int = 0) -> dict:
    splits = jax.random.split(jax.random.key(seed), 6)
    return {
        "tracers": gaussian(splits[0], (TRACERS, LEVELS, NX, NY), 1.0, 6.0, ((2, 16), (3, 8)), jnp.float32),
        "velocity": jnp.clip(jax.random.uniform(splits[1], (2, LEVELS, NX, NY), jnp.float32, -0.2, 0.2) * block_scale(splits[1], (2, LEVELS, NX, NY), ((2, 16), (3, 8)), -0.4, 0.0), -0.2, 0.2),
        "ocean": with_ends((jax.random.randint(splits[2], (NX, NY), 0, 8) < 7).astype(jnp.int32), jax.random.fold_in(splits[2], 1), 0, 1),
        "thickness": jnp.clip(jnp.exp(jax.random.uniform(splits[3], (LEVELS,), jnp.float32, math.log(0.5), math.log(2.0))), 0.5, 2.0),
        "depth": draw_depth(jax.random.fold_in(splits[5], 71), 0),
    }


NEIGHBOURS = ((1, 0, 0.5), (-1, 0, 0.5), (0, 1, 0.5), (0, -1, 0.5), (1, 1, 0.125), (1, -1, 0.125), (-1, 1, 0.125), (-1, -1, 0.125))


def face_flux(speed, here, ahead, wet_here, wet_ahead):
    return (jnp.maximum(speed, 0.0) * here + jnp.minimum(speed, 0.0) * ahead) * (wet_here * wet_ahead)


def shifted_ahead(field, axis):
    size = field.shape[axis]
    rest = lax.slice_in_dim(field, 1, size, axis=axis)
    return jnp.concatenate([rest, jnp.zeros_like(lax.slice_in_dim(field, 0, 1, axis=axis))], axis)


def shifted_behind(field, axis):
    size = field.shape[axis]
    rest = lax.slice_in_dim(field, 0, size - 1, axis=axis)
    return jnp.concatenate([jnp.zeros_like(lax.slice_in_dim(field, 0, 1, axis=axis)), rest], axis)


def operate(padded_p, padded_h):
    rows = padded_p.shape[0] - 2
    cols = padded_p.shape[1] - 2
    center_p = padded_p[1:rows + 1, 1:cols + 1]
    center_h = padded_h[1:rows + 1, 1:cols + 1]
    result = 0.5 * center_p
    for step_a, step_b, weight in NEIGHBOURS:
        near_p = padded_p[1 + step_a:rows + 1 + step_a, 1 + step_b:cols + 1 + step_b]
        near_h = padded_h[1 + step_a:rows + 1 + step_a, 1 + step_b:cols + 1 + step_b]
        result = result + weight * (center_h + near_h) * (center_p - near_p)
    return result


def chebyshev(rhs, apply_fn, lam_max, keep):
    theta = (lam_max + 0.5) / 2.0
    delta = (lam_max - 0.5) / 2.0
    sigma = theta / delta
    rho = 1.0 / sigma
    resid = rhs
    direction = rhs / theta * keep
    solution = jnp.zeros_like(rhs)
    for step in range(ITERS):
        resid = resid - apply_fn(direction)
        solution = solution + direction
        rho_next = 1.0 / (2.0 * sigma - rho)
        direction = (rho_next * rho * direction + (2.0 * rho_next / delta) * resid) * keep
        rho = rho_next
    return solution + direction


def reference(tracers, velocity, ocean, thickness, depth):
    wet = ocean.astype(jnp.float32)
    total = tracers
    for axis, speed in ((2, velocity[0]), (3, velocity[1])):
        ahead = shifted_ahead(tracers, axis)
        wet_ahead = shifted_ahead(wet, axis - 2)
        flux = face_flux(speed[None], tracers, ahead, wet, wet_ahead)
        total = total - (flux - shifted_behind(flux, axis))
    new_tracers = total
    forcing = wet * jnp.sum(thickness[:, None, None] * (0.2 * new_tracers[0] - 0.8 * new_tracers[1]), axis=0)
    coefficient = depth * (0.1 + 0.9 * wet)
    lam_max = 0.5 + 10.0 * jnp.max(coefficient)
    padded_h = jnp.pad(coefficient, 1)

    def apply_fn(direction):
        return operate(jnp.pad(direction, 1), padded_h)

    surface_pressure = chebyshev(forcing, apply_fn, lam_max, 1.0)
    return new_tracers, surface_pressure
```

```python
import functools

import jax
import jax.numpy as jnp
from jax import lax
from jax.experimental import pallas as pl
from jax.experimental.pallas import tpu as pltpu
from jax.sharding import PartitionSpec as P

ITERS = 3
TRACERS = 4
LEVELS = 12
ROWS = 128
COLS = 256
TILES = ROWS // 8
LANE = 128
WET = 60
VMEM = pl.BlockSpec(memory_space=pltpu.VMEM)
SMEM = pl.BlockSpec(memory_space=pltpu.SMEM)


def lanes(shape):
    return lax.broadcasted_iota(jnp.int32, shape, len(shape) - 1)


def sublanes(shape):
    return lax.broadcasted_iota(jnp.int32, shape, len(shape) - 2)


def pack_kernel(t_ref, v_ref, ocean_ref, depth_ref, row_hi, row_lo, col_hi, col_lo, top, wet_out, coef_out):
    k = pl.program_id(0)
    lane = lanes((ROWS, LANE))

    @pl.when(k == 0)
    def _():
        wet = ocean_ref[...].astype(jnp.float32)
        coef = depth_ref[...] * (0.1 + 0.9 * wet)
        wet_out[...] = wet
        coef_out[...] = coef
        most = jnp.max(jnp.max(coef, axis=0, keepdims=True), axis=1, keepdims=True)
        top[...] = jnp.broadcast_to(most[None], top.shape)
        row_hi[...] = jnp.zeros(row_hi.shape, jnp.float32)
        row_lo[...] = jnp.zeros(row_lo.shape, jnp.float32)
        row_hi[pl.ds(WET, 1), :] = wet[ROWS - 1 : ROWS, :]
        row_lo[pl.ds(WET, 1), :] = wet[0:1, :]
        col_hi[...] = jnp.where(lane == WET, pltpu.roll(wet[:, LANE:], WET + 1, 1), 0.0)
        col_lo[...] = jnp.where(lane == WET, pltpu.roll(wet[:, :LANE], WET, 1), 0.0)

    hi = col_hi[...]
    lo = col_lo[...]
    for t in range(TRACERS):
        slot = t * LEVELS + k
        row_hi[pl.ds(slot, 1), :] = t_ref[t, 0, ROWS - 1 : ROWS, :]
        row_lo[pl.ds(slot, 1), :] = t_ref[t, 0, 0:1, :]
        hi = jnp.where(lane == slot, pltpu.roll(t_ref[t, 0, :, LANE:], slot + 1, 1), hi)
        lo = jnp.where(lane == slot, pltpu.roll(t_ref[t, 0, :, :LANE], slot, 1), lo)
    slot = TRACERS * LEVELS + k
    row_hi[pl.ds(slot, 1), :] = v_ref[0, 0, ROWS - 1 : ROWS, :]
    hi = jnp.where(lane == slot, pltpu.roll(v_ref[1, 0, :, LANE:], slot + 1, 1), hi)
    col_hi[...] = hi
    col_lo[...] = lo


def pack(tracers, velocity, ocean, depth):
    whole = lambda *shape: pl.BlockSpec(shape, lambda k: (0,) * len(shape))
    f32 = lambda *shape: jax.ShapeDtypeStruct(shape, jnp.float32)
    shapes = ((64, COLS), (64, COLS), (ROWS, LANE), (ROWS, LANE), (16, 8, LANE), (ROWS, COLS), (ROWS, COLS))
    return pl.pallas_call(
        pack_kernel,
        grid=(LEVELS,),
        in_specs=[
            pl.BlockSpec((TRACERS, 1, ROWS, COLS), lambda k: (0, k, 0, 0)),
            pl.BlockSpec((2, 1, ROWS, COLS), lambda k: (0, k, 0, 0)),
            whole(ROWS, COLS),
            whole(ROWS, COLS),
        ],
        out_specs=[whole(*s) for s in shapes],
        out_shape=[f32(*s) for s in shapes],
        cost_estimate=pl.CostEstimate(flops=4_000_000, bytes_accessed=9_400_000, transcendentals=0),
        name="pack_edges",
    )(tracers, velocity, ocean, depth)


def sided(x, edge_lo, edge_hi):
    lane = lanes((8, LANE))
    a, b = x[:, :LANE], x[:, LANE:]
    ra, rb = pltpu.roll(a, 1, 1), pltpu.roll(b, 1, 1)
    sa, sb = pltpu.roll(a, LANE - 1, 1), pltpu.roll(b, LANE - 1, 1)
    behind = jnp.concatenate([jnp.where(lane == 0, edge_lo, ra), jnp.where(lane == 0, ra, rb)], 1)
    ahead = jnp.concatenate([jnp.where(lane == LANE - 1, sb, sa), jnp.where(lane == LANE - 1, edge_hi, sb)], 1)
    return behind, ahead


def below(load, edge, r):
    if r:
        return load(8 * r - 1)
    return jnp.where(sublanes((8, COLS)) == 0, edge, pltpu.roll(load(0), 1, 0))


def above(load, edge, r):
    if r < TILES - 1:
        return load(8 * r + 1)
    return jnp.where(sublanes((8, COLS)) == 7, edge, pltpu.roll(load(8 * r), 7, 0))


def advect_kernel(first, *refs):
    if first == 0:
        (thick, t_ref, v_ref, wet_ref, row_lo, row_hi, col_lo, col_hi, coef_ref, tops_ref, out_ref, send_ref, w_e, w_w, w_n, w_s, total) = refs
    else:
        (t_ref, v_ref, wet_ref, row_lo, row_hi, col_lo, col_hi, _, out_ref, w_e, w_w, w_n, w_s) = refs
    k = pl.program_id(0)

    @pl.when(k == 0)
    def _():
        load = lambda at: wet_ref[at : at + 8, :]
        for r in range(TILES):
            rows = pl.ds(8 * r, 8)
            here = load(8 * r)
            w_e[rows, :] = here * above(load, row_hi[WET : WET + 1, :], r)
            w_w[rows, :] = here * below(load, row_lo[WET : WET + 1, :], r)
            edge_lo = pltpu.roll(col_lo[rows, :], LANE - WET, 1)
            edge_hi = pltpu.roll(col_hi[rows, :], LANE - 1 - WET, 1)
            behind, ahead = sided(here, edge_lo, edge_hi)
            w_n[rows, :] = here * ahead
            w_s[rows, :] = here * behind
        if first == 0:
            total[...] = jnp.zeros(total.shape, jnp.float32)

    speed_slot = TRACERS * LEVELS + k
    before_u = row_lo[pl.ds(speed_slot, 1), :]
    for r in range(TILES):
        rows = pl.ds(8 * r, 8)
        load_u = lambda at: v_ref[0, 0, at : at + 8, :]
        u = load_u(8 * r)
        u_behind = below(load_u, before_u, r)
        v = v_ref[1, 0, rows, :]
        lo_tile = col_lo[rows, :]
        hi_tile = col_hi[rows, :]
        v_edge = pltpu.roll(lo_tile, LANE - speed_slot, 1)
        lane = lanes((8, LANE))
        va, vb = pltpu.roll(v[:, :LANE], 1, 1), pltpu.roll(v[:, LANE:], 1, 1)
        v_behind = jnp.concatenate([jnp.where(lane == 0, v_edge, va), jnp.where(lane == 0, va, vb)], 1)
        we, ww, wn, ws = w_e[rows, :], w_w[rows, :], w_n[rows, :], w_s[rows, :]
        ahead_x = jnp.minimum(u, 0.0) * we
        behind_x = jnp.maximum(u_behind, 0.0) * ww
        ahead_y = jnp.minimum(v, 0.0) * wn
        behind_y = jnp.maximum(v_behind, 0.0) * ws
        center = (1.0 - (jnp.maximum(u, 0.0) * we - jnp.minimum(u_behind, 0.0) * ww)) - (
            jnp.maximum(v, 0.0) * wn - jnp.minimum(v_behind, 0.0) * ws
        )
        new = []
        for t in range(2):
            load = lambda at: t_ref[t, 0, at : at + 8, :]
            slot = (first + t) * LEVELS + k
            c = load(8 * r)
            c_below = below(load, row_lo[pl.ds(slot, 1), :], r)
            c_above = above(load, row_hi[pl.ds(slot, 1), :], r)
            edge_lo = pltpu.roll(lo_tile, LANE - slot, 1)
            edge_hi = pltpu.roll(hi_tile, LANE - 1 - slot, 1)
            c_behind, c_ahead = sided(c, edge_lo, edge_hi)
            value = center * c - (ahead_x * c_above - behind_x * c_below) - (ahead_y * c_ahead - behind_y * c_behind)
            out_ref[t, 0, rows, :] = value
            new.append(value)
        if first == 0:
            total[rows, :] = total[rows, :] + thick[k] * (0.2 * new[0] - 0.8 * new[1])

    if first == 0:

        @pl.when(k == LEVELS - 1)
        def _():
            most = jnp.max(tops_ref[...], axis=0)
            for j in range(8):
                rows = pl.ds(16 * j, 16)
                send_ref[j, 0:16, :] = total[rows, :] * wet_ref[rows, :]
                send_ref[j, 16:32, :] = coef_ref[rows, :]
                send_ref[j, 32:40, :LANE] = most
                send_ref[j, 32:40, LANE:] = most


def advect(first, tracers, velocity, wet, row_lo, row_hi, col_lo, col_hi, extra):
    whole = lambda *shape: pl.BlockSpec(shape, lambda k: (0,) * len(shape))
    half = first // 2
    ins = [
        pl.BlockSpec((2, 1, ROWS, COLS), lambda k: (half, k, 0, 0)),
        pl.BlockSpec((2, 1, ROWS, COLS), lambda k: (0, k, 0, 0)),
        whole(ROWS, COLS),
        whole(64, COLS),
        whole(64, COLS),
        whole(ROWS, LANE),
        whole(ROWS, LANE),
    ]
    operands = [tracers, velocity, wet, row_lo, row_hi, col_lo, col_hi]
    out_specs = [pl.BlockSpec((2, 1, ROWS, COLS), lambda k: (half, k, 0, 0))]
    out_shape = [jax.ShapeDtypeStruct((TRACERS, LEVELS, ROWS, COLS), jnp.float32)]
    scratch = [pltpu.VMEM((ROWS, COLS), jnp.float32)] * 4
    aliases = {}
    if first == 0:
        thickness, coef, tops = extra
        ins = [SMEM] + ins + [whole(ROWS, COLS), whole(16, 8, LANE)]
        operands = [thickness] + operands + [coef, tops]
        out_specs.append(whole(8, 40, COLS))
        out_shape.append(jax.ShapeDtypeStruct((8, 40, COLS), jnp.float32))
        scratch.append(pltpu.VMEM((ROWS, COLS), jnp.float32))
    else:
        aliases = {len(operands): 0}
        ins = ins + [pl.BlockSpec(memory_space=pl.ANY)]
        operands = operands + [extra]
    return pl.pallas_call(
        functools.partial(advect_kernel, first),
        grid=(LEVELS,),
        in_specs=ins,
        out_specs=out_specs,
        out_shape=out_shape,
        scratch_shapes=scratch,
        input_output_aliases=aliases,
        cost_estimate=pl.CostEstimate(flops=24_000_000, bytes_accessed=9_400_000, transcendentals=0),
        name="advect_forcing" if first == 0 else "advect_rest",
    )(*operands)


def strip_kernel(got_ref, strip_ref, down_ref, up_ref):
    for j in range(8):
        cols = pl.ds(j * COLS, COLS)
        strip_ref[0, :, cols] = got_ref[j, 0:16, :]
        strip_ref[1, :, cols] = got_ref[j, 16:32, :]
        down_ref[0:4, cols] = got_ref[j, 0:4, :]
        down_ref[4:8, cols] = got_ref[j, 16:20, :]
        up_ref[0:4, cols] = got_ref[j, 12:16, :]
        up_ref[4:8, cols] = got_ref[j, 28:32, :]


def strips(got):
    f32 = lambda *shape: jax.ShapeDtypeStruct(shape, jnp.float32)
    return pl.pallas_call(
        strip_kernel,
        in_specs=[VMEM],
        out_specs=[VMEM] * 3,
        out_shape=[f32(2, 16, 8 * COLS), f32(8, 8 * COLS), f32(8, 8 * COLS)],
        cost_estimate=pl.CostEstimate(flops=1000, bytes_accessed=600_000, transcendentals=0),
        name="strip_rows",
    )(got)


WIDE = 8 * COLS
EXT = 24
NEAR = ((1, 0, 0.5), (-1, 0, 0.5), (0, 1, 0.5), (0, -1, 0.5), (1, 1, 0.125), (1, -1, 0.125), (-1, 1, 0.125), (-1, -1, 0.125))


def moved(x, rows, cols):
    if cols:
        lane = lanes(x.shape)
        x = pltpu.roll(x, (-cols) % x.shape[1], 1)
        x = jnp.where(lane == (x.shape[1] - 1 if cols > 0 else 0), 0.0, x)
    if rows:
        x = pltpu.roll(x, (-rows) % x.shape[0], 0)
    return x


def solve_kernel(got_ref, strip_ref, before_ref, after_ref, out_ref, h_ref, p_ref, weight):
    h_ref[0:4, :] = before_ref[4:8, :]
    h_ref[4:20, :] = strip_ref[1]
    h_ref[20:24, :] = after_ref[4:8, :]
    p_ref[0:4, :] = before_ref[0:4, :]
    p_ref[4:20, :] = strip_ref[0]
    p_ref[20:24, :] = after_ref[0:4, :]
    most = jnp.max(got_ref[:, 32:40, 0:LANE], axis=0)[0:1, 0:1]
    lam_max = 0.5 + 10.0 * most
    theta = (lam_max + 0.5) / 2.0
    delta = (lam_max - 0.5) / 2.0
    sigma = theta / delta
    rho = 1.0 / sigma
    h = h_ref[...]
    sides = {c: moved(h, 0, c) for c in (-1, 0, 1)}
    for n, (a, b, w) in enumerate(NEAR):
        weight[n] = w * (h + moved(sides[b], a, 0))
    inside = h > 0.0
    resid = p_ref[...]
    direction = resid / theta
    answer = jnp.zeros_like(resid)
    for _ in range(ITERS):
        sides = {c: moved(direction, 0, c) for c in (-1, 0, 1)}
        applied = 0.5 * direction
        for n, (a, b, w) in enumerate(NEAR):
            applied = applied + weight[n] * (direction - moved(sides[b], a, 0))
        resid = jnp.where(inside, resid - applied, 0.0)
        answer = answer + direction
        rho_next = 1.0 / (2.0 * sigma - rho)
        direction = rho_next * rho * direction + (2.0 * rho_next / delta) * resid
        rho = rho_next
    out_ref[...] = (answer + direction)[4:20, :]


def solve(got, strip, before, after):
    return pl.pallas_call(
        solve_kernel,
        in_specs=[VMEM] * 4,
        out_specs=VMEM,
        out_shape=jax.ShapeDtypeStruct((16, WIDE), jnp.float32),
        scratch_shapes=[
            pltpu.VMEM((EXT, WIDE), jnp.float32),
            pltpu.VMEM((EXT, WIDE), jnp.float32),
            pltpu.VMEM((8, EXT, WIDE), jnp.float32),
        ],
        cost_estimate=pl.CostEstimate(flops=6_000_000, bytes_accessed=600_000, transcendentals=0),
        name="chebyshev",
    )(got, strip, before, after)


def send(x, axes, count, step):
    pairs = [(i, i + step) for i in range(count) if 0 <= i + step < count]
    return lax.ppermute(x, axes, pairs)


def shards(tracers, velocity, ocean, thickness, depth):
    nx, ny = lax.axis_size("bx"), lax.axis_size("by")
    row_hi, row_lo, col_hi, col_lo, top, wet, coef = pack(tracers, velocity, ocean, depth)
    before_row = send(row_hi, "bx", nx, 1)
    after_row = send(row_lo, "bx", nx, -1)
    before_col = send(col_hi, "by", ny, 1)
    after_col = send(col_lo, "by", ny, -1)
    tops = lax.all_to_all(top, "bx", split_axis=0, concat_axis=0, tiled=True)
    halos = (wet, before_row, after_row, before_col, after_col)
    part, parcels = advect(0, tracers, velocity, *halos, (thickness, coef, tops))
    got = lax.all_to_all(parcels, "by", split_axis=0, concat_axis=0, tiled=True)
    new_tracers = advect(2, tracers, velocity, *halos, part)[0]
    strip, down, up = strips(got)
    both = ("bx", "by")
    before = send(up, both, nx * ny, 1)
    after = send(down, both, nx * ny, -1)
    return new_tracers, solve(got, strip, before, after)


def solution(mesh):
    return jax.shard_map(
        shards,
        mesh=mesh,
        in_specs=(
            P(None, None, "bx", "by"),
            P(None, None, "bx", "by"),
            P("bx", "by"),
            P(),
            P("bx", "by"),
        ),
        out_specs=(P(None, None, "bx", "by"), P(("bx", "by"), None)),
        check_vma=False,
    )
```

```python
import functools

import jax
import jax.numpy as jnp
from jax import lax
from jax.experimental import pallas as pl
from jax.experimental.pallas import tpu as pltpu
from jax.sharding import PartitionSpec as P

ITERS = 3
TRACERS = 4
LEVELS = 12
ROWS = 128
COLS = 256
TILES = ROWS // 8
LANE = 128
WIDE = 8 * COLS
EXT = 24
CHUNK = 32

SPEED, WET, PART, COEF, EDGE, MESSAGE = 48, 60, 64, 68, 72, 80
ANY = pl.BlockSpec(memory_space=pl.ANY)
VMEM = pl.BlockSpec(memory_space=pltpu.VMEM)
SMEM = pl.BlockSpec(memory_space=pltpu.SMEM)


def f32(*shape):
    return jax.ShapeDtypeStruct(shape, jnp.float32)


def lanes(shape):
    return lax.broadcasted_iota(jnp.int32, shape, len(shape) - 1)


def sublanes(shape):
    return lax.broadcasted_iota(jnp.int32, shape, len(shape) - 2)


def coefficient(depth, wet):
    return depth * (0.1 + 0.9 * wet)


def positive(x):
    return jnp.maximum(x, 0.0)


def negative(x):
    return jnp.minimum(x, 0.0)


def edge_forcing(q, u, v, wet, thick):
    shape = (8, COLS)
    row, col = sublanes(shape), lanes(shape)
    total = jnp.zeros(shape, jnp.float32)
    flux_x = jnp.zeros(shape, jnp.float32)
    flux_y = jnp.zeros(shape, jnp.float32)
    for k in range(LEVELS):
        depth = thick[k]
        total = total + depth * q[k]
        flux_x = flux_x + depth * (positive(u[k]) * q[k] + negative(u[k]) * pltpu.roll(q[k], 7, 0))
        flux_y = flux_y + depth * (positive(v[k]) * q[k] + negative(v[k]) * pltpu.roll(q[k], COLS - 1, 1))
    flux_x = flux_x * jnp.where(row == 7, 0.0, wet * pltpu.roll(wet, 7, 0))
    flux_y = flux_y * jnp.where(col == COLS - 1, 0.0, wet * pltpu.roll(wet, COLS - 1, 1))
    return wet * (total - (flux_x - pltpu.roll(flux_x, 1, 0)) - (flux_y - pltpu.roll(flux_y, 1, 1)))


def edge_terms(q, v, wet, thick):
    lane = lanes((8, LANE))
    last, first = wet[:, LANE:], wet[:, :LANE]
    upwind = jnp.zeros((8, LANE), jnp.float32)
    terms = jnp.where(lane == 28, pltpu.roll(first, 28, 1), 0.0)
    for k in range(LEVELS):
        depth = thick[k]
        speed = v[k][:, LANE:]
        upwind = upwind + depth * positive(speed) * q[k][:, LANE:]
        terms = jnp.where(lane == k, pltpu.roll(depth * negative(speed) * last, k + 1, 1), terms)
        terms = jnp.where(lane == 16 + k, pltpu.roll(q[k][:, :LANE] * first, 16 + k, 1), terms)
    return jnp.where(lane == LEVELS, pltpu.roll(upwind * last, LEVELS + 1, 1), terms)


def pack_kernel(thick, t_hbm, v_hbm, ocean_hbm, depth_hbm, row_hi, row_lo, col_hi, col_lo, top,
                t_ref, u_top, u_low, v_top, v_low, v_last, ocean_ref, depth_ref, sems):
    def chunk_copy(c):
        rows = pl.ds(pl.multiple_of(c * CHUNK, CHUNK), CHUNK)
        return pltpu.make_async_copy(t_hbm.at[:, :, rows, :], t_ref.at[:, :, rows, :], sems.at[c])

    chunks = ROWS // CHUNK
    small = [
        pltpu.make_async_copy(ocean_hbm, ocean_ref, sems.at[chunks]),
        pltpu.make_async_copy(depth_hbm, depth_ref, sems.at[chunks + 1]),
        pltpu.make_async_copy(v_hbm.at[1, :, :, LANE:], v_last, sems.at[chunks + 2]),
    ]
    tiles = [
        pltpu.make_async_copy(v_hbm.at[0, :, 0:8, :], u_top, sems.at[chunks + 3]),
        pltpu.make_async_copy(v_hbm.at[0, :, ROWS - 8 :, :], u_low, sems.at[chunks + 4]),
        pltpu.make_async_copy(v_hbm.at[1, :, 0:8, :], v_top, sems.at[chunks + 5]),
        pltpu.make_async_copy(v_hbm.at[1, :, ROWS - 8 :, :], v_low, sems.at[chunks + 6]),
    ]
    for copy in small:
        copy.start()
    for c in range(chunks):
        chunk_copy(c).start()
    for copy in tiles:
        copy.start()
    for copy in small:
        copy.wait()
    wet = ocean_ref[...].astype(jnp.float32)
    coef = coefficient(depth_ref[...], wet)
    most = jnp.max(jnp.max(coef, axis=0, keepdims=True), axis=1, keepdims=True)
    top[...] = jnp.broadcast_to(most[None], top.shape)

    def gather(c, _):
        chunk_copy(c).wait()
        lane = lanes((CHUNK, LANE))
        rows = pl.ds(pl.multiple_of(c * CHUNK, CHUNK), CHUNK)
        ocean = ocean_ref[rows, :].astype(jnp.float32)
        hi = jnp.where(lane == 2 * WET, pltpu.roll(ocean[:, LANE:], (2 * WET + 1) % LANE, 1), 0.0)
        lo = jnp.where(lane == 2 * WET - 1, pltpu.roll(ocean[:, :LANE], 2 * WET - 1, 1), 0.0)
        for k in range(LEVELS):
            for t in range(TRACERS):
                s = t * LEVELS + k
                hi = jnp.where(lane == 2 * s, pltpu.roll(t_ref[t, k, rows, LANE:], 2 * s + 1, 1), hi)
                place = (2 * s - 1) % LANE
                lo = jnp.where(lane == place, pltpu.roll(t_ref[t, k, rows, :LANE], place, 1), lo)
            s = SPEED + k
            hi = jnp.where(lane == 2 * s, pltpu.roll(v_last[k, rows, :], 2 * s + 1, 1), hi)
        col_hi[rows, :] = hi
        col_lo[rows, :] = lo
        return 0

    lax.fori_loop(0, chunks, gather, 0)
    for copy in tiles:
        copy.wait()
    for t in range(TRACERS):
        for k in range(LEVELS):
            s = t * LEVELS + k
            row_hi[s : s + 1, :] = t_ref[t, k, ROWS - 1 : ROWS, :]
            row_lo[s : s + 1, :] = t_ref[t, k, 0:1, :]
    for k in range(LEVELS):
        row_hi[SPEED + k : SPEED + k + 1, :] = u_low[k, 7:8, :]
    row_lo[SPEED:WET, :] = jnp.zeros((WET - SPEED, COLS), jnp.float32)
    for row, message, u, v, keep in ((0, row_lo, u_top, v_top, 0), (ROWS - 8, row_hi, u_low, v_low, 4)):
        rows = slice(row, row + 8)
        here = ocean_ref[rows, :].astype(jnp.float32)
        q = [0.2 * t_ref[0, k, rows, :] - 0.8 * t_ref[1, k, rows, :] for k in range(LEVELS)]
        speed_x = [u[k] for k in range(LEVELS)]
        speed_y = [v[k] for k in range(LEVELS)]
        message[WET:PART, :] = jnp.broadcast_to(here[7:8, :] if keep else here[0:1, :], (PART - WET, COLS))
        message[PART:COEF, :] = edge_forcing(q, speed_x, speed_y, here, thick)[keep : keep + 4, :]
        message[COEF:EDGE, :] = coefficient(depth_ref[rows, :], here)[keep : keep + 4, :]
        message[EDGE:MESSAGE, :LANE] = edge_terms(q, speed_y, here, thick)
        message[EDGE:MESSAGE, LANE:] = jnp.zeros((8, LANE), jnp.float32)


def pack(thickness, tracers, velocity, ocean, depth):
    tile = (LEVELS, 8, COLS)
    return pl.pallas_call(
        pack_kernel,
        in_specs=[SMEM, ANY, ANY, ANY, ANY],
        out_specs=[VMEM] * 5,
        out_shape=[f32(MESSAGE, COLS), f32(MESSAGE, COLS), f32(ROWS, LANE), f32(ROWS, LANE), f32(16, 8, LANE)],
        scratch_shapes=[
            pltpu.VMEM((TRACERS, LEVELS, ROWS, COLS), jnp.float32),
            pltpu.VMEM(tile, jnp.float32),
            pltpu.VMEM(tile, jnp.float32),
            pltpu.VMEM(tile, jnp.float32),
            pltpu.VMEM(tile, jnp.float32),
            pltpu.VMEM((LEVELS, ROWS, LANE), jnp.float32),
            pltpu.VMEM((ROWS, COLS), jnp.int32),
            pltpu.VMEM((ROWS, COLS), jnp.float32),
            pltpu.SemaphoreType.DMA((ROWS // CHUNK + 7,)),
        ],
        compiler_params=pltpu.CompilerParams(vmem_limit_bytes=14 * 2**20),
        cost_estimate=pl.CostEstimate(flops=4_000_000, bytes_accessed=7_400_000, transcendentals=0),
        name="pack_edges",
    )(thickness, tracers, velocity, ocean, depth)


def sided(x, edge):
    lane = lanes((8, LANE))
    a, b = x[:, :LANE], x[:, LANE:]
    ra, rb = pltpu.roll(a, 1, 1), pltpu.roll(b, 1, 1)
    sa, sb = pltpu.roll(a, LANE - 1, 1), pltpu.roll(b, LANE - 1, 1)
    behind = jnp.concatenate([jnp.where(lane == 0, edge, ra), jnp.where(lane == 0, ra, rb)], 1)
    ahead = jnp.concatenate([jnp.where(lane == LANE - 1, sb, sa), jnp.where(lane == LANE - 1, edge, sb)], 1)
    return behind, ahead


def below(load, edge, r):
    if r:
        return load(8 * r - 1)
    return jnp.where(sublanes((8, COLS)) == 0, edge, pltpu.roll(load(0), 1, 0))


def above(load, edge, r):
    if r < TILES - 1:
        return load(8 * r + 1)
    return jnp.where(sublanes((8, COLS)) == 7, edge, pltpu.roll(load(8 * r), 7, 0))


def advect_kernel(first, *refs):
    if first == 0:
        (thick, t_hbm, v_hbm, ocean_hbm, row_lo_hbm, row_hi_hbm, col_lo_hbm, col_hi_hbm, depth_hbm, tops_hbm, out_hbm, send_ref,
         t_ref, v_ref, out_ref, ocean_ref, row_lo, row_hi, col_lo, col_hi, w_e, w_w, w_n, w_s, edges, sems, small_sems,
         depth_ref, tops, total, flux, ext) = refs
    else:
        (t_hbm, v_hbm, ocean_hbm, row_lo_hbm, row_hi_hbm, col_lo_hbm, col_hi_hbm, _, out_hbm,
         t_ref, v_ref, out_ref, ocean_ref, row_lo, row_hi, col_lo, col_hi, w_e, w_w, w_n, w_s, edges, sems, small_sems) = refs
    small = [(ocean_hbm, ocean_ref), (row_lo_hbm, row_lo), (row_hi_hbm, row_hi), (col_lo_hbm, col_lo), (col_hi_hbm, col_hi)]
    if first == 0:
        small += [(depth_hbm, depth_ref), (tops_hbm, tops)]
    small = [pltpu.make_async_copy(a, b, small_sems.at[i]) for i, (a, b) in enumerate(small)]

    def tracers_in(k):
        return pltpu.make_async_copy(t_hbm.at[first : first + 2, k], t_ref.at[:, k], sems.at[0, k])

    def velocity_in(k):
        return pltpu.make_async_copy(v_hbm.at[:, k], v_ref.at[:, k], sems.at[1, k])

    def tracers_out(k):
        return pltpu.make_async_copy(out_ref.at[:, k], out_hbm.at[first : first + 2, k], sems.at[2, k])

    for copy in small:
        copy.start()
    for k in range(LEVELS):
        tracers_in(k).start()
        velocity_in(k).start()
    for copy in small:
        copy.wait()
    even = lanes((8, LANE)) % 2 == 0
    load_wet = lambda at: ocean_ref[at : at + 8, :].astype(jnp.float32)
    for r in range(TILES):
        rows = pl.ds(8 * r, 8)
        edge = jnp.where(even, col_lo[rows, :], col_hi[rows, :])
        edges[rows, :] = edge
        here = load_wet(8 * r)
        w_e[rows, :] = here * above(load_wet, row_hi[WET : WET + 1, :], r)
        w_w[rows, :] = here * below(load_wet, row_lo[WET : WET + 1, :], r)
        behind, ahead = sided(here, pltpu.roll(edge, LANE - 2 * WET, 1))
        w_n[rows, :] = here * ahead
        w_s[rows, :] = here * behind
        if first == 0:
            total[rows, :] = jnp.zeros((8, COLS), jnp.float32)
    if first == 0:
        flux[...] = jnp.zeros((8, COLS), jnp.float32)

    def level(k, _):
        tracers_in(k).wait()
        velocity_in(k).wait()
        before_u = row_lo[pl.ds(SPEED + k, 1), :]
        for r in range(TILES):
            rows = pl.ds(8 * r, 8)
            load_u = lambda at: v_ref[0, k, at : at + 8, :]
            u = load_u(8 * r)
            u_behind = below(load_u, before_u, r)
            v = v_ref[1, k, rows, :]
            edge_tile = edges[rows, :]
            lane = lanes((8, LANE))
            va, vb = pltpu.roll(v[:, :LANE], 1, 1), pltpu.roll(v[:, LANE:], 1, 1)
            v_edge = pltpu.roll(edge_tile, LANE - 2 * (SPEED + k), 1)
            v_behind = jnp.concatenate([jnp.where(lane == 0, v_edge, va), jnp.where(lane == 0, va, vb)], 1)
            we, ww, wn, ws = w_e[rows, :], w_w[rows, :], w_n[rows, :], w_s[rows, :]
            ahead_x = negative(u) * we
            behind_x = positive(u_behind) * ww
            ahead_y = negative(v) * wn
            behind_y = positive(v_behind) * ws
            center = (1.0 - (positive(u) * we - negative(u_behind) * ww)) - (positive(v) * wn - negative(v_behind) * ws)
            new = []
            for t in range(2):
                load = lambda at: t_ref[t, k, at : at + 8, :]
                slot = (first + t) * LEVELS + k
                c = load(8 * r)
                c_below = below(load, row_lo[pl.ds(slot, 1), :], r)
                c_above = above(load, row_hi[pl.ds(slot, 1), :], r)
                c_behind, c_ahead = sided(c, pltpu.roll(edge_tile, LANE - 2 * slot, 1))
                value = center * c - (ahead_x * c_above - behind_x * c_below) - (ahead_y * c_ahead - behind_y * c_behind)
                out_ref[t, k, rows, :] = value
                new.append(value)
            if first == 0:
                total[rows, :] = total[rows, :] + thick[k] * (0.2 * new[0] - 0.8 * new[1])
        if first == 0:
            mixed = lambda a, b: 0.2 * a - 0.8 * b
            q_before = mixed(row_lo[pl.ds(k, 1), :], row_lo[pl.ds(LEVELS + k, 1), :])
            q_after = mixed(row_hi[pl.ds(k, 1), :], row_hi[pl.ds(LEVELS + k, 1), :])
            q_first = mixed(t_ref[0, k, 0:1, :], t_ref[1, k, 0:1, :])
            q_last = mixed(t_ref[0, k, ROWS - 1 : ROWS, :], t_ref[1, k, ROWS - 1 : ROWS, :])
            u_last = v_ref[0, k, ROWS - 1 : ROWS, :]
            flux[0:1, :] = flux[0:1, :] + thick[k] * (positive(before_u) * q_before + negative(before_u) * q_first)
            flux[1:2, :] = flux[1:2, :] + thick[k] * (positive(u_last) * q_last + negative(u_last) * q_after)
        tracers_out(k).start()
        return 0

    lax.fori_loop(0, LEVELS, level, 0)

    if first == 0:
        row = sublanes((4, COLS))
        wet_first = load_wet(0)[0:1, :]
        wet_last = load_wet(ROWS - 8)[7:8, :]
        flux_lo = flux[0:1, :] * (row_lo[WET : WET + 1, :] * wet_first)
        flux_hi = flux[1:2, :] * (row_hi[WET : WET + 1, :] * wet_last)
        ext[0, 0:4, :] = row_lo[PART:COEF, :] - jnp.where(row == 3, flux_lo, 0.0)
        ext[0, ROWS + 4 :, :] = row_hi[PART:COEF, :] + jnp.where(row == 0, flux_hi, 0.0)
        ext[1, 0:4, :] = row_lo[COEF:EDGE, :]
        ext[1, ROWS + 4 :, :] = row_hi[COEF:EDGE, :]
        for r in range(TILES):
            rows = pl.ds(8 * r, 8)
            here = load_wet(8 * r)
            ext[0, 8 * r + 4 : 8 * r + 12, :] = total[rows, :] * here
            ext[1, 8 * r + 4 : 8 * r + 12, :] = coefficient(depth_ref[rows, :], here)
        most = jnp.max(tops[...], axis=0)
        tile = sublanes((8, LANE))
        for j in range(8):
            send_ref[j, 0:EXT, :] = ext[0, 16 * j : 16 * j + EXT, :]
            send_ref[j, EXT : 2 * EXT, :] = ext[1, 16 * j : 16 * j + EXT, :]
            edge = jnp.zeros((8, LANE), jnp.float32)
            if j == 0:
                edge = jnp.where((tile >= 1) & (tile <= 3), pltpu.roll(row_lo[EDGE:MESSAGE, :LANE], 4, 0), 0.0)
            if j == 7:
                edge = jnp.where((tile >= 4) & (tile <= 6), pltpu.roll(row_hi[EDGE:MESSAGE, :LANE], 4, 0), 0.0)
            send_ref[j, 2 * EXT : 2 * EXT + 8, :LANE] = edge
            send_ref[j, 2 * EXT : 2 * EXT + 8, LANE:] = most
    for k in range(LEVELS):
        tracers_out(k).wait()


def advect(first, tracers, velocity, ocean, row_lo, row_hi, col_lo, col_hi, extra):
    ins = [ANY] * 7
    operands = [tracers, velocity, ocean, row_lo, row_hi, col_lo, col_hi]
    out_specs = [ANY]
    out_shape = [f32(TRACERS, LEVELS, ROWS, COLS)]
    block = pltpu.VMEM((ROWS, COLS), jnp.float32)
    scratch = [
        pltpu.VMEM((2, LEVELS, ROWS, COLS), jnp.float32),
        pltpu.VMEM((2, LEVELS, ROWS, COLS), jnp.float32),
        pltpu.VMEM((2, LEVELS, ROWS, COLS), jnp.float32),
        pltpu.VMEM((ROWS, COLS), jnp.int32),
        pltpu.VMEM((MESSAGE, COLS), jnp.float32),
        pltpu.VMEM((MESSAGE, COLS), jnp.float32),
        pltpu.VMEM((ROWS, LANE), jnp.float32),
        pltpu.VMEM((ROWS, LANE), jnp.float32),
        block,
        block,
        block,
        block,
        pltpu.VMEM((ROWS, LANE), jnp.float32),
        pltpu.SemaphoreType.DMA((3, LEVELS)),
        pltpu.SemaphoreType.DMA((7,)),
    ]
    aliases = {}
    if first == 0:
        thickness, depth, tops = extra
        ins = [SMEM] + ins + [ANY, ANY]
        operands = [thickness] + operands + [depth, tops]
        out_specs.append(VMEM)
        out_shape.append(f32(8, 2 * EXT + 8, COLS))
        scratch += [
            block,
            pltpu.VMEM((16, 8, LANE), jnp.float32),
            block,
            pltpu.VMEM((8, COLS), jnp.float32),
            pltpu.VMEM((2, ROWS + 8, COLS), jnp.float32),
        ]
    else:
        aliases = {len(operands): 0}
        ins = ins + [ANY]
        operands = operands + [extra]
    return pl.pallas_call(
        functools.partial(advect_kernel, first),
        in_specs=ins,
        out_specs=out_specs,
        out_shape=out_shape,
        scratch_shapes=scratch,
        input_output_aliases=aliases,
        compiler_params=pltpu.CompilerParams(vmem_limit_bytes=16 * 2**20),
        cost_estimate=pl.CostEstimate(flops=24_000_000, bytes_accessed=9_400_000, transcendentals=0),
        name="advect_forcing" if first == 0 else "advect_rest",
    )(*operands)


NEAR = ((1, 0, 0.5), (-1, 0, 0.5), (0, 1, 0.5), (0, -1, 0.5), (1, 1, 0.125), (1, -1, 0.125), (-1, 1, 0.125), (-1, -1, 0.125))


def moved(x, rows, cols):
    if cols:
        lane = lanes(x.shape)
        x = pltpu.roll(x, (-cols) % x.shape[1], 1)
        x = jnp.where(lane == (x.shape[1] - 1 if cols > 0 else 0), 0.0, x)
    if rows:
        x = pltpu.roll(x, (-rows) % x.shape[0], 0)
    return x


def solve_kernel(got_ref, out_ref, h_ref, f_ref, weight):
    for j in range(8):
        cols = pl.ds(j * COLS, COLS)
        f_ref[:, cols] = got_ref[j, 0:EXT, :]
        h_ref[:, cols] = got_ref[j, EXT : 2 * EXT, :]
    lane, tile = lanes((8, LANE)), sublanes((8, LANE))
    edge_rows = pl.ds(2 * EXT, 8)
    for j in range(7):
        pairs = got_ref[j, edge_rows, :LANE] * pltpu.roll(got_ref[j + 1, edge_rows, :LANE], LANE - 16, 1)
        flux = jnp.sum(jnp.where(lane <= LEVELS, pairs, 0.0), axis=1, keepdims=True)
        for rows, there in ((pl.ds(0, 8), tile < 4), (pl.ds(16, 8), tile >= 4)):
            last = pl.ds((j + 1) * COLS - LANE, LANE)
            after = pl.ds((j + 1) * COLS, LANE)
            f_ref[rows, last] = f_ref[rows, last] - jnp.where(there & (lane == LANE - 1), flux, 0.0)
            f_ref[rows, after] = f_ref[rows, after] + jnp.where(there & (lane == 0), flux, 0.0)
    most = jnp.max(got_ref[:, 2 * EXT : 2 * EXT + 8, LANE:], axis=0)[0:1, 0:1]
    lam_max = 0.5 + 10.0 * most
    theta = (lam_max + 0.5) / 2.0
    delta = (lam_max - 0.5) / 2.0
    sigma = theta / delta
    rho = 1.0 / sigma
    h = h_ref[...]
    sides = {c: moved(h, 0, c) for c in (-1, 0, 1)}
    for n, (a, b, w) in enumerate(NEAR):
        weight[n] = w * (h + moved(sides[b], a, 0))
    inside = h > 0.0
    resid = f_ref[...]
    direction = resid / theta
    answer = jnp.zeros_like(resid)
    for _ in range(ITERS):
        sides = {c: moved(direction, 0, c) for c in (-1, 0, 1)}
        applied = 0.5 * direction
        for n, (a, b, w) in enumerate(NEAR):
            applied = applied + weight[n] * (direction - moved(sides[b], a, 0))
        resid = jnp.where(inside, resid - applied, 0.0)
        answer = answer + direction
        rho_next = 1.0 / (2.0 * sigma - rho)
        direction = rho_next * rho * direction + (2.0 * rho_next / delta) * resid
        rho = rho_next
    out_ref[...] = (answer + direction)[4:20, :]


def solve(got):
    return pl.pallas_call(
        solve_kernel,
        in_specs=[VMEM],
        out_specs=VMEM,
        out_shape=f32(16, WIDE),
        scratch_shapes=[
            pltpu.VMEM((EXT, WIDE), jnp.float32),
            pltpu.VMEM((EXT, WIDE), jnp.float32),
            pltpu.VMEM((8, EXT, WIDE), jnp.float32),
        ],
        compiler_params=pltpu.CompilerParams(vmem_limit_bytes=12 * 2**20),
        cost_estimate=pl.CostEstimate(flops=6_000_000, bytes_accessed=600_000, transcendentals=0),
        name="chebyshev",
    )(got)


def send(x, axis, step):
    count = lax.axis_size(axis)
    pairs = [(i, i + step) for i in range(count) if 0 <= i + step < count]
    return lax.ppermute(x, axis, pairs)


def shards(tracers, velocity, ocean, thickness, depth):
    row_hi, row_lo, col_hi, col_lo, top = pack(thickness, tracers, velocity, ocean, depth)
    halos = (send(row_hi, "bx", 1), send(row_lo, "bx", -1), send(col_hi, "by", 1), send(col_lo, "by", -1))
    tops = lax.all_to_all(top, "bx", split_axis=0, concat_axis=0, tiled=True)
    part, parcels = advect(0, tracers, velocity, ocean, *halos, (thickness, depth, tops))
    got = lax.all_to_all(parcels, "by", split_axis=0, concat_axis=0, tiled=True)
    new_tracers = advect(2, tracers, velocity, ocean, *halos, part)[0]
    return new_tracers, solve(got)


def solution(mesh):
    return jax.shard_map(
        shards,
        mesh=mesh,
        in_specs=(
            P(None, None, "bx", "by"),
            P(None, None, "bx", "by"),
            P("bx", "by"),
            P(),
            P("bx", "by"),
        ),
        out_specs=(P(None, None, "bx", "by"), P(("bx", "by"), None)),
        check_vma=False,
    )
```

```python
import functools

import jax
import jax.numpy as jnp
from jax import lax
from jax.experimental import pallas as pl
from jax.experimental.pallas import tpu as pltpu
from jax.sharding import PartitionSpec as P

ITERS = 3
TRACERS = 4
LEVELS = 12
ROWS = 128
COLS = 256
TILES = ROWS // 8
LANE = 128
WIDE = 8 * COLS
EXT = 24
CHUNK = 32

SPEED, WET, PART, COEF, EDGE, MESSAGE = 48, 60, 64, 68, 72, 80
ANY = pl.BlockSpec(memory_space=pl.ANY)
HBM = pl.BlockSpec(memory_space=pltpu.HBM)
VMEM = pl.BlockSpec(memory_space=pltpu.VMEM)


def f32(*shape):
    return jax.ShapeDtypeStruct(shape, jnp.float32)


def lanes(shape):
    return lax.broadcasted_iota(jnp.int32, shape, len(shape) - 1)


def sublanes(shape):
    return lax.broadcasted_iota(jnp.int32, shape, len(shape) - 2)


def coefficient(depth, wet):
    return depth * (0.1 + 0.9 * wet)


def positive(x):
    return jnp.maximum(x, 0.0)


def negative(x):
    return jnp.minimum(x, 0.0)


def edge_forcing(q, u, v, wet, thick):
    shape = (8, COLS)
    row, col = sublanes(shape), lanes(shape)
    total = jnp.zeros(shape, jnp.float32)
    flux_x = jnp.zeros(shape, jnp.float32)
    flux_y = jnp.zeros(shape, jnp.float32)
    for k in range(LEVELS):
        depth = thick[k]
        total = total + depth * q[k]
        flux_x = flux_x + depth * (positive(u[k]) * q[k] + negative(u[k]) * pltpu.roll(q[k], 7, 0))
        flux_y = flux_y + depth * (positive(v[k]) * q[k] + negative(v[k]) * pltpu.roll(q[k], COLS - 1, 1))
    flux_x = flux_x * jnp.where(row == 7, 0.0, wet * pltpu.roll(wet, 7, 0))
    flux_y = flux_y * jnp.where(col == COLS - 1, 0.0, wet * pltpu.roll(wet, COLS - 1, 1))
    return wet * (total - (flux_x - pltpu.roll(flux_x, 1, 0)) - (flux_y - pltpu.roll(flux_y, 1, 1)))


def edge_terms(q, v, wet, thick):
    lane = lanes((8, LANE))
    last, first = wet[:, LANE:], wet[:, :LANE]
    upwind = jnp.zeros((8, LANE), jnp.float32)
    terms = jnp.where(lane == 28, pltpu.roll(first, 28, 1), 0.0)
    for k in range(LEVELS):
        depth = thick[k]
        speed = v[k][:, LANE:]
        upwind = upwind + depth * positive(speed) * q[k][:, LANE:]
        terms = jnp.where(lane == k, pltpu.roll(depth * negative(speed) * last, k + 1, 1), terms)
        terms = jnp.where(lane == 16 + k, pltpu.roll(q[k][:, :LANE] * first, 16 + k, 1), terms)
    return jnp.where(lane == LEVELS, pltpu.roll(upwind * last, LEVELS + 1, 1), terms)


def pack_kernel(thick_hbm, t_hbm, v_hbm, ocean_hbm, depth_hbm, row_even, row_odd, col_even, col_odd, top,
                t_ref, u_top, u_low, v_top, v_low, v_last, ocean_ref, depth_ref, thick, row_both, col_both, sems):
    odd_x, odd_y = lax.axis_index("bx") % 2, lax.axis_index("by") % 2
    row_hi, row_lo = row_both.at[0], row_both.at[1]
    col_hi, col_lo = col_both.at[0], col_both.at[1]

    def chunk_copy(c):
        rows = pl.ds(pl.multiple_of(c * CHUNK, CHUNK), CHUNK)
        return pltpu.make_async_copy(t_hbm.at[:, :, rows, :], t_ref.at[:, :, rows, :], sems.at[c])

    chunks = ROWS // CHUNK
    small = [
        pltpu.make_async_copy(ocean_hbm, ocean_ref, sems.at[chunks]),
        pltpu.make_async_copy(depth_hbm, depth_ref, sems.at[chunks + 1]),
        pltpu.make_async_copy(v_hbm.at[1, :, :, LANE:], v_last, sems.at[chunks + 2]),
        pltpu.make_async_copy(thick_hbm, thick, sems.at[chunks + 7]),
    ]
    tiles = [
        pltpu.make_async_copy(v_hbm.at[0, :, 0:8, :], u_top, sems.at[chunks + 3]),
        pltpu.make_async_copy(v_hbm.at[0, :, ROWS - 8 :, :], u_low, sems.at[chunks + 4]),
        pltpu.make_async_copy(v_hbm.at[1, :, 0:8, :], v_top, sems.at[chunks + 5]),
        pltpu.make_async_copy(v_hbm.at[1, :, ROWS - 8 :, :], v_low, sems.at[chunks + 6]),
    ]
    for copy in small:
        copy.start()
    for c in range(chunks):
        chunk_copy(c).start()
    for copy in tiles:
        copy.start()
    for copy in small:
        copy.wait()
    wet = ocean_ref[...].astype(jnp.float32)
    coef = coefficient(depth_ref[...], wet)
    most = jnp.max(jnp.max(coef, axis=0, keepdims=True), axis=1, keepdims=True)
    top[...] = jnp.broadcast_to(most[None], top.shape)

    def gather(c, _):
        chunk_copy(c).wait()
        lane = lanes((CHUNK, LANE))
        rows = pl.ds(pl.multiple_of(c * CHUNK, CHUNK), CHUNK)
        ocean = ocean_ref[rows, :].astype(jnp.float32)
        hi = jnp.where(lane == 2 * WET, pltpu.roll(ocean[:, LANE:], (2 * WET + 1) % LANE, 1), 0.0)
        lo = jnp.where(lane == 2 * WET - 1, pltpu.roll(ocean[:, :LANE], 2 * WET - 1, 1), 0.0)
        for k in range(LEVELS):
            for t in range(TRACERS):
                s = t * LEVELS + k
                hi = jnp.where(lane == 2 * s, pltpu.roll(t_ref[t, k, rows, LANE:], 2 * s + 1, 1), hi)
                place = (2 * s - 1) % LANE
                lo = jnp.where(lane == place, pltpu.roll(t_ref[t, k, rows, :LANE], place, 1), lo)
            s = SPEED + k
            hi = jnp.where(lane == 2 * s, pltpu.roll(v_last[k, rows, :], 2 * s + 1, 1), hi)
        col_hi[rows, :] = hi
        col_lo[rows, :] = lo
        return 0

    lax.fori_loop(0, chunks, gather, 0)
    for copy in tiles:
        copy.wait()
    for t in range(TRACERS):
        for k in range(LEVELS):
            s = t * LEVELS + k
            row_hi[s : s + 1, :] = t_ref[t, k, ROWS - 1 : ROWS, :]
            row_lo[s : s + 1, :] = t_ref[t, k, 0:1, :]
    for k in range(LEVELS):
        row_hi[SPEED + k : SPEED + k + 1, :] = u_low[k, 7:8, :]
    row_lo[SPEED:WET, :] = jnp.zeros((WET - SPEED, COLS), jnp.float32)
    for row, message, u, v, keep in ((0, row_lo, u_top, v_top, 0), (ROWS - 8, row_hi, u_low, v_low, 4)):
        rows = slice(row, row + 8)
        here = ocean_ref[rows, :].astype(jnp.float32)
        q = [0.2 * t_ref[0, k, rows, :] - 0.8 * t_ref[1, k, rows, :] for k in range(LEVELS)]
        speed_x = [u[k] for k in range(LEVELS)]
        speed_y = [v[k] for k in range(LEVELS)]
        message[WET:PART, :] = jnp.broadcast_to(here[7:8, :] if keep else here[0:1, :], (PART - WET, COLS))
        message[PART:COEF, :] = edge_forcing(q, speed_x, speed_y, here, thick)[keep : keep + 4, :]
        message[COEF:EDGE, :] = coefficient(depth_ref[rows, :], here)[keep : keep + 4, :]
        message[EDGE:MESSAGE, :LANE] = edge_terms(q, speed_y, here, thick)
        message[EDGE:MESSAGE, LANE:] = jnp.zeros((8, LANE), jnp.float32)
    row_even[...] = row_both[odd_x]
    row_odd[...] = row_both[1 - odd_x]
    col_even[...] = col_both[odd_y]
    col_odd[...] = col_both[1 - odd_y]


def pack(thickness, tracers, velocity, ocean, depth):
    tile = (LEVELS, 8, COLS)
    return pl.pallas_call(
        pack_kernel,
        in_specs=[HBM] * 5,
        out_specs=[VMEM] * 5,
        out_shape=[f32(MESSAGE, COLS), f32(MESSAGE, COLS), f32(ROWS, LANE), f32(ROWS, LANE), f32(16, 8, LANE)],
        scratch_shapes=[
            pltpu.VMEM((TRACERS, LEVELS, ROWS, COLS), jnp.float32),
            pltpu.VMEM(tile, jnp.float32),
            pltpu.VMEM(tile, jnp.float32),
            pltpu.VMEM(tile, jnp.float32),
            pltpu.VMEM(tile, jnp.float32),
            pltpu.VMEM((LEVELS, ROWS, LANE), jnp.float32),
            pltpu.VMEM((ROWS, COLS), jnp.int32),
            pltpu.VMEM((ROWS, COLS), jnp.float32),
            pltpu.SMEM((LEVELS,), jnp.float32),
            pltpu.VMEM((2, MESSAGE, COLS), jnp.float32),
            pltpu.VMEM((2, ROWS, LANE), jnp.float32),
            pltpu.SemaphoreType.DMA((ROWS // CHUNK + 8,)),
        ],
        compiler_params=pltpu.CompilerParams(vmem_limit_bytes=60 * 2**20),
        cost_estimate=pl.CostEstimate(flops=4_000_000, bytes_accessed=7_400_000, transcendentals=0),
        name="pack_edges",
    )(thickness, tracers, velocity, ocean, depth)


def ahead_y(x, edge):
    last = lanes((8, LANE)) == LANE - 1
    a, b = pltpu.roll(x[:, :LANE], LANE - 1, 1), pltpu.roll(x[:, LANE:], LANE - 1, 1)
    return jnp.concatenate([jnp.where(last, b, a), jnp.where(last, edge, b)], 1)


def behind_y(x, edge):
    first = lanes((8, LANE)) == 0
    a, b = pltpu.roll(x[:, :LANE], 1, 1), pltpu.roll(x[:, LANE:], 1, 1)
    return jnp.concatenate([jnp.where(first, edge, a), jnp.where(first, a, b)], 1)


def above(load, edge, r):
    if r < TILES - 1:
        return load(8 * r + 1)
    return jnp.where(sublanes((8, COLS)) == 7, edge, pltpu.roll(load(8 * r), 7, 0))


def upwind(speed, here, ahead):
    return speed * jnp.where(speed > 0.0, here, ahead)


def advect_kernel(first, *refs):
    if first == 0:
        (thick_hbm, t_hbm, v_hbm, ocean_hbm, row_even, row_odd, col_even, col_odd, depth_hbm, tops_hbm, out_hbm, send_ref,
         t_ref, v_ref, out_ref, ocean_ref, rows_in, cols_in, w_x, w_y, before_y, edges, flux_x, sems, small_sems,
         depth_ref, tops, total, flux, ext, thick) = refs
    else:
        (t_hbm, v_hbm, ocean_hbm, row_even, row_odd, col_even, col_odd, _, out_hbm,
         t_ref, v_ref, out_ref, ocean_ref, rows_in, cols_in, w_x, w_y, before_y, edges, flux_x, sems, small_sems) = refs
    odd_x, odd_y = lax.axis_index("bx") % 2, lax.axis_index("by") % 2
    row_lo, row_hi = rows_in.at[0], rows_in.at[1]
    small = [
        (ocean_hbm, ocean_ref),
        (row_even, rows_in.at[1 - odd_x]),
        (row_odd, rows_in.at[odd_x]),
        (col_even, cols_in.at[1 - odd_y]),
        (col_odd, cols_in.at[odd_y]),
    ]
    if first == 0:
        small += [(depth_hbm, depth_ref), (tops_hbm, tops), (thick_hbm, thick)]
    small = [pltpu.make_async_copy(a, b, small_sems.at[i]) for i, (a, b) in enumerate(small)]

    def tracers_in(k):
        return pltpu.make_async_copy(t_hbm.at[first : first + 2, k], t_ref.at[:, k], sems.at[0, k])

    def velocity_in(k):
        return pltpu.make_async_copy(v_hbm.at[:, k], v_ref.at[:, k], sems.at[1, k])

    def tracers_out(k):
        return pltpu.make_async_copy(out_ref.at[:, k], out_hbm.at[first : first + 2, k], sems.at[2, k])

    for copy in small:
        copy.start()
    for k in range(LEVELS):
        tracers_in(k).start()
        velocity_in(k).start()
    for copy in small:
        copy.wait()
    even = lanes((8, LANE)) % 2 == 0
    load_wet = lambda at: ocean_ref[at : at + 8, :].astype(jnp.float32)
    for r in range(TILES):
        rows = pl.ds(8 * r, 8)
        edge = jnp.where(even, cols_in[0, rows, :], cols_in[1, rows, :])
        edges[rows, :] = edge
        here = load_wet(8 * r)
        wet_edge = pltpu.roll(edge, LANE - 2 * WET, 1)
        w_x[rows, :] = here * above(load_wet, row_hi[WET : WET + 1, :], r)
        w_y[rows, :] = here * ahead_y(here, wet_edge)
        before_y[rows, :] = here[:, :LANE] * wet_edge
        if first == 0:
            total[rows, :] = jnp.zeros((8, COLS), jnp.float32)
    w_before = load_wet(0)[0:1, :] * row_lo[WET : WET + 1, :]
    if first == 0:
        flux[...] = jnp.zeros((8, COLS), jnp.float32)

    def level(k, _):
        tracers_in(k).wait()
        velocity_in(k).wait()
        u_before = row_lo[pl.ds(SPEED + k, 1), :] * w_before
        for t in range(2):
            flux_x[t, 7:8, :] = upwind(u_before, row_lo[pl.ds((first + t) * LEVELS + k, 1), :], t_ref[t, k, 0:1, :])
        for r in range(TILES):
            rows = pl.ds(8 * r, 8)
            edge_tile = edges[rows, :]
            u = v_ref[0, k, rows, :] * w_x[rows, :]
            v = v_ref[1, k, rows, :] * w_y[rows, :]
            v_before = pltpu.roll(edge_tile, LANE - 2 * (SPEED + k), 1) * before_y[rows, :]
            new = []
            for t in range(2):
                load = lambda at: t_ref[t, k, at : at + 8, :]
                slot = (first + t) * LEVELS + k
                c = load(8 * r)
                c_edge = pltpu.roll(edge_tile, LANE - 2 * slot, 1)
                here_x = upwind(u, c, above(load, row_hi[pl.ds(slot, 1), :], r))
                flux_x[t, 8 * r + 8 : 8 * r + 16, :] = here_x
                here_y = upwind(v, c, ahead_y(c, c_edge))
                past_y = behind_y(here_y, upwind(v_before, c_edge, c[:, :LANE]))
                past_x = flux_x[t, 8 * r + 7 : 8 * r + 15, :]
                value = (c - (here_x - past_x)) - (here_y - past_y)
                out_ref[t, k, rows, :] = value
                new.append(value)
            if first == 0:
                total[rows, :] = total[rows, :] + ((0.2 * thick[k]) * new[0] - (0.8 * thick[k]) * new[1])
        if first == 0:
            mixed = lambda row: thick[k] * (0.2 * flux_x[0, row : row + 1, :] - 0.8 * flux_x[1, row : row + 1, :])
            flux[0:1, :] = flux[0:1, :] + mixed(7)
            flux[1:2, :] = flux[1:2, :] + mixed(ROWS + 7)
        tracers_out(k).start()
        return 0

    lax.fori_loop(0, LEVELS, level, 0)

    if first == 0:
        row = sublanes((4, COLS))
        ext[0, 0:4, :] = row_lo[PART:COEF, :] - jnp.where(row == 3, flux[0:1, :], 0.0)
        ext[0, ROWS + 4 :, :] = row_hi[PART:COEF, :] + jnp.where(row == 0, flux[1:2, :], 0.0)
        ext[1, 0:4, :] = row_lo[COEF:EDGE, :]
        ext[1, ROWS + 4 :, :] = row_hi[COEF:EDGE, :]
        for r in range(TILES):
            rows = pl.ds(8 * r, 8)
            here = load_wet(8 * r)
            ext[0, 8 * r + 4 : 8 * r + 12, :] = total[rows, :] * here
            ext[1, 8 * r + 4 : 8 * r + 12, :] = coefficient(depth_ref[rows, :], here)
        most = jnp.max(tops[...], axis=0)
        tile = sublanes((8, LANE))
        for j in range(8):
            send_ref[j, 0:EXT, :] = ext[0, 16 * j : 16 * j + EXT, :]
            send_ref[j, EXT : 2 * EXT, :] = ext[1, 16 * j : 16 * j + EXT, :]
            edge = jnp.zeros((8, LANE), jnp.float32)
            if j == 0:
                edge = jnp.where((tile >= 1) & (tile <= 3), pltpu.roll(row_lo[EDGE:MESSAGE, :LANE], 4, 0), 0.0)
            if j == 7:
                edge = jnp.where((tile >= 4) & (tile <= 6), pltpu.roll(row_hi[EDGE:MESSAGE, :LANE], 4, 0), 0.0)
            send_ref[j, 2 * EXT : 2 * EXT + 8, :LANE] = edge
            send_ref[j, 2 * EXT : 2 * EXT + 8, LANE:] = most
    for k in range(LEVELS):
        tracers_out(k).wait()


def advect(first, tracers, velocity, ocean, row_even, row_odd, col_even, col_odd, extra):
    ins = [HBM] * 3 + [ANY] * 4
    operands = [tracers, velocity, ocean, row_even, row_odd, col_even, col_odd]
    out_specs = [HBM]
    out_shape = [f32(TRACERS, LEVELS, ROWS, COLS)]
    block = pltpu.VMEM((ROWS, COLS), jnp.float32)
    narrow = pltpu.VMEM((ROWS, LANE), jnp.float32)
    scratch = [
        pltpu.VMEM((2, LEVELS, ROWS, COLS), jnp.float32),
        pltpu.VMEM((2, LEVELS, ROWS, COLS), jnp.float32),
        pltpu.VMEM((2, LEVELS, ROWS, COLS), jnp.float32),
        pltpu.VMEM((ROWS, COLS), jnp.int32),
        pltpu.VMEM((2, MESSAGE, COLS), jnp.float32),
        pltpu.VMEM((2, ROWS, LANE), jnp.float32),
        block,
        block,
        narrow,
        narrow,
        pltpu.VMEM((2, ROWS + 8, COLS), jnp.float32),
        pltpu.SemaphoreType.DMA((3, LEVELS)),
        pltpu.SemaphoreType.DMA((8,)),
    ]
    aliases = {}
    if first == 0:
        thickness, depth, tops = extra
        ins = [HBM] + ins + [HBM, ANY]
        operands = [thickness] + operands + [depth, tops]
        out_specs.append(VMEM)
        out_shape.append(f32(8, 2 * EXT + 8, COLS))
        scratch += [
            block,
            pltpu.VMEM((16, 8, LANE), jnp.float32),
            block,
            pltpu.VMEM((8, COLS), jnp.float32),
            pltpu.VMEM((2, ROWS + 8, COLS), jnp.float32),
            pltpu.SMEM((LEVELS,), jnp.float32),
        ]
    else:
        aliases = {len(operands): 0}
        ins = ins + [HBM]
        operands = operands + [extra]
    return pl.pallas_call(
        functools.partial(advect_kernel, first),
        in_specs=ins,
        out_specs=out_specs,
        out_shape=out_shape,
        scratch_shapes=scratch,
        input_output_aliases=aliases,
        compiler_params=pltpu.CompilerParams(vmem_limit_bytes=58 * 2**20),
        cost_estimate=pl.CostEstimate(flops=24_000_000, bytes_accessed=9_400_000, transcendentals=0),
        name="advect_forcing" if first == 0 else "advect_rest",
    )(*operands)


NEAR = ((1, 0, 0.5), (-1, 0, 0.5), (0, 1, 0.5), (0, -1, 0.5), (1, 1, 0.125), (1, -1, 0.125), (-1, 1, 0.125), (-1, -1, 0.125))


def moved(x, rows, cols):
    if cols:
        lane = lanes(x.shape)
        x = pltpu.roll(x, (-cols) % x.shape[1], 1)
        x = jnp.where(lane == (x.shape[1] - 1 if cols > 0 else 0), 0.0, x)
    if rows:
        x = pltpu.roll(x, (-rows) % x.shape[0], 0)
    return x


def solve_kernel(got, out_ref, h_ref, f_ref, misc, weight, sems):
    copies = []
    for j in range(8):
        cols = pl.ds(j * COLS, COLS)
        copies.append(pltpu.make_async_copy(got.at[j, 0:EXT, :], f_ref.at[:, cols], sems.at[0, j]))
        copies.append(pltpu.make_async_copy(got.at[j, EXT : 2 * EXT, :], h_ref.at[:, cols], sems.at[1, j]))
        copies.append(pltpu.make_async_copy(got.at[j, 2 * EXT :, :], misc.at[j], sems.at[2, j]))
    for copy in copies:
        copy.start()
    for copy in copies:
        copy.wait()
    lane, tile = lanes((8, LANE)), sublanes((8, LANE))
    for j in range(7):
        pairs = misc[j, :, :LANE] * pltpu.roll(misc[j + 1, :, :LANE], LANE - 16, 1)
        flux = jnp.sum(jnp.where(lane <= LEVELS, pairs, 0.0), axis=1, keepdims=True)
        for rows, there in ((pl.ds(0, 8), tile < 4), (pl.ds(16, 8), tile >= 4)):
            last = pl.ds((j + 1) * COLS - LANE, LANE)
            after = pl.ds((j + 1) * COLS, LANE)
            f_ref[rows, last] = f_ref[rows, last] - jnp.where(there & (lane == LANE - 1), flux, 0.0)
            f_ref[rows, after] = f_ref[rows, after] + jnp.where(there & (lane == 0), flux, 0.0)
    most = jnp.max(misc[:, :, LANE:], axis=0)[0:1, 0:1]
    lam_max = 0.5 + 10.0 * most
    theta = (lam_max + 0.5) / 2.0
    delta = (lam_max - 0.5) / 2.0
    sigma = theta / delta
    rho = 1.0 / sigma
    h = h_ref[...]
    sides = {c: moved(h, 0, c) for c in (-1, 0, 1)}
    for n, (a, b, w) in enumerate(NEAR):
        weight[n] = w * (h + moved(sides[b], a, 0))
    inside = h > 0.0
    resid = f_ref[...]
    direction = resid / theta
    answer = jnp.zeros_like(resid)
    for _ in range(ITERS):
        sides = {c: moved(direction, 0, c) for c in (-1, 0, 1)}
        applied = 0.5 * direction
        for n, (a, b, w) in enumerate(NEAR):
            applied = applied + weight[n] * (direction - moved(sides[b], a, 0))
        resid = jnp.where(inside, resid - applied, 0.0)
        answer = answer + direction
        rho_next = 1.0 / (2.0 * sigma - rho)
        direction = rho_next * rho * direction + (2.0 * rho_next / delta) * resid
        rho = rho_next
    out_ref[...] = (answer + direction)[4:20, :]


def solve(got):
    return pl.pallas_call(
        solve_kernel,
        in_specs=[ANY],
        out_specs=VMEM,
        out_shape=f32(16, WIDE),
        scratch_shapes=[
            pltpu.VMEM((EXT, WIDE), jnp.float32),
            pltpu.VMEM((EXT, WIDE), jnp.float32),
            pltpu.VMEM((8, 8, COLS), jnp.float32),
            pltpu.VMEM((8, EXT, WIDE), jnp.float32),
            pltpu.SemaphoreType.DMA((3, 8)),
        ],
        compiler_params=pltpu.CompilerParams(vmem_limit_bytes=12 * 2**20),
        cost_estimate=pl.CostEstimate(flops=6_000_000, bytes_accessed=600_000, transcendentals=0),
        name="chebyshev",
    )(got)


def exchange(x, axis, odd):
    count = lax.axis_size(axis)
    pairs = []
    for i in range(odd, count - 1, 2):
        pairs += [(i, i + 1), (i + 1, i)]
    return lax.ppermute(x, axis, pairs)


def shards(tracers, velocity, ocean, thickness, depth):
    row_even, row_odd, col_even, col_odd, top = pack(thickness, tracers, velocity, ocean, depth)
    halos = (exchange(row_even, "bx", 0), exchange(row_odd, "bx", 1), exchange(col_even, "by", 0), exchange(col_odd, "by", 1))
    tops = lax.all_to_all(top, "bx", split_axis=0, concat_axis=0, tiled=True)
    part, parcels = advect(0, tracers, velocity, ocean, *halos, (thickness, depth, tops))
    got = lax.all_to_all(parcels, "by", split_axis=0, concat_axis=0, tiled=True)
    new_tracers = advect(2, tracers, velocity, ocean, *halos, part)[0]
    return new_tracers, solve(got)


def solution(mesh):
    return jax.shard_map(
        shards,
        mesh=mesh,
        in_specs=(
            P(None, None, "bx", "by"),
            P(None, None, "bx", "by"),
            P("bx", "by"),
            P(),
            P("bx", "by"),
        ),
        out_specs=(P(None, None, "bx", "by"), P(("bx", "by"), None)),
        check_vma=False,
    )
```

```python
import functools

import jax
import jax.numpy as jnp
from jax import lax
from jax.experimental import pallas as pl
from jax.experimental.pallas import tpu as pltpu
from jax.sharding import PartitionSpec as P

ITERS = 3
TRACERS = 4
LEVELS = 12
ROWS = 128
COLS = 256
TILES = ROWS // 8
LANE = 128
WIDE = 8 * COLS
EXT = 24
CHUNK = 32

SPEED, WET, PART, COEF, EDGE, MESSAGE = 48, 60, 64, 68, 72, 80
ANY = pl.BlockSpec(memory_space=pl.ANY)
HBM = pl.BlockSpec(memory_space=pltpu.HBM)
VMEM = pl.BlockSpec(memory_space=pltpu.VMEM)


def f32(*shape):
    return jax.ShapeDtypeStruct(shape, jnp.float32)


def lanes(shape):
    return lax.broadcasted_iota(jnp.int32, shape, len(shape) - 1)


def sublanes(shape):
    return lax.broadcasted_iota(jnp.int32, shape, len(shape) - 2)


def coefficient(depth, wet):
    return depth * (0.1 + 0.9 * wet)


def positive(x):
    return jnp.maximum(x, 0.0)


def negative(x):
    return jnp.minimum(x, 0.0)


def edge_forcing(q, u, v, wet, thick):
    shape = (8, COLS)
    row, col = sublanes(shape), lanes(shape)
    total = jnp.zeros(shape, jnp.float32)
    flux_x = jnp.zeros(shape, jnp.float32)
    flux_y = jnp.zeros(shape, jnp.float32)
    for k in range(LEVELS):
        depth = thick[k]
        total = total + depth * q[k]
        flux_x = flux_x + depth * (positive(u[k]) * q[k] + negative(u[k]) * pltpu.roll(q[k], 7, 0))
        flux_y = flux_y + depth * (positive(v[k]) * q[k] + negative(v[k]) * pltpu.roll(q[k], COLS - 1, 1))
    flux_x = flux_x * jnp.where(row == 7, 0.0, wet * pltpu.roll(wet, 7, 0))
    flux_y = flux_y * jnp.where(col == COLS - 1, 0.0, wet * pltpu.roll(wet, COLS - 1, 1))
    return wet * (total - (flux_x - pltpu.roll(flux_x, 1, 0)) - (flux_y - pltpu.roll(flux_y, 1, 1)))


def edge_terms(q, v, wet, thick):
    lane = lanes((8, LANE))
    last, first = wet[:, LANE:], wet[:, :LANE]
    upwind = jnp.zeros((8, LANE), jnp.float32)
    terms = jnp.where(lane == 28, pltpu.roll(first, 28, 1), 0.0)
    for k in range(LEVELS):
        depth = thick[k]
        speed = v[k][:, LANE:]
        upwind = upwind + depth * positive(speed) * q[k][:, LANE:]
        terms = jnp.where(lane == k, pltpu.roll(depth * negative(speed) * last, k + 1, 1), terms)
        terms = jnp.where(lane == 16 + k, pltpu.roll(q[k][:, :LANE] * first, 16 + k, 1), terms)
    return jnp.where(lane == LEVELS, pltpu.roll(upwind * last, LEVELS + 1, 1), terms)


def pack_kernel(thick_hbm, t_hbm, v_hbm, ocean_hbm, depth_hbm, row_even, row_odd, col_even, col_odd, top,
                t_ref, u_top, u_low, v_top, v_low, v_last, ocean_ref, depth_ref, thick, row_both, col_both, sems):
    odd_x, odd_y = lax.axis_index("bx") % 2, lax.axis_index("by") % 2
    row_hi, row_lo = row_both.at[0], row_both.at[1]
    col_hi, col_lo = col_both.at[0], col_both.at[1]

    def chunk_copy(c):
        rows = pl.ds(pl.multiple_of(c * CHUNK, CHUNK), CHUNK)
        return pltpu.make_async_copy(t_hbm.at[:, :, rows, :], t_ref.at[:, :, rows, :], sems.at[c])

    chunks = ROWS // CHUNK
    small = [
        pltpu.make_async_copy(ocean_hbm, ocean_ref, sems.at[chunks]),
        pltpu.make_async_copy(depth_hbm, depth_ref, sems.at[chunks + 1]),
        pltpu.make_async_copy(v_hbm.at[1, :, :, LANE:], v_last, sems.at[chunks + 2]),
        pltpu.make_async_copy(thick_hbm, thick, sems.at[chunks + 7]),
    ]
    tiles = [
        pltpu.make_async_copy(v_hbm.at[0, :, 0:8, :], u_top, sems.at[chunks + 3]),
        pltpu.make_async_copy(v_hbm.at[0, :, ROWS - 8 :, :], u_low, sems.at[chunks + 4]),
        pltpu.make_async_copy(v_hbm.at[1, :, 0:8, :], v_top, sems.at[chunks + 5]),
        pltpu.make_async_copy(v_hbm.at[1, :, ROWS - 8 :, :], v_low, sems.at[chunks + 6]),
    ]
    for copy in small:
        copy.start()
    for c in range(chunks):
        chunk_copy(c).start()
    for copy in tiles:
        copy.start()
    for copy in small:
        copy.wait()
    wet = ocean_ref[...].astype(jnp.float32)
    coef = coefficient(depth_ref[...], wet)
    most = jnp.max(jnp.max(coef, axis=0, keepdims=True), axis=1, keepdims=True)
    top[...] = jnp.broadcast_to(most[None], top.shape)

    def gather(c, _):
        chunk_copy(c).wait()
        lane = lanes((CHUNK, LANE))
        rows = pl.ds(pl.multiple_of(c * CHUNK, CHUNK), CHUNK)
        ocean = ocean_ref[rows, :].astype(jnp.float32)
        hi = jnp.where(lane == 2 * WET, pltpu.roll(ocean[:, LANE:], (2 * WET + 1) % LANE, 1), 0.0)
        lo = jnp.where(lane == 2 * WET - 1, pltpu.roll(ocean[:, :LANE], 2 * WET - 1, 1), 0.0)
        for k in range(LEVELS):
            for t in range(TRACERS):
                s = t * LEVELS + k
                hi = jnp.where(lane == 2 * s, pltpu.roll(t_ref[t, k, rows, LANE:], 2 * s + 1, 1), hi)
                place = (2 * s - 1) % LANE
                lo = jnp.where(lane == place, pltpu.roll(t_ref[t, k, rows, :LANE], place, 1), lo)
            s = SPEED + k
            hi = jnp.where(lane == 2 * s, pltpu.roll(v_last[k, rows, :], 2 * s + 1, 1), hi)
        col_hi[rows, :] = hi
        col_lo[rows, :] = lo
        return 0

    lax.fori_loop(0, chunks, gather, 0)
    for copy in tiles:
        copy.wait()
    for t in range(TRACERS):
        for k in range(LEVELS):
            s = t * LEVELS + k
            row_hi[s : s + 1, :] = t_ref[t, k, ROWS - 1 : ROWS, :]
            row_lo[s : s + 1, :] = t_ref[t, k, 0:1, :]
    for k in range(LEVELS):
        row_hi[SPEED + k : SPEED + k + 1, :] = u_low[k, 7:8, :]
    row_lo[SPEED:WET, :] = jnp.zeros((WET - SPEED, COLS), jnp.float32)
    for row, message, u, v, keep in ((0, row_lo, u_top, v_top, 0), (ROWS - 8, row_hi, u_low, v_low, 4)):
        rows = slice(row, row + 8)
        here = ocean_ref[rows, :].astype(jnp.float32)
        q = [0.2 * t_ref[0, k, rows, :] - 0.8 * t_ref[1, k, rows, :] for k in range(LEVELS)]
        speed_x = [u[k] for k in range(LEVELS)]
        speed_y = [v[k] for k in range(LEVELS)]
        message[WET:PART, :] = jnp.broadcast_to(here[7:8, :] if keep else here[0:1, :], (PART - WET, COLS))
        message[PART:COEF, :] = edge_forcing(q, speed_x, speed_y, here, thick)[keep : keep + 4, :]
        message[COEF:EDGE, :] = coefficient(depth_ref[rows, :], here)[keep : keep + 4, :]
        message[EDGE:MESSAGE, :LANE] = edge_terms(q, speed_y, here, thick)
        message[EDGE:MESSAGE, LANE:] = jnp.zeros((8, LANE), jnp.float32)
    row_even[...] = row_both[odd_x]
    row_odd[...] = row_both[1 - odd_x]
    col_even[...] = col_both[odd_y]
    col_odd[...] = col_both[1 - odd_y]


def pack(thickness, tracers, velocity, ocean, depth):
    tile = (LEVELS, 8, COLS)
    return pl.pallas_call(
        pack_kernel,
        in_specs=[HBM] * 5,
        out_specs=[VMEM] * 5,
        out_shape=[f32(MESSAGE, COLS), f32(MESSAGE, COLS), f32(ROWS, LANE), f32(ROWS, LANE), f32(16, 8, LANE)],
        scratch_shapes=[
            pltpu.VMEM((TRACERS, LEVELS, ROWS, COLS), jnp.float32),
            pltpu.VMEM(tile, jnp.float32),
            pltpu.VMEM(tile, jnp.float32),
            pltpu.VMEM(tile, jnp.float32),
            pltpu.VMEM(tile, jnp.float32),
            pltpu.VMEM((LEVELS, ROWS, LANE), jnp.float32),
            pltpu.VMEM((ROWS, COLS), jnp.int32),
            pltpu.VMEM((ROWS, COLS), jnp.float32),
            pltpu.SMEM((LEVELS,), jnp.float32),
            pltpu.VMEM((2, MESSAGE, COLS), jnp.float32),
            pltpu.VMEM((2, ROWS, LANE), jnp.float32),
            pltpu.SemaphoreType.DMA((ROWS // CHUNK + 8,)),
        ],
        compiler_params=pltpu.CompilerParams(vmem_limit_bytes=60 * 2**20),
        cost_estimate=pl.CostEstimate(flops=4_000_000, bytes_accessed=7_400_000, transcendentals=0),
        name="pack_edges",
    )(thickness, tracers, velocity, ocean, depth)


def ahead_y(x, edge):
    last = lanes((8, LANE)) == LANE - 1
    a, b = pltpu.roll(x[:, :LANE], LANE - 1, 1), pltpu.roll(x[:, LANE:], LANE - 1, 1)
    return jnp.concatenate([jnp.where(last, b, a), jnp.where(last, edge, b)], 1)


def behind_y(x, edge):
    first = lanes((8, LANE)) == 0
    a, b = pltpu.roll(x[:, :LANE], 1, 1), pltpu.roll(x[:, LANE:], 1, 1)
    return jnp.concatenate([jnp.where(first, edge, a), jnp.where(first, a, b)], 1)


def above(load, edge, r):
    if r < TILES - 1:
        return load(8 * r + 1)
    return jnp.where(sublanes((8, COLS)) == 7, edge, pltpu.roll(load(8 * r), 7, 0))


def upwind(speed, here, ahead):
    return speed * jnp.where(speed > 0.0, here, ahead)


def advect_kernel(first, *refs):
    if first == 0:
        (thick_hbm, t_hbm, v_hbm, ocean_hbm, row_even, row_odd, col_even, col_odd, depth_hbm, out_hbm, send_ref,
         t_ref, v_ref, out_ref, ocean_ref, rows_in, cols_in, w_x, w_y, before_y, edges, sems, small_sems,
         depth_ref, total, flux, ext, thick) = refs
    else:
        (t_hbm, v_hbm, ocean_hbm, row_even, row_odd, col_even, col_odd, _, out_hbm,
         t_ref, v_ref, out_ref, ocean_ref, rows_in, cols_in, w_x, w_y, before_y, edges, sems, small_sems) = refs
    odd_x, odd_y = lax.axis_index("bx") % 2, lax.axis_index("by") % 2
    row_lo, row_hi = rows_in.at[0], rows_in.at[1]
    small = [
        (ocean_hbm, ocean_ref),
        (row_even, rows_in.at[1 - odd_x]),
        (row_odd, rows_in.at[odd_x]),
        (col_even, cols_in.at[1 - odd_y]),
        (col_odd, cols_in.at[odd_y]),
    ]
    if first == 0:
        small += [(depth_hbm, depth_ref), (thick_hbm, thick)]
    small = [pltpu.make_async_copy(a, b, small_sems.at[i]) for i, (a, b) in enumerate(small)]

    def tracers_in(k):
        return pltpu.make_async_copy(t_hbm.at[first : first + 2, k], t_ref.at[:, k], sems.at[0, k])

    def velocity_in(k):
        return pltpu.make_async_copy(v_hbm.at[:, k], v_ref.at[:, k], sems.at[1, k])

    def tracers_out(k):
        return pltpu.make_async_copy(out_ref.at[:, k], out_hbm.at[first : first + 2, k], sems.at[2, k])

    for copy in small:
        copy.start()
    for k in range(LEVELS):
        tracers_in(k).start()
        velocity_in(k).start()
    for copy in small:
        copy.wait()
    even = lanes((8, LANE)) % 2 == 0
    load_wet = lambda at: ocean_ref[at : at + 8, :].astype(jnp.float32)
    for r in range(TILES):
        rows = pl.ds(8 * r, 8)
        edge = jnp.where(even, cols_in[0, rows, :], cols_in[1, rows, :])
        for k in range(LEVELS):
            for i, slot in enumerate((first * LEVELS + k, (first + 1) * LEVELS + k, SPEED + k)):
                edges[i, k, rows, :] = pltpu.roll(edge, (LANE - 2 * slot) % LANE, 1)
        here = load_wet(8 * r)
        wet_edge = pltpu.roll(edge, LANE - 2 * WET, 1)
        w_x[rows, :] = here * above(load_wet, row_hi[WET : WET + 1, :], r)
        w_y[rows, :] = here * ahead_y(here, wet_edge)
        before_y[rows, :] = here[:, :LANE] * wet_edge
        if first == 0:
            total[rows, :] = jnp.zeros((8, COLS), jnp.float32)
    w_before = load_wet(0)[0:1, :] * row_lo[WET : WET + 1, :]
    if first == 0:
        flux[...] = jnp.zeros((8, COLS), jnp.float32)

    def level(k, _):
        tracers_in(k).wait()
        velocity_in(k).wait()
        u_before = row_lo[pl.ds(SPEED + k, 1), :] * w_before
        into_x = [upwind(u_before, row_lo[pl.ds((first + t) * LEVELS + k, 1), :], t_ref[t, k, 0:1, :]) for t in range(2)]
        carry, out_x = list(into_x), [None, None]
        for r in range(TILES):
            rows = pl.ds(8 * r, 8)
            u = v_ref[0, k, rows, :] * w_x[rows, :]
            v = v_ref[1, k, rows, :] * w_y[rows, :]
            v_before = edges[2, k, rows, :] * before_y[rows, :]
            new = []
            for t in range(2):
                load = lambda at: t_ref[t, k, at : at + 8, :]
                slot = (first + t) * LEVELS + k
                c = load(8 * r)
                c_edge = edges[t, k, rows, :]
                here_x = upwind(u, c, above(load, row_hi[pl.ds(slot, 1), :], r))
                turned = pltpu.roll(here_x, 1, 0)
                past_x = jnp.where(sublanes((8, COLS)) == 0, carry[t], turned)
                carry[t] = turned
                if r == TILES - 1:
                    out_x[t] = here_x[7:8, :]
                here_y = upwind(v, c, ahead_y(c, c_edge))
                past_y = behind_y(here_y, upwind(v_before, c_edge, c[:, :LANE]))
                value = (c - (here_x - past_x)) - (here_y - past_y)
                out_ref[t, k, rows, :] = value
                new.append(value)
            if first == 0:
                total[rows, :] = total[rows, :] + ((0.2 * thick[k]) * new[0] - (0.8 * thick[k]) * new[1])
        if first == 0:
            flux[0:1, :] = flux[0:1, :] + thick[k] * (0.2 * into_x[0] - 0.8 * into_x[1])
            flux[1:2, :] = flux[1:2, :] + thick[k] * (0.2 * out_x[0] - 0.8 * out_x[1])
        tracers_out(k).start()
        return 0

    lax.fori_loop(0, LEVELS, level, 0)

    if first == 0:
        row = sublanes((4, COLS))
        ext[0, 0:4, :] = row_lo[PART:COEF, :] - jnp.where(row == 3, flux[0:1, :], 0.0)
        ext[0, ROWS + 4 :, :] = row_hi[PART:COEF, :] + jnp.where(row == 0, flux[1:2, :], 0.0)
        ext[1, 0:4, :] = row_lo[COEF:EDGE, :]
        ext[1, ROWS + 4 :, :] = row_hi[COEF:EDGE, :]
        for r in range(TILES):
            rows = pl.ds(8 * r, 8)
            here = load_wet(8 * r)
            ext[0, 8 * r + 4 : 8 * r + 12, :] = total[rows, :] * here
            ext[1, 8 * r + 4 : 8 * r + 12, :] = coefficient(depth_ref[rows, :], here)
        tile = sublanes((8, LANE))
        for j in range(8):
            send_ref[j, 0:EXT, :] = ext[0, 16 * j : 16 * j + EXT, :]
            send_ref[j, EXT : 2 * EXT, :] = ext[1, 16 * j : 16 * j + EXT, :]
            edge = jnp.zeros((8, LANE), jnp.float32)
            if j == 0:
                edge = jnp.where((tile >= 1) & (tile <= 3), pltpu.roll(row_lo[EDGE:MESSAGE, :LANE], 4, 0), 0.0)
            if j == 7:
                edge = jnp.where((tile >= 4) & (tile <= 6), pltpu.roll(row_hi[EDGE:MESSAGE, :LANE], 4, 0), 0.0)
            send_ref[j, 2 * EXT : 2 * EXT + 8, :LANE] = edge
            send_ref[j, 2 * EXT : 2 * EXT + 8, LANE:] = jnp.zeros((8, LANE), jnp.float32)
    for k in range(LEVELS):
        tracers_out(k).wait()


def advect(first, tracers, velocity, ocean, row_even, row_odd, col_even, col_odd, extra):
    ins = [HBM] * 3 + [ANY] * 4
    operands = [tracers, velocity, ocean, row_even, row_odd, col_even, col_odd]
    out_specs = [HBM]
    out_shape = [f32(TRACERS, LEVELS, ROWS, COLS)]
    block = pltpu.VMEM((ROWS, COLS), jnp.float32)
    narrow = pltpu.VMEM((ROWS, LANE), jnp.float32)
    scratch = [
        pltpu.VMEM((2, LEVELS, ROWS, COLS), jnp.float32),
        pltpu.VMEM((2, LEVELS, ROWS, COLS), jnp.float32),
        pltpu.VMEM((2, LEVELS, ROWS, COLS), jnp.float32),
        pltpu.VMEM((ROWS, COLS), jnp.int32),
        pltpu.VMEM((2, MESSAGE, COLS), jnp.float32),
        pltpu.VMEM((2, ROWS, LANE), jnp.float32),
        block,
        block,
        narrow,
        pltpu.VMEM((3, LEVELS, ROWS, LANE), jnp.float32),
        pltpu.SemaphoreType.DMA((3, LEVELS)),
        pltpu.SemaphoreType.DMA((8,)),
    ]
    aliases = {}
    if first == 0:
        thickness, depth = extra
        ins = [HBM] + ins + [HBM]
        operands = [thickness] + operands + [depth]
        out_specs.append(VMEM)
        out_shape.append(f32(8, 2 * EXT + 8, COLS))
        scratch += [
            block,
            block,
            pltpu.VMEM((8, COLS), jnp.float32),
            pltpu.VMEM((2, ROWS + 8, COLS), jnp.float32),
            pltpu.SMEM((LEVELS,), jnp.float32),
        ]
    else:
        aliases = {len(operands): 0}
        ins = ins + [HBM]
        operands = operands + [extra]
    return pl.pallas_call(
        functools.partial(advect_kernel, first),
        in_specs=ins,
        out_specs=out_specs,
        out_shape=out_shape,
        scratch_shapes=scratch,
        input_output_aliases=aliases,
        compiler_params=pltpu.CompilerParams(vmem_limit_bytes=58 * 2**20),
        cost_estimate=pl.CostEstimate(flops=24_000_000, bytes_accessed=9_400_000, transcendentals=0),
        name="advect_forcing" if first == 0 else "advect_rest",
    )(*operands)


def insert_kernel(_, tops, out_hbm, most, sem):
    top = jnp.max(tops[...], axis=0)
    for j in range(8):
        most[j] = top
    copy = pltpu.make_async_copy(most, out_hbm.at[:, 2 * EXT :, LANE:], sem.at[0])
    copy.start()
    copy.wait()


def insert(parcels, tops):
    return pl.pallas_call(
        insert_kernel,
        in_specs=[HBM, VMEM],
        out_specs=HBM,
        out_shape=f32(8, 2 * EXT + 8, COLS),
        scratch_shapes=[pltpu.VMEM((8, 8, LANE), jnp.float32), pltpu.SemaphoreType.DMA((1,))],
        input_output_aliases={0: 0},
        compiler_params=pltpu.CompilerParams(vmem_limit_bytes=58 * 2**20),
        cost_estimate=pl.CostEstimate(flops=1000, bytes_accessed=100_000, transcendentals=0),
        name="insert_maximum",
    )(parcels, tops)


NEAR = ((1, 0, 0.5), (-1, 0, 0.5), (0, 1, 0.5), (0, -1, 0.5), (1, 1, 0.125), (1, -1, 0.125), (-1, 1, 0.125), (-1, -1, 0.125))


def moved(x, rows, cols):
    if cols:
        lane = lanes(x.shape)
        x = pltpu.roll(x, (-cols) % x.shape[1], 1)
        x = jnp.where(lane == (x.shape[1] - 1 if cols > 0 else 0), 0.0, x)
    if rows:
        x = pltpu.roll(x, (-rows) % x.shape[0], 0)
    return x


def solve_kernel(got, out_ref, h_ref, f_ref, misc, weight, sems):
    copies = []
    for j in range(8):
        cols = pl.ds(j * COLS, COLS)
        copies.append(pltpu.make_async_copy(got.at[j, 0:EXT, :], f_ref.at[:, cols], sems.at[0, j]))
        copies.append(pltpu.make_async_copy(got.at[j, EXT : 2 * EXT, :], h_ref.at[:, cols], sems.at[1, j]))
        copies.append(pltpu.make_async_copy(got.at[j, 2 * EXT :, :], misc.at[j], sems.at[2, j]))
    for copy in copies:
        copy.start()
    for copy in copies:
        copy.wait()
    lane, tile = lanes((8, LANE)), sublanes((8, LANE))
    for j in range(7):
        pairs = misc[j, :, :LANE] * pltpu.roll(misc[j + 1, :, :LANE], LANE - 16, 1)
        flux = jnp.sum(jnp.where(lane <= LEVELS, pairs, 0.0), axis=1, keepdims=True)
        for rows, there in ((pl.ds(0, 8), tile < 4), (pl.ds(16, 8), tile >= 4)):
            last = pl.ds((j + 1) * COLS - LANE, LANE)
            after = pl.ds((j + 1) * COLS, LANE)
            f_ref[rows, last] = f_ref[rows, last] - jnp.where(there & (lane == LANE - 1), flux, 0.0)
            f_ref[rows, after] = f_ref[rows, after] + jnp.where(there & (lane == 0), flux, 0.0)
    most = jnp.max(misc[:, :, LANE:], axis=0)[0:1, 0:1]
    lam_max = 0.5 + 10.0 * most
    theta = (lam_max + 0.5) / 2.0
    delta = (lam_max - 0.5) / 2.0
    sigma = theta / delta
    rho = 1.0 / sigma
    h = h_ref[...]
    sides = {c: moved(h, 0, c) for c in (-1, 0, 1)}
    for n, (a, b, w) in enumerate(NEAR):
        weight[n] = w * (h + moved(sides[b], a, 0))
    inside = h > 0.0
    resid = f_ref[...]
    direction = resid / theta
    answer = jnp.zeros_like(resid)
    for _ in range(ITERS):
        sides = {c: moved(direction, 0, c) for c in (-1, 0, 1)}
        applied = 0.5 * direction
        for n, (a, b, w) in enumerate(NEAR):
            applied = applied + weight[n] * (direction - moved(sides[b], a, 0))
        resid = jnp.where(inside, resid - applied, 0.0)
        answer = answer + direction
        rho_next = 1.0 / (2.0 * sigma - rho)
        direction = rho_next * rho * direction + (2.0 * rho_next / delta) * resid
        rho = rho_next
    out_ref[...] = (answer + direction)[4:20, :]


def solve(got):
    return pl.pallas_call(
        solve_kernel,
        in_specs=[ANY],
        out_specs=VMEM,
        out_shape=f32(16, WIDE),
        scratch_shapes=[
            pltpu.VMEM((EXT, WIDE), jnp.float32),
            pltpu.VMEM((EXT, WIDE), jnp.float32),
            pltpu.VMEM((8, 8, COLS), jnp.float32),
            pltpu.VMEM((8, EXT, WIDE), jnp.float32),
            pltpu.SemaphoreType.DMA((3, 8)),
        ],
        compiler_params=pltpu.CompilerParams(vmem_limit_bytes=12 * 2**20),
        cost_estimate=pl.CostEstimate(flops=6_000_000, bytes_accessed=600_000, transcendentals=0),
        name="chebyshev",
    )(got)


def exchange(x, axis, odd):
    count = lax.axis_size(axis)
    pairs = []
    for i in range(odd, count - 1, 2):
        pairs += [(i, i + 1), (i + 1, i)]
    return lax.ppermute(x, axis, pairs)


def shards(tracers, velocity, ocean, thickness, depth):
    row_even, row_odd, col_even, col_odd, top = pack(thickness, tracers, velocity, ocean, depth)
    halos = (exchange(row_even, "bx", 0), exchange(row_odd, "bx", 1), exchange(col_even, "by", 0), exchange(col_odd, "by", 1))
    tops = lax.all_to_all(top, "bx", split_axis=0, concat_axis=0, tiled=True)
    part, parcels = advect(0, tracers, velocity, ocean, *halos, (thickness, depth))
    got = lax.all_to_all(insert(parcels, tops), "by", split_axis=0, concat_axis=0, tiled=True)
    new_tracers = advect(2, tracers, velocity, ocean, *halos, part)[0]
    return new_tracers, solve(got)


def solution(mesh):
    return jax.shard_map(
        shards,
        mesh=mesh,
        in_specs=(
            P(None, None, "bx", "by"),
            P(None, None, "bx", "by"),
            P("bx", "by"),
            P(),
            P("bx", "by"),
        ),
        out_specs=(P(None, None, "bx", "by"), P(("bx", "by"), None)),
        check_vma=False,
    )
```

```python
import functools

import jax
import jax.numpy as jnp
from jax import lax
from jax.experimental import pallas as pl
from jax.experimental.pallas import tpu as pltpu
from jax.sharding import PartitionSpec as P

ITERS = 3
TRACERS = 4
LEVELS = 12
ROWS = 128
COLS = 256
TILES = ROWS // 8
LANE = 128
WIDE = 8 * COLS
EXT = 24
CHUNK = 32
TALL = 16

SPEED, WET, PART, COEF, EDGE, MESSAGE = 48, 60, 64, 68, 72, 80
ANY = pl.BlockSpec(memory_space=pl.ANY)
HBM = pl.BlockSpec(memory_space=pltpu.HBM)
VMEM = pl.BlockSpec(memory_space=pltpu.VMEM)


def f32(*shape):
    return jax.ShapeDtypeStruct(shape, jnp.float32)


def lanes(shape):
    return lax.broadcasted_iota(jnp.int32, shape, len(shape) - 1)


def sublanes(shape):
    return lax.broadcasted_iota(jnp.int32, shape, len(shape) - 2)


def coefficient(depth, wet):
    return depth * (0.1 + 0.9 * wet)


def positive(x):
    return jnp.maximum(x, 0.0)


def negative(x):
    return jnp.minimum(x, 0.0)


def edge_forcing(q, u, v, wet, thick):
    shape = (8, COLS)
    row, col = sublanes(shape), lanes(shape)
    total = jnp.zeros(shape, jnp.float32)
    flux_x = jnp.zeros(shape, jnp.float32)
    flux_y = jnp.zeros(shape, jnp.float32)
    for k in range(LEVELS):
        depth = thick[k]
        total = total + depth * q[k]
        flux_x = flux_x + depth * (positive(u[k]) * q[k] + negative(u[k]) * pltpu.roll(q[k], 7, 0))
        flux_y = flux_y + depth * (positive(v[k]) * q[k] + negative(v[k]) * pltpu.roll(q[k], COLS - 1, 1))
    flux_x = flux_x * jnp.where(row == 7, 0.0, wet * pltpu.roll(wet, 7, 0))
    flux_y = flux_y * jnp.where(col == COLS - 1, 0.0, wet * pltpu.roll(wet, COLS - 1, 1))
    return wet * (total - (flux_x - pltpu.roll(flux_x, 1, 0)) - (flux_y - pltpu.roll(flux_y, 1, 1)))


def edge_terms(q, v, wet, thick):
    lane = lanes((8, LANE))
    last, first = wet[:, LANE:], wet[:, :LANE]
    upwind = jnp.zeros((8, LANE), jnp.float32)
    terms = jnp.where(lane == 28, pltpu.roll(first, 28, 1), 0.0)
    for k in range(LEVELS):
        depth = thick[k]
        speed = v[k][:, LANE:]
        upwind = upwind + depth * positive(speed) * q[k][:, LANE:]
        terms = jnp.where(lane == k, pltpu.roll(depth * negative(speed) * last, k + 1, 1), terms)
        terms = jnp.where(lane == 16 + k, pltpu.roll(q[k][:, :LANE] * first, 16 + k, 1), terms)
    return jnp.where(lane == LEVELS, pltpu.roll(upwind * last, LEVELS + 1, 1), terms)


def pack_kernel(thick_hbm, t_hbm, v_hbm, ocean_hbm, depth_hbm, row_even, row_odd, col_even, col_odd, top,
                t_ref, u_top, u_low, v_top, v_low, v_last, ocean_ref, depth_ref, thick, row_both, col_both, sems):
    odd_x, odd_y = lax.axis_index("bx") % 2, lax.axis_index("by") % 2
    row_hi, row_lo = row_both.at[0], row_both.at[1]
    col_hi, col_lo = col_both.at[0], col_both.at[1]

    def chunk_copy(c):
        rows = pl.ds(pl.multiple_of(c * CHUNK, CHUNK), CHUNK)
        return pltpu.make_async_copy(t_hbm.at[:, :, rows, :], t_ref.at[:, :, rows, :], sems.at[c])

    chunks = ROWS // CHUNK
    small = [
        pltpu.make_async_copy(ocean_hbm, ocean_ref, sems.at[chunks]),
        pltpu.make_async_copy(depth_hbm, depth_ref, sems.at[chunks + 1]),
        pltpu.make_async_copy(v_hbm.at[1, :, :, LANE:], v_last, sems.at[chunks + 2]),
        pltpu.make_async_copy(thick_hbm, thick, sems.at[chunks + 7]),
    ]
    tiles = [
        pltpu.make_async_copy(v_hbm.at[0, :, 0:8, :], u_top, sems.at[chunks + 3]),
        pltpu.make_async_copy(v_hbm.at[0, :, ROWS - 8 :, :], u_low, sems.at[chunks + 4]),
        pltpu.make_async_copy(v_hbm.at[1, :, 0:8, :], v_top, sems.at[chunks + 5]),
        pltpu.make_async_copy(v_hbm.at[1, :, ROWS - 8 :, :], v_low, sems.at[chunks + 6]),
    ]
    for copy in small:
        copy.start()
    for c in range(chunks):
        chunk_copy(c).start()
    for copy in tiles:
        copy.start()
    for copy in small:
        copy.wait()
    wet = ocean_ref[...].astype(jnp.float32)
    coef = coefficient(depth_ref[...], wet)
    most = jnp.max(jnp.max(coef, axis=0, keepdims=True), axis=1, keepdims=True)
    top[...] = jnp.broadcast_to(most[None], top.shape)

    def gather(c, _):
        chunk_copy(c).wait()
        lane = lanes((CHUNK, LANE))
        rows = pl.ds(pl.multiple_of(c * CHUNK, CHUNK), CHUNK)
        ocean = ocean_ref[rows, :].astype(jnp.float32)
        hi = jnp.where(lane == 2 * WET, pltpu.roll(ocean[:, LANE:], (2 * WET + 1) % LANE, 1), 0.0)
        lo = jnp.where(lane == 2 * WET - 1, pltpu.roll(ocean[:, :LANE], 2 * WET - 1, 1), 0.0)
        for k in range(LEVELS):
            for t in range(TRACERS):
                s = t * LEVELS + k
                hi = jnp.where(lane == 2 * s, pltpu.roll(t_ref[t, k, rows, LANE:], 2 * s + 1, 1), hi)
                place = (2 * s - 1) % LANE
                lo = jnp.where(lane == place, pltpu.roll(t_ref[t, k, rows, :LANE], place, 1), lo)
            s = SPEED + k
            hi = jnp.where(lane == 2 * s, pltpu.roll(v_last[k, rows, :], 2 * s + 1, 1), hi)
        col_hi[rows, :] = hi
        col_lo[rows, :] = lo
        return 0

    lax.fori_loop(0, chunks, gather, 0)
    for copy in tiles:
        copy.wait()
    for t in range(TRACERS):
        for k in range(LEVELS):
            s = t * LEVELS + k
            row_hi[s : s + 1, :] = t_ref[t, k, ROWS - 1 : ROWS, :]
            row_lo[s : s + 1, :] = t_ref[t, k, 0:1, :]
    for k in range(LEVELS):
        row_hi[SPEED + k : SPEED + k + 1, :] = u_low[k, 7:8, :]
    row_lo[SPEED:WET, :] = jnp.zeros((WET - SPEED, COLS), jnp.float32)
    for row, message, u, v, keep in ((0, row_lo, u_top, v_top, 0), (ROWS - 8, row_hi, u_low, v_low, 4)):
        rows = slice(row, row + 8)
        here = ocean_ref[rows, :].astype(jnp.float32)
        q = [0.2 * t_ref[0, k, rows, :] - 0.8 * t_ref[1, k, rows, :] for k in range(LEVELS)]
        speed_x = [u[k] for k in range(LEVELS)]
        speed_y = [v[k] for k in range(LEVELS)]
        message[WET:PART, :] = jnp.broadcast_to(here[7:8, :] if keep else here[0:1, :], (PART - WET, COLS))
        message[PART:COEF, :] = edge_forcing(q, speed_x, speed_y, here, thick)[keep : keep + 4, :]
        message[COEF:EDGE, :] = coefficient(depth_ref[rows, :], here)[keep : keep + 4, :]
        message[EDGE:MESSAGE, :LANE] = edge_terms(q, speed_y, here, thick)
        message[EDGE:MESSAGE, LANE:] = jnp.zeros((8, LANE), jnp.float32)
    row_even[...] = row_both[odd_x]
    row_odd[...] = row_both[1 - odd_x]
    col_even[...] = col_both[odd_y]
    col_odd[...] = col_both[1 - odd_y]


def pack(thickness, tracers, velocity, ocean, depth):
    tile = (LEVELS, 8, COLS)
    return pl.pallas_call(
        pack_kernel,
        in_specs=[HBM] * 5,
        out_specs=[VMEM] * 5,
        out_shape=[f32(MESSAGE, COLS), f32(MESSAGE, COLS), f32(ROWS, LANE), f32(ROWS, LANE), f32(16, 8, LANE)],
        scratch_shapes=[
            pltpu.VMEM((TRACERS, LEVELS, ROWS, COLS), jnp.float32),
            pltpu.VMEM(tile, jnp.float32),
            pltpu.VMEM(tile, jnp.float32),
            pltpu.VMEM(tile, jnp.float32),
            pltpu.VMEM(tile, jnp.float32),
            pltpu.VMEM((LEVELS, ROWS, LANE), jnp.float32),
            pltpu.VMEM((ROWS, COLS), jnp.int32),
            pltpu.VMEM((ROWS, COLS), jnp.float32),
            pltpu.SMEM((LEVELS,), jnp.float32),
            pltpu.VMEM((2, MESSAGE, COLS), jnp.float32),
            pltpu.VMEM((2, ROWS, LANE), jnp.float32),
            pltpu.SemaphoreType.DMA((ROWS // CHUNK + 8,)),
        ],
        compiler_params=pltpu.CompilerParams(vmem_limit_bytes=60 * 2**20),
        cost_estimate=pl.CostEstimate(flops=4_000_000, bytes_accessed=7_400_000, transcendentals=0),
        name="pack_edges",
    )(thickness, tracers, velocity, ocean, depth)


def ahead_y(x, edge):
    last = lanes((x.shape[0], LANE)) == LANE - 1
    a, b = pltpu.roll(x[:, :LANE], LANE - 1, 1), pltpu.roll(x[:, LANE:], LANE - 1, 1)
    return jnp.concatenate([jnp.where(last, b, a), jnp.where(last, edge, b)], 1)


def behind_y(x, edge):
    first = lanes((x.shape[0], LANE)) == 0
    a, b = pltpu.roll(x[:, :LANE], 1, 1), pltpu.roll(x[:, LANE:], 1, 1)
    return jnp.concatenate([jnp.where(first, edge, a), jnp.where(first, a, b)], 1)


def above(load, edge, r, tall=8):
    if (r + 1) * tall < ROWS:
        return load(tall * r + 1)
    return jnp.where(sublanes((tall, COLS)) == tall - 1, edge, pltpu.roll(load(tall * r), tall - 1, 0))


def upwind(speed, here, ahead):
    return speed * jnp.where(speed > 0.0, here, ahead)


def advect_kernel(first, *refs):
    if first == 0:
        (thick_hbm, t_hbm, v_hbm, ocean_hbm, row_even, row_odd, col_even, col_odd, depth_hbm, out_hbm, send_ref,
         t_ref, v_ref, out_ref, ocean_ref, rows_in, cols_in, w_x, w_y, before_y, edges, sems, small_sems,
         depth_ref, total, flux, ext, thick) = refs
    else:
        (t_hbm, v_hbm, ocean_hbm, row_even, row_odd, col_even, col_odd, _, out_hbm,
         t_ref, v_ref, out_ref, ocean_ref, rows_in, cols_in, w_x, w_y, before_y, edges, sems, small_sems) = refs
    odd_x, odd_y = lax.axis_index("bx") % 2, lax.axis_index("by") % 2
    row_lo, row_hi = rows_in.at[0], rows_in.at[1]
    small = [
        (ocean_hbm, ocean_ref),
        (row_even, rows_in.at[1 - odd_x]),
        (row_odd, rows_in.at[odd_x]),
        (col_even, cols_in.at[1 - odd_y]),
        (col_odd, cols_in.at[odd_y]),
    ]
    if first == 0:
        small += [(depth_hbm, depth_ref), (thick_hbm, thick)]
    small = [pltpu.make_async_copy(a, b, small_sems.at[i]) for i, (a, b) in enumerate(small)]

    def tracers_in(k):
        return pltpu.make_async_copy(t_hbm.at[first : first + 2, k], t_ref.at[:, k], sems.at[0, k])

    def velocity_in(k):
        return pltpu.make_async_copy(v_hbm.at[:, k], v_ref.at[:, k], sems.at[1, k])

    def tracers_out(k):
        return pltpu.make_async_copy(out_ref.at[:, k], out_hbm.at[first : first + 2, k], sems.at[2, k])

    for copy in small:
        copy.start()
    for k in range(LEVELS):
        tracers_in(k).start()
        velocity_in(k).start()
    for copy in small:
        copy.wait()
    even = lanes((8, LANE)) % 2 == 0
    load_wet = lambda at: ocean_ref[at : at + 8, :].astype(jnp.float32)
    for r in range(TILES):
        rows = pl.ds(8 * r, 8)
        edge = jnp.where(even, cols_in[0, rows, :], cols_in[1, rows, :])
        for k in range(LEVELS):
            for i, slot in enumerate((first * LEVELS + k, (first + 1) * LEVELS + k, SPEED + k)):
                edges[i, k, rows, :] = pltpu.roll(edge, (LANE - 2 * slot) % LANE, 1)
        here = load_wet(8 * r)
        wet_edge = pltpu.roll(edge, LANE - 2 * WET, 1)
        w_x[rows, :] = here * above(load_wet, row_hi[WET : WET + 1, :], r)
        w_y[rows, :] = here * ahead_y(here, wet_edge)
        before_y[rows, :] = here[:, :LANE] * wet_edge
        if first == 0:
            total[rows, :] = jnp.zeros((8, COLS), jnp.float32)
    w_before = load_wet(0)[0:1, :] * row_lo[WET : WET + 1, :]
    if first == 0:
        flux[...] = jnp.zeros((8, COLS), jnp.float32)

    def level(k, _):
        tracers_in(k).wait()
        velocity_in(k).wait()
        u_before = row_lo[pl.ds(SPEED + k, 1), :] * w_before
        into_x = [upwind(u_before, row_lo[pl.ds((first + t) * LEVELS + k, 1), :], t_ref[t, k, 0:1, :]) for t in range(2)]
        carry, out_x = list(into_x), [None, None]
        for r in range(ROWS // TALL):
            rows = pl.ds(TALL * r, TALL)
            u = v_ref[0, k, rows, :] * w_x[rows, :]
            v = v_ref[1, k, rows, :] * w_y[rows, :]
            v_before = edges[2, k, rows, :] * before_y[rows, :]
            new = []
            for t in range(2):
                load = lambda at: t_ref[t, k, at : at + TALL, :]
                slot = (first + t) * LEVELS + k
                c = load(TALL * r)
                c_edge = edges[t, k, rows, :]
                here_x = upwind(u, c, above(load, row_hi[pl.ds(slot, 1), :], r, TALL))
                turned = pltpu.roll(here_x, 1, 0)
                past_x = jnp.where(sublanes((TALL, COLS)) == 0, carry[t], turned)
                carry[t] = turned[0:1, :]
                if r == ROWS // TALL - 1:
                    out_x[t] = here_x[TALL - 1 :, :]
                here_y = upwind(v, c, ahead_y(c, c_edge))
                past_y = behind_y(here_y, upwind(v_before, c_edge, c[:, :LANE]))
                value = (c - (here_x - past_x)) - (here_y - past_y)
                out_ref[t, k, rows, :] = value
                new.append(value)
            if first == 0:
                total[rows, :] = total[rows, :] + ((0.2 * thick[k]) * new[0] - (0.8 * thick[k]) * new[1])
        if first == 0:
            flux[0:1, :] = flux[0:1, :] + thick[k] * (0.2 * into_x[0] - 0.8 * into_x[1])
            flux[1:2, :] = flux[1:2, :] + thick[k] * (0.2 * out_x[0] - 0.8 * out_x[1])
        tracers_out(k).start()
        return 0

    lax.fori_loop(0, LEVELS, level, 0)

    if first == 0:
        row = sublanes((4, COLS))
        ext[0, 0:4, :] = row_lo[PART:COEF, :] - jnp.where(row == 3, flux[0:1, :], 0.0)
        ext[0, ROWS + 4 :, :] = row_hi[PART:COEF, :] + jnp.where(row == 0, flux[1:2, :], 0.0)
        ext[1, 0:4, :] = row_lo[COEF:EDGE, :]
        ext[1, ROWS + 4 :, :] = row_hi[COEF:EDGE, :]
        for r in range(TILES):
            rows = pl.ds(8 * r, 8)
            here = load_wet(8 * r)
            ext[0, 8 * r + 4 : 8 * r + 12, :] = total[rows, :] * here
            ext[1, 8 * r + 4 : 8 * r + 12, :] = coefficient(depth_ref[rows, :], here)
        tile = sublanes((8, LANE))
        for j in range(8):
            send_ref[j, 0:EXT, :] = ext[0, 16 * j : 16 * j + EXT, :]
            send_ref[j, EXT : 2 * EXT, :] = ext[1, 16 * j : 16 * j + EXT, :]
            edge = jnp.zeros((8, LANE), jnp.float32)
            if j == 0:
                edge = jnp.where((tile >= 1) & (tile <= 3), pltpu.roll(row_lo[EDGE:MESSAGE, :LANE], 4, 0), 0.0)
            if j == 7:
                edge = jnp.where((tile >= 4) & (tile <= 6), pltpu.roll(row_hi[EDGE:MESSAGE, :LANE], 4, 0), 0.0)
            send_ref[j, 2 * EXT : 2 * EXT + 8, :LANE] = edge
            send_ref[j, 2 * EXT : 2 * EXT + 8, LANE:] = jnp.zeros((8, LANE), jnp.float32)
    for k in range(LEVELS):
        tracers_out(k).wait()


def advect(first, tracers, velocity, ocean, row_even, row_odd, col_even, col_odd, extra):
    ins = [HBM] * 3 + [ANY] * 4
    operands = [tracers, velocity, ocean, row_even, row_odd, col_even, col_odd]
    out_specs = [HBM]
    out_shape = [f32(TRACERS, LEVELS, ROWS, COLS)]
    block = pltpu.VMEM((ROWS, COLS), jnp.float32)
    narrow = pltpu.VMEM((ROWS, LANE), jnp.float32)
    scratch = [
        pltpu.VMEM((2, LEVELS, ROWS, COLS), jnp.float32),
        pltpu.VMEM((2, LEVELS, ROWS, COLS), jnp.float32),
        pltpu.VMEM((2, LEVELS, ROWS, COLS), jnp.float32),
        pltpu.VMEM((ROWS, COLS), jnp.int32),
        pltpu.VMEM((2, MESSAGE, COLS), jnp.float32),
        pltpu.VMEM((2, ROWS, LANE), jnp.float32),
        block,
        block,
        narrow,
        pltpu.VMEM((3, LEVELS, ROWS, LANE), jnp.float32),
        pltpu.SemaphoreType.DMA((3, LEVELS)),
        pltpu.SemaphoreType.DMA((8,)),
    ]
    aliases = {}
    if first == 0:
        thickness, depth = extra
        ins = [HBM] + ins + [HBM]
        operands = [thickness] + operands + [depth]
        out_specs.append(VMEM)
        out_shape.append(f32(8, 2 * EXT + 8, COLS))
        scratch += [
            block,
            block,
            pltpu.VMEM((8, COLS), jnp.float32),
            pltpu.VMEM((2, ROWS + 8, COLS), jnp.float32),
            pltpu.SMEM((LEVELS,), jnp.float32),
        ]
    else:
        aliases = {len(operands): 0}
        ins = ins + [HBM]
        operands = operands + [extra]
    return pl.pallas_call(
        functools.partial(advect_kernel, first),
        in_specs=ins,
        out_specs=out_specs,
        out_shape=out_shape,
        scratch_shapes=scratch,
        input_output_aliases=aliases,
        compiler_params=pltpu.CompilerParams(vmem_limit_bytes=48 * 2**20),
        cost_estimate=pl.CostEstimate(flops=24_000_000, bytes_accessed=9_400_000, transcendentals=0),
        name="advect_forcing" if first == 0 else "advect_rest",
    )(*operands)


def insert_kernel(_, tops, out_hbm, most, sem):
    top = jnp.max(tops[...], axis=0)
    for j in range(8):
        most[j] = top
    copy = pltpu.make_async_copy(most, out_hbm.at[:, 2 * EXT :, LANE:], sem.at[0])
    copy.start()
    copy.wait()


def insert(parcels, tops):
    return pl.pallas_call(
        insert_kernel,
        in_specs=[HBM, VMEM],
        out_specs=HBM,
        out_shape=f32(8, 2 * EXT + 8, COLS),
        scratch_shapes=[pltpu.VMEM((8, 8, LANE), jnp.float32), pltpu.SemaphoreType.DMA((1,))],
        input_output_aliases={0: 0},
        compiler_params=pltpu.CompilerParams(vmem_limit_bytes=48 * 2**20),
        cost_estimate=pl.CostEstimate(flops=1000, bytes_accessed=100_000, transcendentals=0),
        name="insert_maximum",
    )(parcels, tops)


NEAR = ((1, 0, 0.5), (-1, 0, 0.5), (0, 1, 0.5), (0, -1, 0.5), (1, 1, 0.125), (1, -1, 0.125), (-1, 1, 0.125), (-1, -1, 0.125))


def moved(x, rows, cols):
    if cols:
        lane = lanes(x.shape)
        x = pltpu.roll(x, (-cols) % x.shape[1], 1)
        x = jnp.where(lane == (x.shape[1] - 1 if cols > 0 else 0), 0.0, x)
    if rows:
        x = pltpu.roll(x, (-rows) % x.shape[0], 0)
    return x


def solve_kernel(got, out_ref, h_ref, f_ref, misc, weight, sems):
    copies = []
    for j in range(8):
        cols = pl.ds(j * COLS, COLS)
        copies.append(pltpu.make_async_copy(got.at[j, 0:EXT, :], f_ref.at[:, cols], sems.at[0, j]))
        copies.append(pltpu.make_async_copy(got.at[j, EXT : 2 * EXT, :], h_ref.at[:, cols], sems.at[1, j]))
        copies.append(pltpu.make_async_copy(got.at[j, 2 * EXT :, :], misc.at[j], sems.at[2, j]))
    for copy in copies:
        copy.start()
    for copy in copies:
        copy.wait()
    lane, tile = lanes((8, LANE)), sublanes((8, LANE))
    for j in range(7):
        pairs = misc[j, :, :LANE] * pltpu.roll(misc[j + 1, :, :LANE], LANE - 16, 1)
        flux = jnp.sum(jnp.where(lane <= LEVELS, pairs, 0.0), axis=1, keepdims=True)
        for rows, there in ((pl.ds(0, 8), tile < 4), (pl.ds(16, 8), tile >= 4)):
            last = pl.ds((j + 1) * COLS - LANE, LANE)
            after = pl.ds((j + 1) * COLS, LANE)
            f_ref[rows, last] = f_ref[rows, last] - jnp.where(there & (lane == LANE - 1), flux, 0.0)
            f_ref[rows, after] = f_ref[rows, after] + jnp.where(there & (lane == 0), flux, 0.0)
    most = jnp.max(misc[:, :, LANE:], axis=0)[0:1, 0:1]
    lam_max = 0.5 + 10.0 * most
    theta = (lam_max + 0.5) / 2.0
    delta = (lam_max - 0.5) / 2.0
    sigma = theta / delta
    rho = 1.0 / sigma
    h = h_ref[...]
    sides = {c: moved(h, 0, c) for c in (-1, 0, 1)}
    for n, (a, b, w) in enumerate(NEAR):
        weight[n] = w * (h + moved(sides[b], a, 0))
    inside = h > 0.0
    resid = f_ref[...]
    direction = resid / theta
    answer = jnp.zeros_like(resid)
    for _ in range(ITERS):
        sides = {c: moved(direction, 0, c) for c in (-1, 0, 1)}
        applied = 0.5 * direction
        for n, (a, b, w) in enumerate(NEAR):
            applied = applied + weight[n] * (direction - moved(sides[b], a, 0))
        resid = jnp.where(inside, resid - applied, 0.0)
        answer = answer + direction
        rho_next = 1.0 / (2.0 * sigma - rho)
        direction = rho_next * rho * direction + (2.0 * rho_next / delta) * resid
        rho = rho_next
    out_ref[...] = (answer + direction)[4:20, :]


def solve(got):
    return pl.pallas_call(
        solve_kernel,
        in_specs=[ANY],
        out_specs=VMEM,
        out_shape=f32(16, WIDE),
        scratch_shapes=[
            pltpu.VMEM((EXT, WIDE), jnp.float32),
            pltpu.VMEM((EXT, WIDE), jnp.float32),
            pltpu.VMEM((8, 8, COLS), jnp.float32),
            pltpu.VMEM((8, EXT, WIDE), jnp.float32),
            pltpu.SemaphoreType.DMA((3, 8)),
        ],
        compiler_params=pltpu.CompilerParams(vmem_limit_bytes=12 * 2**20),
        cost_estimate=pl.CostEstimate(flops=6_000_000, bytes_accessed=600_000, transcendentals=0),
        name="chebyshev",
    )(got)


def exchange(x, axis, odd):
    count = lax.axis_size(axis)
    pairs = []
    for i in range(odd, count - 1, 2):
        pairs += [(i, i + 1), (i + 1, i)]
    return lax.ppermute(x, axis, pairs)


def shards(tracers, velocity, ocean, thickness, depth):
    row_even, row_odd, col_even, col_odd, top = pack(thickness, tracers, velocity, ocean, depth)
    halos = (exchange(row_even, "bx", 0), exchange(row_odd, "bx", 1), exchange(col_even, "by", 0), exchange(col_odd, "by", 1))
    tops = lax.all_to_all(top, "bx", split_axis=0, concat_axis=0, tiled=True)
    part, parcels = advect(0, tracers, velocity, ocean, *halos, (thickness, depth))
    got = lax.all_to_all(insert(parcels, tops), "by", split_axis=0, concat_axis=0, tiled=True)
    new_tracers = advect(2, tracers, velocity, ocean, *halos, part)[0]
    return new_tracers, solve(got)


def solution(mesh):
    return jax.shard_map(
        shards,
        mesh=mesh,
        in_specs=(
            P(None, None, "bx", "by"),
            P(None, None, "bx", "by"),
            P("bx", "by"),
            P(),
            P("bx", "by"),
        ),
        out_specs=(P(None, None, "bx", "by"), P(("bx", "by"), None)),
        check_vma=False,
    )
```

```python
import functools

import jax
import jax.numpy as jnp
from jax import lax
from jax.experimental import pallas as pl
from jax.experimental.pallas import tpu as pltpu
from jax.sharding import PartitionSpec as P

ITERS = 3
TRACERS = 4
LEVELS = 12
ROWS = 128
COLS = 256
TILES = ROWS // 8
LANE = 128
WIDE = 8 * COLS
EXT = 24
CHUNK = 32
TALL = 16

SPEED, WET, PART, COEF, EDGE, MIXED, MESSAGE = 48, 60, 64, 68, 72, 80, 96
MOST = 100
ANY = pl.BlockSpec(memory_space=pl.ANY)
HBM = pl.BlockSpec(memory_space=pltpu.HBM)
VMEM = pl.BlockSpec(memory_space=pltpu.VMEM)


def f32(*shape):
    return jax.ShapeDtypeStruct(shape, jnp.float32)


def lanes(shape):
    return lax.broadcasted_iota(jnp.int32, shape, len(shape) - 1)


def sublanes(shape):
    return lax.broadcasted_iota(jnp.int32, shape, len(shape) - 2)


def coefficient(depth, wet):
    return depth * (0.1 + 0.9 * wet)


def positive(x):
    return jnp.maximum(x, 0.0)


def negative(x):
    return jnp.minimum(x, 0.0)


def upwind(speed, here, ahead):
    return speed * jnp.where(speed > 0.0, here, ahead)


def edge_terms(hi, lo, wet, thick_lanes):
    lane = lanes(hi.shape)
    used = (lane % 2 == 0) & (lane < 2 * LEVELS)
    last = jnp.broadcast_to(wet[:, COLS - 1 :], hi.shape)
    first = jnp.broadcast_to(wet[:, 0:1], hi.shape)
    speed = jnp.where(used, pltpu.roll(hi, LANE - 2 * SPEED, 1), 0.0)
    q_last = thick_lanes * (0.2 * hi - 0.8 * pltpu.roll(hi, LANE - 2 * LEVELS, 1))
    share = jnp.sum(jnp.where(speed > 0.0, speed * q_last, 0.0), axis=1, keepdims=True)
    terms = jnp.where(lane == 2 * LEVELS, share, jnp.minimum(speed, 0.0)) * last
    turned = pltpu.roll(lo, 65, 1)
    q_first = pltpu.roll(thick_lanes, 64, 1) * (0.2 * turned - 0.8 * pltpu.roll(turned, LANE - 2 * LEVELS, 1))
    used = (lane % 2 == 0) & (lane >= 64) & (lane < 64 + 2 * LEVELS)
    return terms + jnp.where(used, q_first, jnp.where(lane == 64 + 2 * LEVELS, 1.0, 0.0)) * first


def pack_kernel(thick_hbm, t_hbm, v_hbm, ocean_hbm, depth_hbm, row_even, row_odd, col_even, col_odd, top, part, terms,
                t_ref, v_ref, ocean_ref, depth_ref, thick, row_both, col_both, total, flux_x, flux_y, sems):
    odd_x, odd_y = lax.axis_index("bx") % 2, lax.axis_index("by") % 2
    row_hi, row_lo = row_both.at[0], row_both.at[1]
    col_hi, col_lo = col_both.at[0], col_both.at[1]
    chunks = ROWS // CHUNK

    def chunk_copies(c):
        rows = pl.ds(pl.multiple_of(c * CHUNK, CHUNK), CHUNK)
        return (
            pltpu.make_async_copy(t_hbm.at[:, :, rows, :], t_ref.at[:, :, rows, :], sems.at[0, c]),
            pltpu.make_async_copy(v_hbm.at[:, :, rows, :], v_ref.at[:, :, rows, :], sems.at[1, c]),
        )

    small = [
        pltpu.make_async_copy(ocean_hbm, ocean_ref, sems.at[2, 0]),
        pltpu.make_async_copy(depth_hbm, depth_ref, sems.at[2, 1]),
        pltpu.make_async_copy(thick_hbm, thick, sems.at[2, 2]),
    ]
    for copy in small:
        copy.start()
    for c in range(chunks):
        for copy in chunk_copies(c):
            copy.start()
    for copy in small:
        copy.wait()
    wet = ocean_ref[...].astype(jnp.float32)
    coef = coefficient(depth_ref[...], wet)
    most = jnp.max(jnp.max(coef, axis=0, keepdims=True), axis=1, keepdims=True)
    top[...] = jnp.broadcast_to(most[None], top.shape)
    thick_lanes = jnp.zeros((1, LANE), jnp.float32)
    for k in range(LEVELS):
        thick_lanes = jnp.where(lanes((1, LANE)) == 2 * k, thick[k], thick_lanes)

    def gather(c, _):
        for copy in chunk_copies(c):
            copy.wait()
        lane = lanes((CHUNK, LANE))
        rows = pl.ds(pl.multiple_of(c * CHUNK, CHUNK), CHUNK)
        before = pl.ds(jnp.maximum(c * CHUNK - 1, 0), 1)
        start = pl.ds(pl.multiple_of(c * CHUNK, CHUNK), 1)
        ocean = ocean_ref[rows, :].astype(jnp.float32)
        hi = jnp.where(lane == 2 * WET, pltpu.roll(ocean[:, LANE:], (2 * WET + 1) % LANE, 1), 0.0)
        lo = jnp.where(lane == 2 * WET - 1, pltpu.roll(ocean[:, :LANE], 2 * WET - 1, 1), 0.0)
        for k in range(LEVELS):
            for t in range(TRACERS):
                s = t * LEVELS + k
                hi = jnp.where(lane == 2 * s, pltpu.roll(t_ref[t, k, rows, LANE:], 2 * s + 1, 1), hi)
                place = (2 * s - 1) % LANE
                lo = jnp.where(lane == place, pltpu.roll(t_ref[t, k, rows, :LANE], place, 1), lo)
            s = SPEED + k
            hi = jnp.where(lane == 2 * s, pltpu.roll(v_ref[1, k, rows, LANE:], 2 * s + 1, 1), hi)
        col_hi[rows, :] = hi
        col_lo[rows, :] = lo
        terms[rows, :] = edge_terms(hi, lo, ocean, thick_lanes)
        whole = jnp.zeros((CHUNK, COLS), jnp.float32)
        out_x = jnp.zeros((CHUNK, COLS), jnp.float32)
        out_y = jnp.zeros((CHUNK, COLS), jnp.float32)
        between = jnp.zeros((1, COLS), jnp.float32)
        for k in range(LEVELS):
            warm, salt = 0.2 * thick[k], 0.8 * thick[k]
            q = warm * t_ref[0, k, rows, :] - salt * t_ref[1, k, rows, :]
            whole = whole + q
            out_x = out_x + upwind(v_ref[0, k, rows, :], q, pltpu.roll(q, CHUNK - 1, 0))
            out_y = out_y + upwind(v_ref[1, k, rows, :], q, pltpu.roll(q, COLS - 1, 1))
            mixed = lambda at: warm * t_ref[0, k, at, :] - salt * t_ref[1, k, at, :]
            between = between + upwind(v_ref[0, k, before, :], mixed(before), mixed(start))
        total[rows, :] = whole
        flux_y[rows, :] = out_y
        flux_x[before, :] = between
        flux_x[rows, :] = out_x
        return 0

    lax.fori_loop(0, chunks, gather, 0)
    load_wet = lambda at: ocean_ref[at : at + 8, :].astype(jnp.float32)
    row, col = sublanes((8, COLS)), lanes((8, COLS))
    turned = jnp.zeros((8, COLS), jnp.float32)
    for r in range(TILES):
        rows = pl.ds(8 * r, 8)
        here = load_wet(8 * r)
        out_x = flux_x[rows, :] * here
        if r < TILES - 1:
            out_x = out_x * load_wet(8 * r + 1)
        else:
            out_x = jnp.where(row == 7, 0.0, out_x * pltpu.roll(here, 7, 0))
        out_y = jnp.where(col == COLS - 1, 0.0, flux_y[rows, :] * (here * pltpu.roll(here, COLS - 1, 1)))
        past = turned
        turned = pltpu.roll(out_x, 1, 0)
        past_x = jnp.where(row == 0, past, turned)
        part[rows, :] = here * (total[rows, :] - (out_x - past_x) - (out_y - pltpu.roll(out_y, 1, 1)))
    for t in range(TRACERS):
        for k in range(LEVELS):
            s = t * LEVELS + k
            row_hi[s : s + 1, :] = t_ref[t, k, ROWS - 1 : ROWS, :]
            row_lo[s : s + 1, :] = t_ref[t, k, 0:1, :]
    row_lo[SPEED:WET, :] = jnp.zeros((WET - SPEED, COLS), jnp.float32)
    for k in range(LEVELS):
        row_hi[SPEED + k : SPEED + k + 1, :] = v_ref[0, k, ROWS - 1 : ROWS, :]
        for message, at in ((row_hi, ROWS - 1), (row_lo, 0)):
            line = slice(at, at + 1)
            message[MIXED + k : MIXED + k + 1, :] = (0.2 * thick[k]) * t_ref[0, k, line, :] - (0.8 * thick[k]) * t_ref[1, k, line, :]
    for message, rows, edge in ((row_hi, slice(ROWS - 4, ROWS), ROWS - 1), (row_lo, slice(0, 4), 0)):
        tile = slice(rows.start // 8 * 8, rows.start // 8 * 8 + 8)
        here = load_wet(tile.start)
        keep = slice(rows.start - tile.start, rows.stop - tile.start)
        message[WET:PART, :] = jnp.broadcast_to(here[edge - tile.start : edge - tile.start + 1, :], (PART - WET, COLS))
        message[PART:COEF, :] = part[tile, :][keep, :]
        message[COEF:EDGE, :] = coefficient(depth_ref[tile, :], here)[keep, :]
        message[EDGE:MIXED, :LANE] = terms[tile, :]
        message[EDGE:MIXED, LANE:] = jnp.zeros((8, LANE), jnp.float32)
        message[MIXED + LEVELS :, :] = jnp.zeros((MESSAGE - MIXED - LEVELS, COLS), jnp.float32)
    row_even[...] = row_both[odd_x]
    row_odd[...] = row_both[1 - odd_x]
    col_even[...] = col_both[odd_y]
    col_odd[...] = col_both[1 - odd_y]


def pack(thickness, tracers, velocity, ocean, depth):
    block = pltpu.VMEM((ROWS, COLS), jnp.float32)
    return pl.pallas_call(
        pack_kernel,
        in_specs=[HBM] * 5,
        out_specs=[VMEM] * 7,
        out_shape=[f32(MESSAGE, COLS)] * 2 + [f32(ROWS, LANE)] * 2 + [f32(16, 8, LANE), f32(ROWS, COLS), f32(ROWS, LANE)],
        scratch_shapes=[
            pltpu.VMEM((TRACERS, LEVELS, ROWS, COLS), jnp.float32),
            pltpu.VMEM((2, LEVELS, ROWS, COLS), jnp.float32),
            pltpu.VMEM((ROWS, COLS), jnp.int32),
            block,
            pltpu.SMEM((LEVELS,), jnp.float32),
            pltpu.VMEM((2, MESSAGE, COLS), jnp.float32),
            pltpu.VMEM((2, ROWS, LANE), jnp.float32),
            block,
            block,
            block,
            pltpu.SemaphoreType.DMA((3, 4)),
        ],
        compiler_params=pltpu.CompilerParams(vmem_limit_bytes=60 * 2**20),
        cost_estimate=pl.CostEstimate(flops=20_000_000, bytes_accessed=9_400_000, transcendentals=0),
        name="pack_edges",
    )(thickness, tracers, velocity, ocean, depth)


def parcel_kernel(even_hbm, odd_hbm, own_even_hbm, own_odd_hbm, part_hbm, terms_hbm, ocean_hbm, depth_hbm, tops_hbm, send_ref,
                  rows_in, rows_out, part, terms, ocean_ref, depth_ref, tops, ext, ext_terms, sems):
    odd_x = lax.axis_index("bx") % 2
    copies = [
        (even_hbm, rows_in.at[1 - odd_x]),
        (odd_hbm, rows_in.at[odd_x]),
        (own_even_hbm, rows_out.at[1 - odd_x]),
        (own_odd_hbm, rows_out.at[odd_x]),
        (part_hbm, part),
        (terms_hbm, terms),
        (ocean_hbm, ocean_ref),
        (depth_hbm, depth_ref),
        (tops_hbm, tops),
    ]
    copies = [pltpu.make_async_copy(a, b, sems.at[i]) for i, (a, b) in enumerate(copies)]
    for copy in copies:
        copy.start()
    for copy in copies:
        copy.wait()
    before, after, first, last = rows_in.at[0], rows_in.at[1], rows_out.at[0], rows_out.at[1]
    speed, mixed, wet = slice(SPEED, WET), slice(MIXED, MIXED + LEVELS), slice(WET, WET + 1)
    flux_lo = jnp.sum(upwind(before[speed, :], before[mixed, :], first[mixed, :]), axis=0, keepdims=True)
    flux_hi = jnp.sum(upwind(last[speed, :], last[mixed, :], after[mixed, :]), axis=0, keepdims=True)
    flux_lo = flux_lo * (before[wet, :] * first[wet, :])
    flux_hi = flux_hi * (last[wet, :] * after[wet, :])
    row = sublanes((4, COLS))
    ext[0, 0:4, :] = before[PART:COEF, :] - jnp.where(row == 3, flux_lo, 0.0)
    ext[0, ROWS + 4 :, :] = after[PART:COEF, :] + jnp.where(row == 0, flux_hi, 0.0)
    ext[1, 0:4, :] = before[COEF:EDGE, :]
    ext[1, ROWS + 4 :, :] = after[COEF:EDGE, :]
    ext_terms[0:4, :] = before[EDGE + 4 : MIXED, :LANE]
    ext_terms[ROWS + 4 :, :] = after[EDGE : EDGE + 4, :LANE]
    row = sublanes((8, COLS))
    for r in range(TILES):
        rows = slice(8 * r, 8 * r + 8)
        value = part[rows, :]
        if r == 0:
            value = value + jnp.where(row == 0, flux_lo, 0.0)
        if r == TILES - 1:
            value = value - jnp.where(row == 7, flux_hi, 0.0)
        ext[0, 8 * r + 4 : 8 * r + 12, :] = value
        ext[1, 8 * r + 4 : 8 * r + 12, :] = coefficient(depth_ref[rows, :], ocean_ref[rows, :].astype(jnp.float32))
        ext_terms[8 * r + 4 : 8 * r + 12, :] = terms[rows, :]
    most = jnp.max(tops[...], axis=0)[0:1, :]
    for j in range(8):
        at = 16 * j
        send_ref[j, 0:22, :] = ext[0, at + 1 : at + 23, :]
        send_ref[j, 22:44, :] = ext[1, at + 1 : at + 23, :]
        for half in range(2):
            value = ext_terms[at + 12 * half : at + 12 * half + 12, :]
            send_ref[j, 44:56, half * LANE : (half + 1) * LANE] = jnp.where(lanes((12, LANE)) == MOST, most, value)


def parcel(even, odd, own_even, own_odd, part, terms, ocean, depth, tops):
    block = pltpu.VMEM((ROWS, COLS), jnp.float32)
    return pl.pallas_call(
        parcel_kernel,
        in_specs=[ANY] * 9,
        out_specs=VMEM,
        out_shape=f32(8, 56, COLS),
        scratch_shapes=[
            pltpu.VMEM((2, MESSAGE, COLS), jnp.float32),
            pltpu.VMEM((2, MESSAGE, COLS), jnp.float32),
            block,
            pltpu.VMEM((ROWS, LANE), jnp.float32),
            pltpu.VMEM((ROWS, COLS), jnp.int32),
            block,
            pltpu.VMEM((16, 8, LANE), jnp.float32),
            pltpu.VMEM((2, ROWS + 8, COLS), jnp.float32),
            pltpu.VMEM((ROWS + 8, LANE), jnp.float32),
            pltpu.SemaphoreType.DMA((9,)),
        ],
        compiler_params=pltpu.CompilerParams(vmem_limit_bytes=53 * 2**20),
        cost_estimate=pl.CostEstimate(flops=1_000_000, bytes_accessed=1_500_000, transcendentals=0),
        name="parcels",
    )(even, odd, own_even, own_odd, part, terms, ocean, depth, tops)


def ahead_y(x, edge):
    last = lanes((x.shape[0], LANE)) == LANE - 1
    a, b = pltpu.roll(x[:, :LANE], LANE - 1, 1), pltpu.roll(x[:, LANE:], LANE - 1, 1)
    return jnp.concatenate([jnp.where(last, b, a), jnp.where(last, edge, b)], 1)


def behind_y(x, edge):
    first = lanes((x.shape[0], LANE)) == 0
    a, b = pltpu.roll(x[:, :LANE], 1, 1), pltpu.roll(x[:, LANE:], 1, 1)
    return jnp.concatenate([jnp.where(first, edge, a), jnp.where(first, a, b)], 1)


def above(load, edge, r, tall=8):
    if (r + 1) * tall < ROWS:
        return load(tall * r + 1)
    return jnp.where(sublanes((tall, COLS)) == tall - 1, edge, pltpu.roll(load(tall * r), tall - 1, 0))


def advect_kernel(t_hbm, v_hbm, ocean_hbm, row_even, row_odd, col_even, col_odd, out_hbm,
                  t_ref, v_ref, out_ref, ocean_ref, rows_in, cols_in, w_x, w_y, before_y, edges, sems, small_sems):
    odd_x, odd_y = lax.axis_index("bx") % 2, lax.axis_index("by") % 2
    row_lo, row_hi = rows_in.at[0], rows_in.at[1]
    small = [
        (ocean_hbm, ocean_ref),
        (row_even, rows_in.at[1 - odd_x]),
        (row_odd, rows_in.at[odd_x]),
        (col_even, cols_in.at[1 - odd_y]),
        (col_odd, cols_in.at[odd_y]),
    ]
    small = [pltpu.make_async_copy(a, b, small_sems.at[i]) for i, (a, b) in enumerate(small)]

    def tracers_in(k):
        return pltpu.make_async_copy(t_hbm.at[:, k], t_ref.at[:, k], sems.at[0, k])

    def velocity_in(k):
        return pltpu.make_async_copy(v_hbm.at[:, k], v_ref.at[:, k], sems.at[1, k])

    def tracers_out(k):
        return pltpu.make_async_copy(out_ref.at[:, k], out_hbm.at[:, k], sems.at[2, k])

    for copy in small:
        copy.start()
    for k in range(LEVELS):
        tracers_in(k).start()
        velocity_in(k).start()
    for copy in small:
        copy.wait()
    even = lanes((8, LANE)) % 2 == 0
    load_wet = lambda at: ocean_ref[at : at + 8, :].astype(jnp.float32)
    for r in range(TILES):
        rows = pl.ds(8 * r, 8)
        edge = jnp.where(even, cols_in[0, rows, :], cols_in[1, rows, :])
        for k in range(LEVELS):
            for i in range(TRACERS + 1):
                edges[i, k, rows, :] = pltpu.roll(edge, (LANE - 2 * (i * LEVELS + k)) % LANE, 1)
        here = load_wet(8 * r)
        wet_edge = pltpu.roll(edge, LANE - 2 * WET, 1)
        w_x[rows, :] = here * above(load_wet, row_hi[WET : WET + 1, :], r)
        w_y[rows, :] = here * ahead_y(here, wet_edge)
        before_y[rows, :] = here[:, :LANE] * wet_edge
    w_before = load_wet(0)[0:1, :] * row_lo[WET : WET + 1, :]

    def level(k, _):
        tracers_in(k).wait()
        velocity_in(k).wait()
        u_before = row_lo[pl.ds(SPEED + k, 1), :] * w_before
        carry = [upwind(u_before, row_lo[pl.ds(t * LEVELS + k, 1), :], t_ref[t, k, 0:1, :]) for t in range(TRACERS)]
        for r in range(ROWS // TALL):
            rows = pl.ds(TALL * r, TALL)
            u = v_ref[0, k, rows, :] * w_x[rows, :]
            v = v_ref[1, k, rows, :] * w_y[rows, :]
            v_before = edges[TRACERS, k, rows, :] * before_y[rows, :]
            for t in range(TRACERS):
                load = lambda at: t_ref[t, k, at : at + TALL, :]
                c = load(TALL * r)
                c_edge = edges[t, k, rows, :]
                here_x = upwind(u, c, above(load, row_hi[pl.ds(t * LEVELS + k, 1), :], r, TALL))
                turned = pltpu.roll(here_x, 1, 0)
                past_x = jnp.where(sublanes((TALL, COLS)) == 0, carry[t], turned)
                carry[t] = turned[0:1, :]
                here_y = upwind(v, c, ahead_y(c, c_edge))
                past_y = behind_y(here_y, upwind(v_before, c_edge, c[:, :LANE]))
                out_ref[t, k, rows, :] = (c - (here_x - past_x)) - (here_y - past_y)
        tracers_out(k).start()
        return 0

    lax.fori_loop(0, LEVELS, level, 0)
    for k in range(LEVELS):
        tracers_out(k).wait()


def advect(tracers, velocity, ocean, row_even, row_odd, col_even, col_odd):
    block = pltpu.VMEM((ROWS, COLS), jnp.float32)
    return pl.pallas_call(
        advect_kernel,
        in_specs=[HBM] * 3 + [ANY] * 4,
        out_specs=HBM,
        out_shape=f32(TRACERS, LEVELS, ROWS, COLS),
        scratch_shapes=[
            pltpu.VMEM((TRACERS, LEVELS, ROWS, COLS), jnp.float32),
            pltpu.VMEM((2, LEVELS, ROWS, COLS), jnp.float32),
            pltpu.VMEM((TRACERS, LEVELS, ROWS, COLS), jnp.float32),
            pltpu.VMEM((ROWS, COLS), jnp.int32),
            pltpu.VMEM((2, MESSAGE, COLS), jnp.float32),
            pltpu.VMEM((2, ROWS, LANE), jnp.float32),
            block,
            block,
            pltpu.VMEM((ROWS, LANE), jnp.float32),
            pltpu.VMEM((TRACERS + 1, LEVELS, ROWS, LANE), jnp.float32),
            pltpu.SemaphoreType.DMA((3, LEVELS)),
            pltpu.SemaphoreType.DMA((5,)),
        ],
        compiler_params=pltpu.CompilerParams(vmem_limit_bytes=52 * 2**20),
        cost_estimate=pl.CostEstimate(flops=40_000_000, bytes_accessed=15_800_000, transcendentals=0),
        name="advect",
    )(tracers, velocity, ocean, row_even, row_odd, col_even, col_odd)


NEAR = ((1, 0, 0.5), (-1, 0, 0.5), (0, 1, 0.5), (0, -1, 0.5), (1, 1, 0.125), (1, -1, 0.125), (-1, 1, 0.125), (-1, -1, 0.125))


def moved(x, rows, cols):
    if cols:
        lane = lanes(x.shape)
        x = pltpu.roll(x, (-cols) % x.shape[1], 1)
        x = jnp.where(lane == (x.shape[1] - 1 if cols > 0 else 0), 0.0, x)
    if rows:
        x = pltpu.roll(x, (-rows) % x.shape[0], 0)
    return x


def solve_kernel(got_ref, out_ref, h_ref, f_ref, weight):
    for j in range(8):
        cols = pl.ds(j * COLS, COLS)
        f_ref[1:23, cols] = got_ref[j, 0:22, :]
        h_ref[1:23, cols] = got_ref[j, 22:44, :]
    for ref in (f_ref, h_ref):
        for row in (0, EXT - 1):
            ref[row : row + 1, :] = jnp.zeros((1, WIDE), jnp.float32)
    lane = lanes((12, LANE))
    for j in range(7):
        for half in range(2):
            rows, part = slice(12 * half, 12 * half + 12), slice(LANE * half, LANE * half + LANE)
            pairs = got_ref[j, 44:56, part] * pltpu.roll(got_ref[j + 1, 44:56, part], 64, 1)
            flux = jnp.sum(jnp.where(lane < 32, pairs, 0.0), axis=1, keepdims=True)
            last = pl.ds((j + 1) * COLS - LANE, LANE)
            after = pl.ds((j + 1) * COLS, LANE)
            f_ref[rows, last] = f_ref[rows, last] - jnp.where(lane == LANE - 1, flux, 0.0)
            f_ref[rows, after] = f_ref[rows, after] + jnp.where(lane == 0, flux, 0.0)
    most = got_ref[0, 44:45, MOST : MOST + 1]
    for j in range(1, 8):
        most = jnp.maximum(most, got_ref[j, 44:45, MOST : MOST + 1])
    lam_max = 0.5 + 10.0 * most
    theta = (lam_max + 0.5) / 2.0
    delta = (lam_max - 0.5) / 2.0
    sigma = theta / delta
    rho = 1.0 / sigma
    h = h_ref[...]
    sides = {c: moved(h, 0, c) for c in (-1, 0, 1)}
    for n, (a, b, w) in enumerate(NEAR):
        weight[n] = w * (h + moved(sides[b], a, 0))
    inside = h > 0.0
    resid = f_ref[...]
    direction = resid / theta
    answer = jnp.zeros_like(resid)
    for _ in range(ITERS):
        sides = {c: moved(direction, 0, c) for c in (-1, 0, 1)}
        applied = 0.5 * direction
        for n, (a, b, w) in enumerate(NEAR):
            applied = applied + weight[n] * (direction - moved(sides[b], a, 0))
        resid = jnp.where(inside, resid - applied, 0.0)
        answer = answer + direction
        rho_next = 1.0 / (2.0 * sigma - rho)
        direction = rho_next * rho * direction + (2.0 * rho_next / delta) * resid
        rho = rho_next
    out_ref[...] = (answer + direction)[4:20, :]


def solve(got):
    return pl.pallas_call(
        solve_kernel,
        in_specs=[VMEM],
        out_specs=VMEM,
        out_shape=f32(16, WIDE),
        scratch_shapes=[
            pltpu.VMEM((EXT, WIDE), jnp.float32),
            pltpu.VMEM((EXT, WIDE), jnp.float32),
            pltpu.VMEM((8, EXT, WIDE), jnp.float32),
        ],
        compiler_params=pltpu.CompilerParams(vmem_limit_bytes=12 * 2**20),
        cost_estimate=pl.CostEstimate(flops=6_000_000, bytes_accessed=600_000, transcendentals=0),
        name="chebyshev",
    )(got)


def exchange(x, axis, odd):
    count = lax.axis_size(axis)
    pairs = []
    for i in range(odd, count - 1, 2):
        pairs += [(i, i + 1), (i + 1, i)]
    return lax.ppermute(x, axis, pairs)


def shards(tracers, velocity, ocean, thickness, depth):
    row_even, row_odd, col_even, col_odd, top, part, terms = pack(thickness, tracers, velocity, ocean, depth)
    from_even, from_odd = exchange(row_even, "bx", 0), exchange(row_odd, "bx", 1)
    tops = lax.all_to_all(top, "bx", split_axis=0, concat_axis=0, tiled=True)
    halos = (from_even, from_odd, exchange(col_even, "by", 0), exchange(col_odd, "by", 1))
    parcels = parcel(from_even, from_odd, row_even, row_odd, part, terms, ocean, depth, tops)
    got = lax.all_to_all(parcels, "by", split_axis=0, concat_axis=0, tiled=True)
    return advect(tracers, velocity, ocean, *halos), solve(got)


def solution(mesh):
    return jax.shard_map(
        shards,
        mesh=mesh,
        in_specs=(
            P(None, None, "bx", "by"),
            P(None, None, "bx", "by"),
            P("bx", "by"),
            P(),
            P("bx", "by"),
        ),
        out_specs=(P(None, None, "bx", "by"), P(("bx", "by"), None)),
        check_vma=False,
    )
```

```python
import functools

import jax
import jax.numpy as jnp
from jax import lax
from jax.experimental import pallas as pl
from jax.experimental.pallas import tpu as pltpu
from jax.sharding import PartitionSpec as P

ITERS = 3
TRACERS = 4
LEVELS = 12
ROWS = 128
COLS = 256
TILES = ROWS // 8
LANE = 128
WIDE = 8 * COLS
EXT = 24
CHUNK = 32
TALL = 16

SPEED, WET, PART, COEF, EDGE, MIXED, MESSAGE = 48, 60, 64, 68, 72, 80, 96
MOST = 100
ANY = pl.BlockSpec(memory_space=pl.ANY)
HBM = pl.BlockSpec(memory_space=pltpu.HBM)
VMEM = pl.BlockSpec(memory_space=pltpu.VMEM)


def f32(*shape):
    return jax.ShapeDtypeStruct(shape, jnp.float32)


def lanes(shape):
    return lax.broadcasted_iota(jnp.int32, shape, len(shape) - 1)


def sublanes(shape):
    return lax.broadcasted_iota(jnp.int32, shape, len(shape) - 2)


def coefficient(depth, wet):
    return depth * (0.1 + 0.9 * wet)


def positive(x):
    return jnp.maximum(x, 0.0)


def negative(x):
    return jnp.minimum(x, 0.0)


def upwind(speed, here, ahead):
    return speed * jnp.where(speed > 0.0, here, ahead)


def edge_terms(hi, lo, wet, thick_lanes):
    lane = lanes(hi.shape)
    used = (lane % 2 == 0) & (lane < 2 * LEVELS)
    last = jnp.broadcast_to(wet[:, COLS - 1 :], hi.shape)
    first = jnp.broadcast_to(wet[:, 0:1], hi.shape)
    speed = jnp.where(used, pltpu.roll(hi, LANE - 2 * SPEED, 1), 0.0)
    q_last = thick_lanes * (0.2 * hi - 0.8 * pltpu.roll(hi, LANE - 2 * LEVELS, 1))
    share = jnp.sum(jnp.where(speed > 0.0, speed * q_last, 0.0), axis=1, keepdims=True)
    terms = jnp.where(lane == 2 * LEVELS, share, jnp.minimum(speed, 0.0)) * last
    turned = pltpu.roll(lo, 65, 1)
    q_first = pltpu.roll(thick_lanes, 64, 1) * (0.2 * turned - 0.8 * pltpu.roll(turned, LANE - 2 * LEVELS, 1))
    used = (lane % 2 == 0) & (lane >= 64) & (lane < 64 + 2 * LEVELS)
    return terms + jnp.where(used, q_first, jnp.where(lane == 64 + 2 * LEVELS, 1.0, 0.0)) * first


def pack_kernel(thick_hbm, t_hbm, v_hbm, ocean_hbm, depth_hbm, row_even, row_odd, col_even, col_odd, top, part, terms,
                t_ref, v_ref, ocean_ref, depth_ref, thick, row_both, col_both, total, flux_x, flux_y, sems):
    odd_x, odd_y = lax.axis_index("bx") % 2, lax.axis_index("by") % 2
    row_hi, row_lo = row_both.at[0], row_both.at[1]
    col_hi, col_lo = col_both.at[0], col_both.at[1]
    chunks = ROWS // CHUNK

    def chunk_copies(c):
        rows = pl.ds(pl.multiple_of(c * CHUNK, CHUNK), CHUNK)
        return (
            pltpu.make_async_copy(t_hbm.at[:, :, rows, :], t_ref.at[:, :, rows, :], sems.at[0, c]),
            pltpu.make_async_copy(v_hbm.at[:, :, rows, :], v_ref.at[:, :, rows, :], sems.at[1, c]),
        )

    small = [
        pltpu.make_async_copy(ocean_hbm, ocean_ref, sems.at[2, 0]),
        pltpu.make_async_copy(depth_hbm, depth_ref, sems.at[2, 1]),
        pltpu.make_async_copy(thick_hbm, thick, sems.at[2, 2]),
    ]
    for copy in small:
        copy.start()
    for c in range(chunks):
        for copy in chunk_copies(c):
            copy.start()
    for copy in small:
        copy.wait()
    wet = ocean_ref[...].astype(jnp.float32)
    coef = coefficient(depth_ref[...], wet)
    most = jnp.max(jnp.max(coef, axis=0, keepdims=True), axis=1, keepdims=True)
    top[...] = jnp.broadcast_to(most[None], top.shape)
    thick_lanes = jnp.zeros((1, LANE), jnp.float32)
    for k in range(LEVELS):
        thick_lanes = jnp.where(lanes((1, LANE)) == 2 * k, thick[k], thick_lanes)

    def gather(c, _):
        for copy in chunk_copies(c):
            copy.wait()
        lane = lanes((CHUNK, LANE))
        rows = pl.ds(pl.multiple_of(c * CHUNK, CHUNK), CHUNK)
        before = pl.ds(jnp.maximum(c * CHUNK - 1, 0), 1)
        start = pl.ds(pl.multiple_of(c * CHUNK, CHUNK), 1)
        ocean = ocean_ref[rows, :].astype(jnp.float32)
        hi = jnp.where(lane == 2 * WET, pltpu.roll(ocean[:, LANE:], (2 * WET + 1) % LANE, 1), 0.0)
        lo = jnp.where(lane == 2 * WET - 1, pltpu.roll(ocean[:, :LANE], 2 * WET - 1, 1), 0.0)
        for k in range(LEVELS):
            for t in range(TRACERS):
                s = t * LEVELS + k
                hi = jnp.where(lane == 2 * s, pltpu.roll(t_ref[t, k, rows, LANE:], 2 * s + 1, 1), hi)
                place = (2 * s - 1) % LANE
                lo = jnp.where(lane == place, pltpu.roll(t_ref[t, k, rows, :LANE], place, 1), lo)
            s = SPEED + k
            hi = jnp.where(lane == 2 * s, pltpu.roll(v_ref[1, k, rows, LANE:], 2 * s + 1, 1), hi)
        col_hi[rows, :] = hi
        col_lo[rows, :] = lo
        terms[rows, :] = edge_terms(hi, lo, ocean, thick_lanes)
        whole = jnp.zeros((CHUNK, COLS), jnp.float32)
        out_x = jnp.zeros((CHUNK, COLS), jnp.float32)
        out_y = jnp.zeros((CHUNK, COLS), jnp.float32)
        between = jnp.zeros((1, COLS), jnp.float32)
        for k in range(LEVELS):
            warm, salt = 0.2 * thick[k], 0.8 * thick[k]
            q = warm * t_ref[0, k, rows, :] - salt * t_ref[1, k, rows, :]
            whole = whole + q
            out_x = out_x + upwind(v_ref[0, k, rows, :], q, pltpu.roll(q, CHUNK - 1, 0))
            out_y = out_y + upwind(v_ref[1, k, rows, :], q, pltpu.roll(q, COLS - 1, 1))
            mixed = lambda at: warm * t_ref[0, k, at, :] - salt * t_ref[1, k, at, :]
            between = between + upwind(v_ref[0, k, before, :], mixed(before), mixed(start))
        total[rows, :] = whole
        flux_y[rows, :] = out_y
        flux_x[before, :] = between
        flux_x[rows, :] = out_x
        return 0

    lax.fori_loop(0, chunks, gather, 0)
    load_wet = lambda at: ocean_ref[at : at + 8, :].astype(jnp.float32)
    row, col = sublanes((8, COLS)), lanes((8, COLS))
    turned = jnp.zeros((8, COLS), jnp.float32)
    for r in range(TILES):
        rows = pl.ds(8 * r, 8)
        here = load_wet(8 * r)
        out_x = flux_x[rows, :] * here
        if r < TILES - 1:
            out_x = out_x * load_wet(8 * r + 1)
        else:
            out_x = jnp.where(row == 7, 0.0, out_x * pltpu.roll(here, 7, 0))
        out_y = jnp.where(col == COLS - 1, 0.0, flux_y[rows, :] * (here * pltpu.roll(here, COLS - 1, 1)))
        past = turned
        turned = pltpu.roll(out_x, 1, 0)
        past_x = jnp.where(row == 0, past, turned)
        part[rows, :] = here * (total[rows, :] - (out_x - past_x) - (out_y - pltpu.roll(out_y, 1, 1)))
    for t in range(TRACERS):
        for k in range(LEVELS):
            s = t * LEVELS + k
            row_hi[s : s + 1, :] = t_ref[t, k, ROWS - 1 : ROWS, :]
            row_lo[s : s + 1, :] = t_ref[t, k, 0:1, :]
    row_lo[SPEED:WET, :] = jnp.zeros((WET - SPEED, COLS), jnp.float32)
    for k in range(LEVELS):
        row_hi[SPEED + k : SPEED + k + 1, :] = v_ref[0, k, ROWS - 1 : ROWS, :]
        for message, at in ((row_hi, ROWS - 1), (row_lo, 0)):
            line = slice(at, at + 1)
            message[MIXED + k : MIXED + k + 1, :] = (0.2 * thick[k]) * t_ref[0, k, line, :] - (0.8 * thick[k]) * t_ref[1, k, line, :]
    for message, rows, edge in ((row_hi, slice(ROWS - 4, ROWS), ROWS - 1), (row_lo, slice(0, 4), 0)):
        tile = slice(rows.start // 8 * 8, rows.start // 8 * 8 + 8)
        here = load_wet(tile.start)
        keep = slice(rows.start - tile.start, rows.stop - tile.start)
        message[WET:PART, :] = jnp.broadcast_to(here[edge - tile.start : edge - tile.start + 1, :], (PART - WET, COLS))
        message[PART:COEF, :] = part[tile, :][keep, :]
        message[COEF:EDGE, :] = coefficient(depth_ref[tile, :], here)[keep, :]
        message[EDGE:MIXED, :LANE] = terms[tile, :]
        message[EDGE:MIXED, LANE:] = jnp.zeros((8, LANE), jnp.float32)
        message[MIXED + LEVELS :, :] = jnp.zeros((MESSAGE - MIXED - LEVELS, COLS), jnp.float32)
    row_even[...] = row_both[odd_x]
    row_odd[...] = row_both[1 - odd_x]
    col_even[...] = col_both[odd_y]
    col_odd[...] = col_both[1 - odd_y]


def pack(thickness, tracers, velocity, ocean, depth):
    block = pltpu.VMEM((ROWS, COLS), jnp.float32)
    return pl.pallas_call(
        pack_kernel,
        in_specs=[HBM] * 5,
        out_specs=[VMEM] * 7,
        out_shape=[f32(MESSAGE, COLS)] * 2 + [f32(ROWS, LANE)] * 2 + [f32(16, 8, LANE), f32(ROWS, COLS), f32(ROWS, LANE)],
        scratch_shapes=[
            pltpu.VMEM((TRACERS, LEVELS, ROWS, COLS), jnp.float32),
            pltpu.VMEM((2, LEVELS, ROWS, COLS), jnp.float32),
            pltpu.VMEM((ROWS, COLS), jnp.int32),
            block,
            pltpu.SMEM((LEVELS,), jnp.float32),
            pltpu.VMEM((2, MESSAGE, COLS), jnp.float32),
            pltpu.VMEM((2, ROWS, LANE), jnp.float32),
            block,
            block,
            block,
            pltpu.SemaphoreType.DMA((3, 4)),
        ],
        compiler_params=pltpu.CompilerParams(vmem_limit_bytes=60 * 2**20),
        cost_estimate=pl.CostEstimate(flops=20_000_000, bytes_accessed=9_400_000, transcendentals=0),
        name="pack_edges",
    )(thickness, tracers, velocity, ocean, depth)


def parcel_kernel(even_hbm, odd_hbm, own_even_hbm, own_odd_hbm, part_hbm, terms_hbm, ocean_hbm, depth_hbm, tops_hbm, _, __, send_ref,
                  rows_in, rows_out, part, terms, ocean_ref, depth_ref, tops, ext, ext_terms, sems):
    odd_x = lax.axis_index("bx") % 2
    copies = [
        (even_hbm, rows_in.at[1 - odd_x]),
        (odd_hbm, rows_in.at[odd_x]),
        (own_even_hbm, rows_out.at[1 - odd_x]),
        (own_odd_hbm, rows_out.at[odd_x]),
        (part_hbm, part),
        (terms_hbm, terms),
        (ocean_hbm, ocean_ref),
        (depth_hbm, depth_ref),
        (tops_hbm, tops),
    ]
    copies = [pltpu.make_async_copy(a, b, sems.at[i]) for i, (a, b) in enumerate(copies)]
    for copy in copies:
        copy.start()
    for copy in copies:
        copy.wait()
    before, after, first, last = rows_in.at[0], rows_in.at[1], rows_out.at[0], rows_out.at[1]
    speed, mixed, wet = slice(SPEED, WET), slice(MIXED, MIXED + LEVELS), slice(WET, WET + 1)
    flux_lo = jnp.sum(upwind(before[speed, :], before[mixed, :], first[mixed, :]), axis=0, keepdims=True)
    flux_hi = jnp.sum(upwind(last[speed, :], last[mixed, :], after[mixed, :]), axis=0, keepdims=True)
    flux_lo = flux_lo * (before[wet, :] * first[wet, :])
    flux_hi = flux_hi * (last[wet, :] * after[wet, :])
    row = sublanes((4, COLS))
    ext[0, 0:4, :] = before[PART:COEF, :] - jnp.where(row == 3, flux_lo, 0.0)
    ext[0, ROWS + 4 :, :] = after[PART:COEF, :] + jnp.where(row == 0, flux_hi, 0.0)
    ext[1, 0:4, :] = before[COEF:EDGE, :]
    ext[1, ROWS + 4 :, :] = after[COEF:EDGE, :]
    ext_terms[0:4, :] = before[EDGE + 4 : MIXED, :LANE]
    ext_terms[ROWS + 4 :, :] = after[EDGE : EDGE + 4, :LANE]
    row = sublanes((8, COLS))
    for r in range(TILES):
        rows = slice(8 * r, 8 * r + 8)
        value = part[rows, :]
        if r == 0:
            value = value + jnp.where(row == 0, flux_lo, 0.0)
        if r == TILES - 1:
            value = value - jnp.where(row == 7, flux_hi, 0.0)
        ext[0, 8 * r + 4 : 8 * r + 12, :] = value
        ext[1, 8 * r + 4 : 8 * r + 12, :] = coefficient(depth_ref[rows, :], ocean_ref[rows, :].astype(jnp.float32))
        ext_terms[8 * r + 4 : 8 * r + 12, :] = terms[rows, :]
    most = jnp.max(tops[...], axis=0)[0:1, :]
    for j in range(8):
        at = 16 * j
        send_ref[j, 0:22, :] = ext[0, at + 1 : at + 23, :]
        send_ref[j, 22:44, :] = ext[1, at + 1 : at + 23, :]
        for half in range(2):
            value = ext_terms[at + 12 * half : at + 12 * half + 12, :]
            send_ref[j, 44:56, half * LANE : (half + 1) * LANE] = jnp.where(lanes((12, LANE)) == MOST, most, value)


def parcel(even, odd, own_even, own_odd, part, terms, ocean, depth, tops, col_even, col_odd):
    block = pltpu.VMEM((ROWS, COLS), jnp.float32)
    return pl.pallas_call(
        parcel_kernel,
        in_specs=[ANY] * 11,
        out_specs=VMEM,
        out_shape=f32(8, 56, COLS),
        scratch_shapes=[
            pltpu.VMEM((2, MESSAGE, COLS), jnp.float32),
            pltpu.VMEM((2, MESSAGE, COLS), jnp.float32),
            block,
            pltpu.VMEM((ROWS, LANE), jnp.float32),
            pltpu.VMEM((ROWS, COLS), jnp.int32),
            block,
            pltpu.VMEM((16, 8, LANE), jnp.float32),
            pltpu.VMEM((2, ROWS + 8, COLS), jnp.float32),
            pltpu.VMEM((ROWS + 8, LANE), jnp.float32),
            pltpu.SemaphoreType.DMA((9,)),
        ],
        compiler_params=pltpu.CompilerParams(vmem_limit_bytes=60 * 2**20),
        cost_estimate=pl.CostEstimate(flops=1_000_000, bytes_accessed=1_500_000, transcendentals=0),
        name="parcels",
    )(even, odd, own_even, own_odd, part, terms, ocean, depth, tops, col_even, col_odd)


def ahead_y(x, edge):
    last = lanes((x.shape[0], LANE)) == LANE - 1
    a, b = pltpu.roll(x[:, :LANE], LANE - 1, 1), pltpu.roll(x[:, LANE:], LANE - 1, 1)
    return jnp.concatenate([jnp.where(last, b, a), jnp.where(last, edge, b)], 1)


def behind_y(x, edge):
    first = lanes((x.shape[0], LANE)) == 0
    a, b = pltpu.roll(x[:, :LANE], 1, 1), pltpu.roll(x[:, LANE:], 1, 1)
    return jnp.concatenate([jnp.where(first, edge, a), jnp.where(first, a, b)], 1)


def above(load, edge, r, tall=8):
    if (r + 1) * tall < ROWS:
        return load(tall * r + 1)
    return jnp.where(sublanes((tall, COLS)) == tall - 1, edge, pltpu.roll(load(tall * r), tall - 1, 0))


def advect_kernel(t_hbm, v_hbm, ocean_hbm, row_even, row_odd, col_even, col_odd, out_hbm,
                  t_ref, v_ref, out_ref, ocean_ref, rows_in, cols_in, w_x, w_y, before_y, edges, sems, small_sems):
    odd_x, odd_y = lax.axis_index("bx") % 2, lax.axis_index("by") % 2
    row_lo, row_hi = rows_in.at[0], rows_in.at[1]
    small = [
        (ocean_hbm, ocean_ref),
        (row_even, rows_in.at[1 - odd_x]),
        (row_odd, rows_in.at[odd_x]),
        (col_even, cols_in.at[1 - odd_y]),
        (col_odd, cols_in.at[odd_y]),
    ]
    small = [pltpu.make_async_copy(a, b, small_sems.at[i]) for i, (a, b) in enumerate(small)]

    def tracers_in(k):
        return pltpu.make_async_copy(t_hbm.at[:, k], t_ref.at[k], sems.at[0, k])

    def velocity_in(k):
        return pltpu.make_async_copy(v_hbm.at[:, k], v_ref.at[k], sems.at[1, k])

    def tracers_out(k):
        return pltpu.make_async_copy(out_ref.at[k], out_hbm.at[:, k], sems.at[2, k])

    for copy in small:
        copy.start()
    for k in range(LEVELS):
        tracers_in(k).start()
        velocity_in(k).start()
    for copy in small:
        copy.wait()
    even = lanes((8, LANE)) % 2 == 0
    load_wet = lambda at: ocean_ref[at : at + 8, :].astype(jnp.float32)
    for r in range(TILES):
        rows = pl.ds(8 * r, 8)
        edge = jnp.where(even, cols_in[0, rows, :], cols_in[1, rows, :])
        for k in range(LEVELS):
            for i in range(TRACERS + 1):
                edges[k, i, rows, :] = pltpu.roll(edge, (LANE - 2 * (i * LEVELS + k)) % LANE, 1)
        here = load_wet(8 * r)
        wet_edge = pltpu.roll(edge, LANE - 2 * WET, 1)
        w_x[rows, :] = here * above(load_wet, row_hi[WET : WET + 1, :], r)
        w_y[rows, :] = here * ahead_y(here, wet_edge)
        before_y[rows, :] = here[:, :LANE] * wet_edge
    w_before = load_wet(0)[0:1, :] * row_lo[WET : WET + 1, :]

    def level(k, _):
        tracers_in(k).wait()
        velocity_in(k).wait()
        u_before = row_lo[pl.ds(SPEED + k, 1), :] * w_before

        def pair(p, _):
            tracers = [2 * p, 2 * p + 1]
            carry = [upwind(u_before, row_lo[pl.ds(t * LEVELS + k, 1), :], t_ref[k, t, 0:1, :]) for t in tracers]
            for r in range(ROWS // TALL):
                rows = pl.ds(TALL * r, TALL)
                u = v_ref[k, 0, rows, :] * w_x[rows, :]
                v = v_ref[k, 1, rows, :] * w_y[rows, :]
                v_before = edges[k, TRACERS, rows, :] * before_y[rows, :]
                for i, t in enumerate(tracers):
                    load = lambda at: t_ref[k, t, at : at + TALL, :]
                    c = load(TALL * r)
                    c_edge = edges[k, t, rows, :]
                    here_x = upwind(u, c, above(load, row_hi[pl.ds(t * LEVELS + k, 1), :], r, TALL))
                    turned = pltpu.roll(here_x, 1, 0)
                    past_x = jnp.where(sublanes((TALL, COLS)) == 0, carry[i], turned)
                    carry[i] = turned[0:1, :]
                    here_y = upwind(v, c, ahead_y(c, c_edge))
                    past_y = behind_y(here_y, upwind(v_before, c_edge, c[:, :LANE]))
                    out_ref[k, t, rows, :] = (c - (here_x - past_x)) - (here_y - past_y)
            return 0

        lax.fori_loop(0, 2, pair, 0)
        tracers_out(k).start()
        return 0

    lax.fori_loop(0, LEVELS, level, 0)
    for k in range(LEVELS):
        tracers_out(k).wait()


def advect(tracers, velocity, ocean, row_even, row_odd, col_even, col_odd):
    block = pltpu.VMEM((ROWS, COLS), jnp.float32)
    return pl.pallas_call(
        advect_kernel,
        in_specs=[HBM] * 3 + [ANY] * 4,
        out_specs=HBM,
        out_shape=f32(TRACERS, LEVELS, ROWS, COLS),
        scratch_shapes=[
            pltpu.VMEM((LEVELS, TRACERS, ROWS, COLS), jnp.float32),
            pltpu.VMEM((LEVELS, 2, ROWS, COLS), jnp.float32),
            pltpu.VMEM((LEVELS, TRACERS, ROWS, COLS), jnp.float32),
            pltpu.VMEM((ROWS, COLS), jnp.int32),
            pltpu.VMEM((2, MESSAGE, COLS), jnp.float32),
            pltpu.VMEM((2, ROWS, LANE), jnp.float32),
            block,
            block,
            pltpu.VMEM((ROWS, LANE), jnp.float32),
            pltpu.VMEM((LEVELS, TRACERS + 1, ROWS, LANE), jnp.float32),
            pltpu.SemaphoreType.DMA((3, LEVELS)),
            pltpu.SemaphoreType.DMA((5,)),
        ],
        compiler_params=pltpu.CompilerParams(vmem_limit_bytes=60 * 2**20),
        cost_estimate=pl.CostEstimate(flops=40_000_000, bytes_accessed=15_800_000, transcendentals=0),
        name="advect",
    )(tracers, velocity, ocean, row_even, row_odd, col_even, col_odd)


NEAR = ((1, 0, 0.5), (-1, 0, 0.5), (0, 1, 0.5), (0, -1, 0.5), (1, 1, 0.125), (1, -1, 0.125), (-1, 1, 0.125), (-1, -1, 0.125))


def moved(x, rows, cols):
    if cols:
        lane = lanes(x.shape)
        x = pltpu.roll(x, (-cols) % x.shape[1], 1)
        x = jnp.where(lane == (x.shape[1] - 1 if cols > 0 else 0), 0.0, x)
    if rows:
        x = pltpu.roll(x, (-rows) % x.shape[0], 0)
    return x


def solve_kernel(got_ref, out_ref, h_ref, f_ref, weight):
    for j in range(8):
        cols = pl.ds(j * COLS, COLS)
        f_ref[1:23, cols] = got_ref[j, 0:22, :]
        h_ref[1:23, cols] = got_ref[j, 22:44, :]
    for ref in (f_ref, h_ref):
        for row in (0, EXT - 1):
            ref[row : row + 1, :] = jnp.zeros((1, WIDE), jnp.float32)
    lane = lanes((12, LANE))
    for j in range(7):
        for half in range(2):
            rows, part = slice(12 * half, 12 * half + 12), slice(LANE * half, LANE * half + LANE)
            pairs = got_ref[j, 44:56, part] * pltpu.roll(got_ref[j + 1, 44:56, part], 64, 1)
            flux = jnp.sum(jnp.where(lane < 32, pairs, 0.0), axis=1, keepdims=True)
            last = pl.ds((j + 1) * COLS - LANE, LANE)
            after = pl.ds((j + 1) * COLS, LANE)
            f_ref[rows, last] = f_ref[rows, last] - jnp.where(lane == LANE - 1, flux, 0.0)
            f_ref[rows, after] = f_ref[rows, after] + jnp.where(lane == 0, flux, 0.0)
    most = got_ref[0, 44:45, MOST : MOST + 1]
    for j in range(1, 8):
        most = jnp.maximum(most, got_ref[j, 44:45, MOST : MOST + 1])
    lam_max = 0.5 + 10.0 * most
    theta = (lam_max + 0.5) / 2.0
    delta = (lam_max - 0.5) / 2.0
    sigma = theta / delta
    rho = 1.0 / sigma
    h = h_ref[...]
    sides = {c: moved(h, 0, c) for c in (-1, 0, 1)}
    for n, (a, b, w) in enumerate(NEAR):
        weight[n] = w * (h + moved(sides[b], a, 0))
    inside = h > 0.0
    resid = f_ref[...]
    direction = resid / theta
    answer = jnp.zeros_like(resid)
    for _ in range(ITERS):
        sides = {c: moved(direction, 0, c) for c in (-1, 0, 1)}
        applied = 0.5 * direction
        for n, (a, b, w) in enumerate(NEAR):
            applied = applied + weight[n] * (direction - moved(sides[b], a, 0))
        resid = jnp.where(inside, resid - applied, 0.0)
        answer = answer + direction
        rho_next = 1.0 / (2.0 * sigma - rho)
        direction = rho_next * rho * direction + (2.0 * rho_next / delta) * resid
        rho = rho_next
    out_ref[...] = (answer + direction)[4:20, :]


def solve(got):
    return pl.pallas_call(
        solve_kernel,
        in_specs=[VMEM],
        out_specs=VMEM,
        out_shape=f32(16, WIDE),
        scratch_shapes=[
            pltpu.VMEM((EXT, WIDE), jnp.float32),
            pltpu.VMEM((EXT, WIDE), jnp.float32),
            pltpu.VMEM((8, EXT, WIDE), jnp.float32),
        ],
        compiler_params=pltpu.CompilerParams(vmem_limit_bytes=60 * 2**20),
        cost_estimate=pl.CostEstimate(flops=6_000_000, bytes_accessed=600_000, transcendentals=0),
        name="chebyshev",
    )(got)


def exchange(x, axis, odd):
    count = lax.axis_size(axis)
    pairs = []
    for i in range(odd, count - 1, 2):
        pairs += [(i, i + 1), (i + 1, i)]
    return lax.ppermute(x, axis, pairs)


def shards(tracers, velocity, ocean, thickness, depth):
    row_even, row_odd, col_even, col_odd, top, part, terms = pack(thickness, tracers, velocity, ocean, depth)
    from_even, from_odd = exchange(row_even, "bx", 0), exchange(row_odd, "bx", 1)
    tops = lax.all_to_all(top, "bx", split_axis=0, concat_axis=0, tiled=True)
    halos = (from_even, from_odd, exchange(col_even, "by", 0), exchange(col_odd, "by", 1))
    parcels = parcel(from_even, from_odd, row_even, row_odd, part, terms, ocean, depth, tops, *halos[2:])
    got = lax.all_to_all(parcels, "by", split_axis=0, concat_axis=0, tiled=True)
    return advect(tracers, velocity, ocean, *halos), solve(got)


def solution(mesh):
    return jax.shard_map(
        shards,
        mesh=mesh,
        in_specs=(
            P(None, None, "bx", "by"),
            P(None, None, "bx", "by"),
            P("bx", "by"),
            P(),
            P("bx", "by"),
        ),
        out_specs=(P(None, None, "bx", "by"), P(("bx", "by"), None)),
        check_vma=False,
    )
```

```python
import functools

import jax
import jax.numpy as jnp
from jax import lax
from jax.experimental import pallas as pl
from jax.experimental.pallas import tpu as pltpu
from jax.sharding import PartitionSpec as P

ITERS = 3
TRACERS = 4
LEVELS = 12
ROWS = 128
COLS = 256
TILES = ROWS // 8
LANE = 128
WIDE = 8 * COLS
EXT = 24
CHUNK = 32
TALL = 16
LIMA, LIMB = 48, 48

SPEED, WET, THICK, PART, COEF, EDGE, MESSAGE = 48, 60, 61, 64, 68, 72, 80
ANY = pl.BlockSpec(memory_space=pl.ANY)
HBM = pl.BlockSpec(memory_space=pltpu.HBM)
VMEM = pl.BlockSpec(memory_space=pltpu.VMEM)


def f32(*shape):
    return jax.ShapeDtypeStruct(shape, jnp.float32)


def lanes(shape):
    return lax.broadcasted_iota(jnp.int32, shape, len(shape) - 1)


def sublanes(shape):
    return lax.broadcasted_iota(jnp.int32, shape, len(shape) - 2)


def coefficient(depth, wet):
    return depth * (0.1 + 0.9 * wet)


def positive(x):
    return jnp.maximum(x, 0.0)


def negative(x):
    return jnp.minimum(x, 0.0)


def edge_forcing(q, u, v, wet, thick):
    shape = (8, COLS)
    row, col = sublanes(shape), lanes(shape)
    total = jnp.zeros(shape, jnp.float32)
    flux_x = jnp.zeros(shape, jnp.float32)
    flux_y = jnp.zeros(shape, jnp.float32)
    for k in range(LEVELS):
        depth = thick[k]
        total = total + depth * q[k]
        flux_x = flux_x + depth * (positive(u[k]) * q[k] + negative(u[k]) * pltpu.roll(q[k], 7, 0))
        flux_y = flux_y + depth * (positive(v[k]) * q[k] + negative(v[k]) * pltpu.roll(q[k], COLS - 1, 1))
    flux_x = flux_x * jnp.where(row == 7, 0.0, wet * pltpu.roll(wet, 7, 0))
    flux_y = flux_y * jnp.where(col == COLS - 1, 0.0, wet * pltpu.roll(wet, COLS - 1, 1))
    return wet * (total - (flux_x - pltpu.roll(flux_x, 1, 0)) - (flux_y - pltpu.roll(flux_y, 1, 1)))


def edge_terms(q, v, wet, thick):
    lane = lanes((8, LANE))
    last, first = wet[:, LANE:], wet[:, :LANE]
    upwind = jnp.zeros((8, LANE), jnp.float32)
    terms = jnp.where(lane == 28, pltpu.roll(first, 28, 1), 0.0)
    for k in range(LEVELS):
        depth = thick[k]
        speed = v[k][:, LANE:]
        upwind = upwind + depth * positive(speed) * q[k][:, LANE:]
        terms = jnp.where(lane == k, pltpu.roll(depth * negative(speed) * last, k + 1, 1), terms)
        terms = jnp.where(lane == 16 + k, pltpu.roll(q[k][:, :LANE] * first, 16 + k, 1), terms)
    return jnp.where(lane == LEVELS, pltpu.roll(upwind * last, LEVELS + 1, 1), terms)


def pack_kernel(thick_hbm, t_hbm, v_hbm, ocean_hbm, depth_hbm, row_even, row_odd, col_even, col_odd, top,
                t_ref, u_top, u_low, v_top, v_low, v_last, ocean_ref, depth_ref, thick, row_both, col_both, sems):
    odd_x, odd_y = lax.axis_index("bx") % 2, lax.axis_index("by") % 2
    row_hi, row_lo = row_both.at[0], row_both.at[1]
    col_hi, col_lo = col_both.at[0], col_both.at[1]

    def chunk_copy(c):
        rows = pl.ds(pl.multiple_of(c * CHUNK, CHUNK), CHUNK)
        return pltpu.make_async_copy(t_hbm.at[:, :, rows, :], t_ref.at[:, :, rows, :], sems.at[c])

    chunks = ROWS // CHUNK
    small = [
        pltpu.make_async_copy(ocean_hbm, ocean_ref, sems.at[chunks]),
        pltpu.make_async_copy(depth_hbm, depth_ref, sems.at[chunks + 1]),
        pltpu.make_async_copy(v_hbm.at[1, :, :, LANE:], v_last, sems.at[chunks + 2]),
        pltpu.make_async_copy(thick_hbm, thick, sems.at[chunks + 7]),
    ]
    tiles = [
        pltpu.make_async_copy(v_hbm.at[0, :, 0:8, :], u_top, sems.at[chunks + 3]),
        pltpu.make_async_copy(v_hbm.at[0, :, ROWS - 8 :, :], u_low, sems.at[chunks + 4]),
        pltpu.make_async_copy(v_hbm.at[1, :, 0:8, :], v_top, sems.at[chunks + 5]),
        pltpu.make_async_copy(v_hbm.at[1, :, ROWS - 8 :, :], v_low, sems.at[chunks + 6]),
    ]
    for copy in small:
        copy.start()
    for c in range(chunks):
        chunk_copy(c).start()
    for copy in tiles:
        copy.start()
    for copy in small:
        copy.wait()
    wet = ocean_ref[...].astype(jnp.float32)
    coef = coefficient(depth_ref[...], wet)
    most = jnp.max(jnp.max(coef, axis=0, keepdims=True), axis=1, keepdims=True)
    top[...] = jnp.broadcast_to(most[None], top.shape)
    thick_lanes = jnp.zeros((1, COLS), jnp.float32)
    for k in range(LEVELS):
        thick_lanes = jnp.where(lanes((1, COLS)) == k, thick[k], thick_lanes)

    def gather(c, _):
        chunk_copy(c).wait()
        lane = lanes((CHUNK, LANE))
        rows = pl.ds(pl.multiple_of(c * CHUNK, CHUNK), CHUNK)
        ocean = ocean_ref[rows, :].astype(jnp.float32)
        hi = jnp.where(lane == 2 * WET, pltpu.roll(ocean[:, LANE:], (2 * WET + 1) % LANE, 1), 0.0)
        lo = jnp.where(lane == 2 * WET - 1, pltpu.roll(ocean[:, :LANE], 2 * WET - 1, 1), 0.0)
        for k in range(LEVELS):
            for t in range(TRACERS):
                s = t * LEVELS + k
                hi = jnp.where(lane == 2 * s, pltpu.roll(t_ref[t, k, rows, LANE:], 2 * s + 1, 1), hi)
                place = (2 * s - 1) % LANE
                lo = jnp.where(lane == place, pltpu.roll(t_ref[t, k, rows, :LANE], place, 1), lo)
            s = SPEED + k
            hi = jnp.where(lane == 2 * s, pltpu.roll(v_last[k, rows, :], 2 * s + 1, 1), hi)
        col_hi[rows, :] = hi
        col_lo[rows, :] = lo
        return 0

    lax.fori_loop(0, chunks, gather, 0)
    for copy in tiles:
        copy.wait()
    for t in range(TRACERS):
        for k in range(LEVELS):
            s = t * LEVELS + k
            row_hi[s : s + 1, :] = t_ref[t, k, ROWS - 1 : ROWS, :]
            row_lo[s : s + 1, :] = t_ref[t, k, 0:1, :]
    for k in range(LEVELS):
        row_hi[SPEED + k : SPEED + k + 1, :] = u_low[k, 7:8, :]
    row_lo[SPEED:WET, :] = jnp.zeros((WET - SPEED, COLS), jnp.float32)
    for row, message, u, v, keep in ((0, row_lo, u_top, v_top, 0), (ROWS - 8, row_hi, u_low, v_low, 4)):
        rows = slice(row, row + 8)
        here = ocean_ref[rows, :].astype(jnp.float32)
        q = [0.2 * t_ref[0, k, rows, :] - 0.8 * t_ref[1, k, rows, :] for k in range(LEVELS)]
        speed_x = [u[k] for k in range(LEVELS)]
        speed_y = [v[k] for k in range(LEVELS)]
        message[WET:THICK, :] = here[7:8, :] if keep else here[0:1, :]
        message[THICK:PART, :] = jnp.broadcast_to(thick_lanes, (PART - THICK, COLS))
        message[PART:COEF, :] = edge_forcing(q, speed_x, speed_y, here, thick)[keep : keep + 4, :]
        message[COEF:EDGE, :] = coefficient(depth_ref[rows, :], here)[keep : keep + 4, :]
        message[EDGE:MESSAGE, :LANE] = edge_terms(q, speed_y, here, thick)
        message[EDGE:MESSAGE, LANE:] = jnp.zeros((8, LANE), jnp.float32)
    row_even[...] = row_both[odd_x]
    row_odd[...] = row_both[1 - odd_x]
    col_even[...] = col_both[odd_y]
    col_odd[...] = col_both[1 - odd_y]


def pack(thickness, tracers, velocity, ocean, depth):
    tile = (LEVELS, 8, COLS)
    return pl.pallas_call(
        pack_kernel,
        in_specs=[HBM] * 5,
        out_specs=[VMEM] * 5,
        out_shape=[f32(MESSAGE, COLS), f32(MESSAGE, COLS), f32(ROWS, LANE), f32(ROWS, LANE), f32(16, 8, LANE)],
        scratch_shapes=[
            pltpu.VMEM((TRACERS, LEVELS, ROWS, COLS), jnp.float32),
            pltpu.VMEM(tile, jnp.float32),
            pltpu.VMEM(tile, jnp.float32),
            pltpu.VMEM(tile, jnp.float32),
            pltpu.VMEM(tile, jnp.float32),
            pltpu.VMEM((LEVELS, ROWS, LANE), jnp.float32),
            pltpu.VMEM((ROWS, COLS), jnp.int32),
            pltpu.VMEM((ROWS, COLS), jnp.float32),
            pltpu.SMEM((LEVELS,), jnp.float32),
            pltpu.VMEM((2, MESSAGE, COLS), jnp.float32),
            pltpu.VMEM((2, ROWS, LANE), jnp.float32),
            pltpu.SemaphoreType.DMA((ROWS // CHUNK + 8,)),
        ],
        compiler_params=pltpu.CompilerParams(vmem_limit_bytes=60 * 2**20),
        cost_estimate=pl.CostEstimate(flops=4_000_000, bytes_accessed=7_400_000, transcendentals=0),
        name="pack_edges",
    )(thickness, tracers, velocity, ocean, depth)


def ahead_y(x, edge):
    last = lanes((x.shape[0], LANE)) == LANE - 1
    a, b = pltpu.roll(x[:, :LANE], LANE - 1, 1), pltpu.roll(x[:, LANE:], LANE - 1, 1)
    return jnp.concatenate([jnp.where(last, b, a), jnp.where(last, edge, b)], 1)


def behind_y(x, edge):
    first = lanes((x.shape[0], LANE)) == 0
    a, b = pltpu.roll(x[:, :LANE], 1, 1), pltpu.roll(x[:, LANE:], 1, 1)
    return jnp.concatenate([jnp.where(first, edge, a), jnp.where(first, a, b)], 1)


def above(load, edge, r, tall=8):
    if (r + 1) * tall < ROWS:
        return load(tall * r + 1)
    return jnp.where(sublanes((tall, COLS)) == tall - 1, edge, pltpu.roll(load(tall * r), tall - 1, 0))


def upwind(speed, here, ahead):
    return speed * jnp.where(speed > 0.0, here, ahead)


def advect_kernel(first, *refs):
    if first == 0:
        (t_hbm, v_hbm, ocean_hbm, row_even, row_odd, col_even, col_odd, depth_hbm, out_hbm, send_ref,
         t_ref, v_ref, out_ref, ocean_ref, rows_in, cols_in, w_x, w_y, before_y, edges, sems, small_sems,
         depth_ref, total, flux, ext, thick) = refs
    else:
        (t_hbm, v_hbm, ocean_hbm, row_even, row_odd, col_even, col_odd, _, out_hbm,
         t_ref, v_ref, out_ref, ocean_ref, rows_in, cols_in, w_x, w_y, before_y, edges, sems, small_sems) = refs
    odd_x, odd_y = lax.axis_index("bx") % 2, lax.axis_index("by") % 2
    row_lo, row_hi = rows_in.at[0], rows_in.at[1]
    small = [
        (ocean_hbm, ocean_ref),
        (row_even, rows_in.at[1 - odd_x]),
        (row_odd, rows_in.at[odd_x]),
        (col_even, cols_in.at[1 - odd_y]),
        (col_odd, cols_in.at[odd_y]),
    ]
    if first == 0:
        small += [(depth_hbm, depth_ref)]
    small = [pltpu.make_async_copy(a, b, small_sems.at[i]) for i, (a, b) in enumerate(small)]

    def tracers_in(k):
        return pltpu.make_async_copy(t_hbm.at[first : first + 2, k], t_ref.at[k], sems.at[0, k])

    def velocity_in(k):
        return pltpu.make_async_copy(v_hbm.at[:, k], v_ref.at[k], sems.at[1, k])

    def tracers_out(k):
        return pltpu.make_async_copy(out_ref.at[k], out_hbm.at[first : first + 2, k], sems.at[2, k])

    for copy in small:
        copy.start()
    for k in range(LEVELS):
        tracers_in(k).start()
        velocity_in(k).start()
    for copy in small:
        copy.wait()
    even = lanes((8, LANE)) % 2 == 0
    load_wet = lambda at: ocean_ref[at : at + 8, :].astype(jnp.float32)
    for r in range(TILES):
        rows = pl.ds(8 * r, 8)
        edge = jnp.where(even, cols_in[0, rows, :], cols_in[1, rows, :])
        for k in range(LEVELS):
            for i, slot in enumerate((first * LEVELS + k, (first + 1) * LEVELS + k, SPEED + k)):
                edges[k, i, rows, :] = pltpu.roll(edge, (LANE - 2 * slot) % LANE, 1)
        here = load_wet(8 * r)
        wet_edge = pltpu.roll(edge, LANE - 2 * WET, 1)
        w_x[rows, :] = here * above(load_wet, row_hi[WET : WET + 1, :], r)
        w_y[rows, :] = here * ahead_y(here, wet_edge)
        before_y[rows, :] = here[:, :LANE] * wet_edge
        if first == 0:
            total[rows, :] = jnp.zeros((8, COLS), jnp.float32)
    w_before = load_wet(0)[0:1, :] * row_lo[WET : WET + 1, :]
    if first == 0:
        flux[...] = jnp.zeros((8, COLS), jnp.float32)
        line = rows_in[1 - odd_x, THICK : THICK + 1, :]
        for k in range(LEVELS):
            thick[k : k + 1, :] = jnp.broadcast_to(line[:, k : k + 1], (1, COLS))

    def level(k, _):
        tracers_in(k).wait()
        velocity_in(k).wait()
        u_before = row_lo[pl.ds(SPEED + k, 1), :] * w_before
        into_x = [upwind(u_before, row_lo[pl.ds((first + t) * LEVELS + k, 1), :], t_ref[k, t, 0:1, :]) for t in range(2)]
        carry, out_x = list(into_x), [None, None]
        if first == 0:
            depth = thick[pl.ds(k, 1), :]
        for r in range(ROWS // TALL):
            rows = pl.ds(TALL * r, TALL)
            u = v_ref[k, 0, rows, :] * w_x[rows, :]
            v = v_ref[k, 1, rows, :] * w_y[rows, :]
            v_before = edges[k, 2, rows, :] * before_y[rows, :]
            new = []
            for t in range(2):
                load = lambda at: t_ref[k, t, at : at + TALL, :]
                slot = (first + t) * LEVELS + k
                c = load(TALL * r)
                c_edge = edges[k, t, rows, :]
                here_x = upwind(u, c, above(load, row_hi[pl.ds(slot, 1), :], r, TALL))
                turned = pltpu.roll(here_x, 1, 0)
                past_x = jnp.where(sublanes((TALL, COLS)) == 0, carry[t], turned)
                carry[t] = turned[0:1, :]
                if r == ROWS // TALL - 1:
                    out_x[t] = here_x[TALL - 1 :, :]
                here_y = upwind(v, c, ahead_y(c, c_edge))
                past_y = behind_y(here_y, upwind(v_before, c_edge, c[:, :LANE]))
                value = (c - (here_x - past_x)) - (here_y - past_y)
                out_ref[k, t, rows, :] = value
                new.append(value)
            if first == 0:
                total[rows, :] = total[rows, :] + depth * (0.2 * new[0] - 0.8 * new[1])
        if first == 0:
            flux[0:1, :] = flux[0:1, :] + depth * (0.2 * into_x[0] - 0.8 * into_x[1])
            flux[1:2, :] = flux[1:2, :] + depth * (0.2 * out_x[0] - 0.8 * out_x[1])
        tracers_out(k).start()
        return 0

    lax.fori_loop(0, LEVELS, level, 0)

    if first == 0:
        row = sublanes((4, COLS))
        ext[0, 0:4, :] = row_lo[PART:COEF, :] - jnp.where(row == 3, flux[0:1, :], 0.0)
        ext[0, ROWS + 4 :, :] = row_hi[PART:COEF, :] + jnp.where(row == 0, flux[1:2, :], 0.0)
        ext[1, 0:4, :] = row_lo[COEF:EDGE, :]
        ext[1, ROWS + 4 :, :] = row_hi[COEF:EDGE, :]
        for r in range(TILES):
            rows = pl.ds(8 * r, 8)
            here = load_wet(8 * r)
            ext[0, 8 * r + 4 : 8 * r + 12, :] = total[rows, :] * here
            ext[1, 8 * r + 4 : 8 * r + 12, :] = coefficient(depth_ref[rows, :], here)
        tile = sublanes((8, LANE))
        for j in range(8):
            send_ref[j, 0:EXT, :] = ext[0, 16 * j : 16 * j + EXT, :]
            send_ref[j, EXT : 2 * EXT, :] = ext[1, 16 * j : 16 * j + EXT, :]
            edge = jnp.zeros((8, LANE), jnp.float32)
            if j == 0:
                edge = jnp.where((tile >= 1) & (tile <= 3), pltpu.roll(row_lo[EDGE:MESSAGE, :LANE], 4, 0), 0.0)
            if j == 7:
                edge = jnp.where((tile >= 4) & (tile <= 6), pltpu.roll(row_hi[EDGE:MESSAGE, :LANE], 4, 0), 0.0)
            send_ref[j, 2 * EXT : 2 * EXT + 8, :LANE] = edge
            send_ref[j, 2 * EXT : 2 * EXT + 8, LANE:] = jnp.zeros((8, LANE), jnp.float32)
    for k in range(LEVELS):
        tracers_out(k).wait()


def advect(first, tracers, velocity, ocean, row_even, row_odd, col_even, col_odd, extra):
    ins = [HBM] * 3 + [ANY] * 4
    operands = [tracers, velocity, ocean, row_even, row_odd, col_even, col_odd]
    out_specs = [HBM]
    out_shape = [f32(TRACERS, LEVELS, ROWS, COLS)]
    block = pltpu.VMEM((ROWS, COLS), jnp.float32)
    narrow = pltpu.VMEM((ROWS, LANE), jnp.float32)
    scratch = [
        pltpu.VMEM((LEVELS, 2, ROWS, COLS), jnp.float32),
        pltpu.VMEM((LEVELS, 2, ROWS, COLS), jnp.float32),
        pltpu.VMEM((LEVELS, 2, ROWS, COLS), jnp.float32),
        pltpu.VMEM((ROWS, COLS), jnp.int32),
        pltpu.VMEM((2, MESSAGE, COLS), jnp.float32),
        pltpu.VMEM((2, ROWS, LANE), jnp.float32),
        block,
        block,
        narrow,
        pltpu.VMEM((LEVELS, 3, ROWS, LANE), jnp.float32),
        pltpu.SemaphoreType.DMA((3, LEVELS)),
        pltpu.SemaphoreType.DMA((8,)),
    ]
    aliases = {}
    if first == 0:
        ins = ins + [HBM]
        operands = operands + [extra]
        out_specs.append(VMEM)
        out_shape.append(f32(8, 2 * EXT + 8, COLS))
        scratch += [
            block,
            block,
            pltpu.VMEM((8, COLS), jnp.float32),
            pltpu.VMEM((2, ROWS + 8, COLS), jnp.float32),
            pltpu.VMEM((16, COLS), jnp.float32),
        ]
    else:
        aliases = {len(operands): 0}
        ins = ins + [HBM]
        operands = operands + [extra]
    return pl.pallas_call(
        functools.partial(advect_kernel, first),
        in_specs=ins,
        out_specs=out_specs,
        out_shape=out_shape,
        scratch_shapes=scratch,
        input_output_aliases=aliases,
        compiler_params=pltpu.CompilerParams(vmem_limit_bytes=(LIMA if first == 0 else LIMB) * 2**20),
        cost_estimate=pl.CostEstimate(flops=24_000_000, bytes_accessed=9_400_000, transcendentals=0),
        name="advect_forcing" if first == 0 else "advect_rest",
    )(*operands)


def insert_kernel(_, tops, out_hbm, most, sem):
    top = jnp.max(tops[...], axis=0)
    for j in range(8):
        most[j] = top
    copy = pltpu.make_async_copy(most, out_hbm.at[:, 2 * EXT :, LANE:], sem.at[0])
    copy.start()
    copy.wait()


def insert(parcels, tops):
    return pl.pallas_call(
        insert_kernel,
        in_specs=[HBM, VMEM],
        out_specs=HBM,
        out_shape=f32(8, 2 * EXT + 8, COLS),
        scratch_shapes=[pltpu.VMEM((8, 8, LANE), jnp.float32), pltpu.SemaphoreType.DMA((1,))],
        input_output_aliases={0: 0},
        compiler_params=pltpu.CompilerParams(vmem_limit_bytes=60 * 2**20),
        cost_estimate=pl.CostEstimate(flops=1000, bytes_accessed=100_000, transcendentals=0),
        name="insert_maximum",
    )(parcels, tops)


NEAR = ((1, 0, 0.5), (-1, 0, 0.5), (0, 1, 0.5), (0, -1, 0.5), (1, 1, 0.125), (1, -1, 0.125), (-1, 1, 0.125), (-1, -1, 0.125))


def moved(x, rows, cols):
    if cols:
        lane = lanes(x.shape)
        x = pltpu.roll(x, (-cols) % x.shape[1], 1)
        x = jnp.where(lane == (x.shape[1] - 1 if cols > 0 else 0), 0.0, x)
    if rows:
        x = pltpu.roll(x, (-rows) % x.shape[0], 0)
    return x


def solve_kernel(got, out_ref, h_ref, f_ref, misc, weight, sems):
    copies = []
    for j in range(8):
        cols = pl.ds(j * COLS, COLS)
        copies.append(pltpu.make_async_copy(got.at[j, 0:EXT, :], f_ref.at[:, cols], sems.at[0, j]))
        copies.append(pltpu.make_async_copy(got.at[j, EXT : 2 * EXT, :], h_ref.at[:, cols], sems.at[1, j]))
        copies.append(pltpu.make_async_copy(got.at[j, 2 * EXT :, :], misc.at[j], sems.at[2, j]))
    for copy in copies:
        copy.start()
    for copy in copies:
        copy.wait()
    lane, tile = lanes((8, LANE)), sublanes((8, LANE))
    for j in range(7):
        pairs = misc[j, :, :LANE] * pltpu.roll(misc[j + 1, :, :LANE], LANE - 16, 1)
        flux = jnp.sum(jnp.where(lane <= LEVELS, pairs, 0.0), axis=1, keepdims=True)
        for rows, there in ((pl.ds(0, 8), tile < 4), (pl.ds(16, 8), tile >= 4)):
            last = pl.ds((j + 1) * COLS - LANE, LANE)
            after = pl.ds((j + 1) * COLS, LANE)
            f_ref[rows, last] = f_ref[rows, last] - jnp.where(there & (lane == LANE - 1), flux, 0.0)
            f_ref[rows, after] = f_ref[rows, after] + jnp.where(there & (lane == 0), flux, 0.0)
    most = jnp.max(misc[:, :, LANE:], axis=0)[0:1, 0:1]
    lam_max = 0.5 + 10.0 * most
    theta = (lam_max + 0.5) / 2.0
    delta = (lam_max - 0.5) / 2.0
    sigma = theta / delta
    rho = 1.0 / sigma
    h = h_ref[...]
    sides = {c: moved(h, 0, c) for c in (-1, 0, 1)}
    for n, (a, b, w) in enumerate(NEAR):
        weight[n] = w * (h + moved(sides[b], a, 0))
    inside = h > 0.0
    resid = f_ref[...]
    direction = resid / theta
    answer = jnp.zeros_like(resid)
    for _ in range(ITERS):
        sides = {c: moved(direction, 0, c) for c in (-1, 0, 1)}
        applied = 0.5 * direction
        for n, (a, b, w) in enumerate(NEAR):
            applied = applied + weight[n] * (direction - moved(sides[b], a, 0))
        resid = jnp.where(inside, resid - applied, 0.0)
        answer = answer + direction
        rho_next = 1.0 / (2.0 * sigma - rho)
        direction = rho_next * rho * direction + (2.0 * rho_next / delta) * resid
        rho = rho_next
    out_ref[...] = (answer + direction)[4:20, :]


def solve(got):
    return pl.pallas_call(
        solve_kernel,
        in_specs=[ANY],
        out_specs=VMEM,
        out_shape=f32(16, WIDE),
        scratch_shapes=[
            pltpu.VMEM((EXT, WIDE), jnp.float32),
            pltpu.VMEM((EXT, WIDE), jnp.float32),
            pltpu.VMEM((8, 8, COLS), jnp.float32),
            pltpu.VMEM((8, EXT, WIDE), jnp.float32),
            pltpu.SemaphoreType.DMA((3, 8)),
        ],
        compiler_params=pltpu.CompilerParams(vmem_limit_bytes=12 * 2**20),
        cost_estimate=pl.CostEstimate(flops=6_000_000, bytes_accessed=600_000, transcendentals=0),
        name="chebyshev",
    )(got)


def exchange(x, axis, odd):
    count = lax.axis_size(axis)
    pairs = []
    for i in range(odd, count - 1, 2):
        pairs += [(i, i + 1), (i + 1, i)]
    return lax.ppermute(x, axis, pairs)


def shards(tracers, velocity, ocean, thickness, depth):
    row_even, row_odd, col_even, col_odd, top = pack(thickness, tracers, velocity, ocean, depth)
    halos = (exchange(row_even, "bx", 0), exchange(row_odd, "bx", 1), exchange(col_even, "by", 0), exchange(col_odd, "by", 1))
    tops = lax.all_to_all(top, "bx", split_axis=0, concat_axis=0, tiled=True)
    part, parcels = advect(0, tracers, velocity, ocean, *halos, depth)
    got = lax.all_to_all(insert(parcels, tops), "by", split_axis=0, concat_axis=0, tiled=True)
    new_tracers = advect(2, tracers, velocity, ocean, *halos, part)[0]
    return new_tracers, solve(got)


def solution(mesh):
    return jax.shard_map(
        shards,
        mesh=mesh,
        in_specs=(
            P(None, None, "bx", "by"),
            P(None, None, "bx", "by"),
            P("bx", "by"),
            P(),
            P("bx", "by"),
        ),
        out_specs=(P(None, None, "bx", "by"), P(("bx", "by"), None)),
        check_vma=False,
    )
```

```python
import functools

import jax
import jax.numpy as jnp
from jax import lax
from jax.experimental import pallas as pl
from jax.experimental.pallas import tpu as pltpu
from jax.sharding import PartitionSpec as P

ITERS = 3
TRACERS = 4
LEVELS = 12
ROWS = 128
COLS = 256
TILES = ROWS // 8
LANE = 128
WIDE = 8 * COLS
EXT = 24
CHUNK = 32
TALL = 16
LIMA, LIMB, LIMC = 48, 48, 53

SPEED, WET, THICK, PART, COEF, EDGE, MESSAGE = 48, 60, 61, 64, 68, 72, 80
ANY = pl.BlockSpec(memory_space=pl.ANY)
HBM = pl.BlockSpec(memory_space=pltpu.HBM)
VMEM = pl.BlockSpec(memory_space=pltpu.VMEM)


def f32(*shape):
    return jax.ShapeDtypeStruct(shape, jnp.float32)


def lanes(shape):
    return lax.broadcasted_iota(jnp.int32, shape, len(shape) - 1)


def sublanes(shape):
    return lax.broadcasted_iota(jnp.int32, shape, len(shape) - 2)


def coefficient(depth, wet):
    return depth * (0.1 + 0.9 * wet)


def positive(x):
    return jnp.maximum(x, 0.0)


def negative(x):
    return jnp.minimum(x, 0.0)


def edge_forcing(q, u, v, wet, thick):
    shape = (8, COLS)
    row, col = sublanes(shape), lanes(shape)
    total = jnp.zeros(shape, jnp.float32)
    flux_x = jnp.zeros(shape, jnp.float32)
    flux_y = jnp.zeros(shape, jnp.float32)
    for k in range(LEVELS):
        depth = thick[k]
        total = total + depth * q[k]
        flux_x = flux_x + depth * (positive(u[k]) * q[k] + negative(u[k]) * pltpu.roll(q[k], 7, 0))
        flux_y = flux_y + depth * (positive(v[k]) * q[k] + negative(v[k]) * pltpu.roll(q[k], COLS - 1, 1))
    flux_x = flux_x * jnp.where(row == 7, 0.0, wet * pltpu.roll(wet, 7, 0))
    flux_y = flux_y * jnp.where(col == COLS - 1, 0.0, wet * pltpu.roll(wet, COLS - 1, 1))
    return wet * (total - (flux_x - pltpu.roll(flux_x, 1, 0)) - (flux_y - pltpu.roll(flux_y, 1, 1)))


def edge_terms(q, v, wet, thick):
    lane = lanes((8, LANE))
    last, first = wet[:, LANE:], wet[:, :LANE]
    upwind = jnp.zeros((8, LANE), jnp.float32)
    terms = jnp.where(lane == 28, pltpu.roll(first, 28, 1), 0.0)
    for k in range(LEVELS):
        depth = thick[k]
        speed = v[k][:, LANE:]
        upwind = upwind + depth * positive(speed) * q[k][:, LANE:]
        terms = jnp.where(lane == k, pltpu.roll(depth * negative(speed) * last, k + 1, 1), terms)
        terms = jnp.where(lane == 16 + k, pltpu.roll(q[k][:, :LANE] * first, 16 + k, 1), terms)
    return jnp.where(lane == LEVELS, pltpu.roll(upwind * last, LEVELS + 1, 1), terms)


def pack_kernel(thick_hbm, t_hbm, v_hbm, ocean_hbm, depth_hbm, row_even, row_odd, col_even, col_odd, top,
                t_ref, u_top, u_low, v_top, v_low, v_last, ocean_ref, depth_ref, thick, row_both, col_both, sems):
    odd_x, odd_y = lax.axis_index("bx") % 2, lax.axis_index("by") % 2
    row_hi, row_lo = row_both.at[0], row_both.at[1]
    col_hi, col_lo = col_both.at[0], col_both.at[1]

    def chunk_copy(c):
        rows = pl.ds(pl.multiple_of(c * CHUNK, CHUNK), CHUNK)
        return pltpu.make_async_copy(t_hbm.at[:, :, rows, :], t_ref.at[:, :, rows, :], sems.at[c])

    chunks = ROWS // CHUNK
    small = [
        pltpu.make_async_copy(ocean_hbm, ocean_ref, sems.at[chunks]),
        pltpu.make_async_copy(depth_hbm, depth_ref, sems.at[chunks + 1]),
        pltpu.make_async_copy(v_hbm.at[1, :, :, LANE:], v_last, sems.at[chunks + 2]),
        pltpu.make_async_copy(thick_hbm, thick, sems.at[chunks + 7]),
    ]
    tiles = [
        pltpu.make_async_copy(v_hbm.at[0, :, 0:8, :], u_top, sems.at[chunks + 3]),
        pltpu.make_async_copy(v_hbm.at[0, :, ROWS - 8 :, :], u_low, sems.at[chunks + 4]),
        pltpu.make_async_copy(v_hbm.at[1, :, 0:8, :], v_top, sems.at[chunks + 5]),
        pltpu.make_async_copy(v_hbm.at[1, :, ROWS - 8 :, :], v_low, sems.at[chunks + 6]),
    ]
    for copy in small:
        copy.start()
    for c in range(chunks):
        chunk_copy(c).start()
    for copy in tiles:
        copy.start()
    for copy in small:
        copy.wait()
    wet = ocean_ref[...].astype(jnp.float32)
    coef = coefficient(depth_ref[...], wet)
    most = jnp.max(jnp.max(coef, axis=0, keepdims=True), axis=1, keepdims=True)
    top[...] = jnp.broadcast_to(most[None], top.shape)
    thick_lanes = jnp.zeros((1, COLS), jnp.float32)
    for k in range(LEVELS):
        thick_lanes = jnp.where(lanes((1, COLS)) == k, thick[k], thick_lanes)

    def gather(c, _):
        chunk_copy(c).wait()
        lane = lanes((CHUNK, LANE))
        rows = pl.ds(pl.multiple_of(c * CHUNK, CHUNK), CHUNK)
        ocean = ocean_ref[rows, :].astype(jnp.float32)
        hi = jnp.where(lane == 2 * WET, pltpu.roll(ocean[:, LANE:], (2 * WET + 1) % LANE, 1), 0.0)
        lo = jnp.where(lane == 2 * WET - 1, pltpu.roll(ocean[:, :LANE], 2 * WET - 1, 1), 0.0)
        for k in range(LEVELS):
            for t in range(TRACERS):
                s = t * LEVELS + k
                hi = jnp.where(lane == 2 * s, pltpu.roll(t_ref[t, k, rows, LANE:], 2 * s + 1, 1), hi)
                place = (2 * s - 1) % LANE
                lo = jnp.where(lane == place, pltpu.roll(t_ref[t, k, rows, :LANE], place, 1), lo)
            s = SPEED + k
            hi = jnp.where(lane == 2 * s, pltpu.roll(v_last[k, rows, :], 2 * s + 1, 1), hi)
        col_hi[rows, :] = hi
        col_lo[rows, :] = lo
        return 0

    lax.fori_loop(0, chunks, gather, 0)
    for copy in tiles:
        copy.wait()
    for t in range(TRACERS):
        for k in range(LEVELS):
            s = t * LEVELS + k
            row_hi[s : s + 1, :] = t_ref[t, k, ROWS - 1 : ROWS, :]
            row_lo[s : s + 1, :] = t_ref[t, k, 0:1, :]
    for k in range(LEVELS):
        row_hi[SPEED + k : SPEED + k + 1, :] = u_low[k, 7:8, :]
    row_lo[SPEED:WET, :] = jnp.zeros((WET - SPEED, COLS), jnp.float32)
    for row, message, u, v, keep in ((0, row_lo, u_top, v_top, 0), (ROWS - 8, row_hi, u_low, v_low, 4)):
        rows = slice(row, row + 8)
        here = ocean_ref[rows, :].astype(jnp.float32)
        q = [0.2 * t_ref[0, k, rows, :] - 0.8 * t_ref[1, k, rows, :] for k in range(LEVELS)]
        speed_x = [u[k] for k in range(LEVELS)]
        speed_y = [v[k] for k in range(LEVELS)]
        message[WET:THICK, :] = here[7:8, :] if keep else here[0:1, :]
        message[THICK:PART, :] = jnp.broadcast_to(thick_lanes, (PART - THICK, COLS))
        message[PART:COEF, :] = edge_forcing(q, speed_x, speed_y, here, thick)[keep : keep + 4, :]
        message[COEF:EDGE, :] = coefficient(depth_ref[rows, :], here)[keep : keep + 4, :]
        message[EDGE:MESSAGE, :LANE] = edge_terms(q, speed_y, here, thick)
        message[EDGE:MESSAGE, LANE:] = jnp.zeros((8, LANE), jnp.float32)
    row_even[...] = row_both[odd_x]
    row_odd[...] = row_both[1 - odd_x]
    col_even[...] = col_both[odd_y]
    col_odd[...] = col_both[1 - odd_y]


def pack(thickness, tracers, velocity, ocean, depth):
    tile = (LEVELS, 8, COLS)
    return pl.pallas_call(
        pack_kernel,
        in_specs=[HBM] * 5,
        out_specs=[VMEM] * 5,
        out_shape=[f32(MESSAGE, COLS), f32(MESSAGE, COLS), f32(ROWS, LANE), f32(ROWS, LANE), f32(16, 8, LANE)],
        scratch_shapes=[
            pltpu.VMEM((TRACERS, LEVELS, ROWS, COLS), jnp.float32),
            pltpu.VMEM(tile, jnp.float32),
            pltpu.VMEM(tile, jnp.float32),
            pltpu.VMEM(tile, jnp.float32),
            pltpu.VMEM(tile, jnp.float32),
            pltpu.VMEM((LEVELS, ROWS, LANE), jnp.float32),
            pltpu.VMEM((ROWS, COLS), jnp.int32),
            pltpu.VMEM((ROWS, COLS), jnp.float32),
            pltpu.SMEM((LEVELS,), jnp.float32),
            pltpu.VMEM((2, MESSAGE, COLS), jnp.float32),
            pltpu.VMEM((2, ROWS, LANE), jnp.float32),
            pltpu.SemaphoreType.DMA((ROWS // CHUNK + 8,)),
        ],
        compiler_params=pltpu.CompilerParams(vmem_limit_bytes=60 * 2**20),
        cost_estimate=pl.CostEstimate(flops=4_000_000, bytes_accessed=7_400_000, transcendentals=0),
        name="pack_edges",
    )(thickness, tracers, velocity, ocean, depth)


def ahead_y(x, edge):
    last = lanes((x.shape[0], LANE)) == LANE - 1
    a, b = pltpu.roll(x[:, :LANE], LANE - 1, 1), pltpu.roll(x[:, LANE:], LANE - 1, 1)
    return jnp.concatenate([jnp.where(last, b, a), jnp.where(last, edge, b)], 1)


def behind_y(x, edge):
    first = lanes((x.shape[0], LANE)) == 0
    a, b = pltpu.roll(x[:, :LANE], 1, 1), pltpu.roll(x[:, LANE:], 1, 1)
    return jnp.concatenate([jnp.where(first, edge, a), jnp.where(first, a, b)], 1)


def above(load, edge, r, tall=8):
    if (r + 1) * tall < ROWS:
        return load(tall * r + 1)
    return jnp.where(sublanes((tall, COLS)) == tall - 1, edge, pltpu.roll(load(tall * r), tall - 1, 0))


def upwind(speed, here, ahead):
    return speed * jnp.where(speed > 0.0, here, ahead)


def advect_kernel(first, *refs):
    if first == 0:
        (t_hbm, v_hbm, ocean_hbm, row_even, row_odd, col_even, col_odd, depth_hbm, out_hbm, send_ref,
         t_ref, v_ref, out_ref, ocean_ref, rows_in, cols_in, w_x, w_y, before_y, edges, sems, small_sems,
         depth_ref, total, flux, ext, thick) = refs
    else:
        (t_hbm, v_hbm, ocean_hbm, row_even, row_odd, col_even, col_odd, _, out_hbm,
         t_ref, v_ref, out_ref, ocean_ref, rows_in, cols_in, w_x, w_y, before_y, edges, sems, small_sems) = refs
    odd_x, odd_y = lax.axis_index("bx") % 2, lax.axis_index("by") % 2
    row_lo, row_hi = rows_in.at[0], rows_in.at[1]
    small = [
        (ocean_hbm, ocean_ref),
        (row_even, rows_in.at[1 - odd_x]),
        (row_odd, rows_in.at[odd_x]),
        (col_even, cols_in.at[1 - odd_y]),
        (col_odd, cols_in.at[odd_y]),
    ]
    if first == 0:
        small += [(depth_hbm, depth_ref)]
    small = [pltpu.make_async_copy(a, b, small_sems.at[i]) for i, (a, b) in enumerate(small)]

    def tracers_in(k):
        return pltpu.make_async_copy(t_hbm.at[first : first + 2, k], t_ref.at[k], sems.at[0, k])

    def velocity_in(k):
        return pltpu.make_async_copy(v_hbm.at[:, k], v_ref.at[k], sems.at[1, k])

    def tracers_out(k):
        return pltpu.make_async_copy(out_ref.at[k], out_hbm.at[first : first + 2, k], sems.at[2, k])

    for copy in small:
        copy.start()
    for k in range(LEVELS):
        tracers_in(k).start()
        velocity_in(k).start()
    for copy in small:
        copy.wait()
    even = lanes((8, LANE)) % 2 == 0
    load_wet = lambda at: ocean_ref[at : at + 8, :].astype(jnp.float32)
    for r in range(TILES):
        rows = pl.ds(8 * r, 8)
        edge = jnp.where(even, cols_in[0, rows, :], cols_in[1, rows, :])
        for k in range(LEVELS):
            for i, slot in enumerate((first * LEVELS + k, (first + 1) * LEVELS + k, SPEED + k)):
                edges[k, i, rows, :] = pltpu.roll(edge, (LANE - 2 * slot) % LANE, 1)
        here = load_wet(8 * r)
        wet_edge = pltpu.roll(edge, LANE - 2 * WET, 1)
        w_x[rows, :] = here * above(load_wet, row_hi[WET : WET + 1, :], r)
        w_y[rows, :] = here * ahead_y(here, wet_edge)
        before_y[rows, :] = here[:, :LANE] * wet_edge
        if first == 0:
            total[rows, :] = jnp.zeros((8, COLS), jnp.float32)
    w_before = load_wet(0)[0:1, :] * row_lo[WET : WET + 1, :]
    if first == 0:
        flux[...] = jnp.zeros((8, COLS), jnp.float32)
        line = rows_in[1 - odd_x, THICK : THICK + 1, :]
        for k in range(LEVELS):
            thick[k : k + 1, :] = jnp.broadcast_to(line[:, k : k + 1], (1, COLS))

    def level(k, _):
        tracers_in(k).wait()
        velocity_in(k).wait()
        u_before = row_lo[pl.ds(SPEED + k, 1), :] * w_before
        into_x = [upwind(u_before, row_lo[pl.ds((first + t) * LEVELS + k, 1), :], t_ref[k, t, 0:1, :]) for t in range(2)]
        carry, out_x = list(into_x), [None, None]
        if first == 0:
            depth = thick[pl.ds(k, 1), :]
        for r in range(ROWS // TALL):
            rows = pl.ds(TALL * r, TALL)
            u = v_ref[k, 0, rows, :] * w_x[rows, :]
            v = v_ref[k, 1, rows, :] * w_y[rows, :]
            v_before = edges[k, 2, rows, :] * before_y[rows, :]
            new = []
            for t in range(2):
                load = lambda at: t_ref[k, t, at : at + TALL, :]
                slot = (first + t) * LEVELS + k
                c = load(TALL * r)
                c_edge = edges[k, t, rows, :]
                here_x = upwind(u, c, above(load, row_hi[pl.ds(slot, 1), :], r, TALL))
                turned = pltpu.roll(here_x, 1, 0)
                past_x = jnp.where(sublanes((TALL, COLS)) == 0, carry[t], turned)
                carry[t] = turned[0:1, :]
                if r == ROWS // TALL - 1:
                    out_x[t] = here_x[TALL - 1 :, :]
                here_y = upwind(v, c, ahead_y(c, c_edge))
                past_y = behind_y(here_y, upwind(v_before, c_edge, c[:, :LANE]))
                value = (c - (here_x - past_x)) - (here_y - past_y)
                out_ref[k, t, rows, :] = value
                new.append(value)
            if first == 0:
                total[rows, :] = total[rows, :] + depth * (0.2 * new[0] - 0.8 * new[1])
        if first == 0:
            flux[0:1, :] = flux[0:1, :] + depth * (0.2 * into_x[0] - 0.8 * into_x[1])
            flux[1:2, :] = flux[1:2, :] + depth * (0.2 * out_x[0] - 0.8 * out_x[1])
        tracers_out(k).start()
        return 0

    lax.fori_loop(0, LEVELS, level, 0)

    if first == 0:
        row = sublanes((4, COLS))
        ext[0, 0:4, :] = row_lo[PART:COEF, :] - jnp.where(row == 3, flux[0:1, :], 0.0)
        ext[0, ROWS + 4 :, :] = row_hi[PART:COEF, :] + jnp.where(row == 0, flux[1:2, :], 0.0)
        ext[1, 0:4, :] = row_lo[COEF:EDGE, :]
        ext[1, ROWS + 4 :, :] = row_hi[COEF:EDGE, :]
        for r in range(TILES):
            rows = pl.ds(8 * r, 8)
            here = load_wet(8 * r)
            ext[0, 8 * r + 4 : 8 * r + 12, :] = total[rows, :] * here
            ext[1, 8 * r + 4 : 8 * r + 12, :] = coefficient(depth_ref[rows, :], here)
        for j in range(8):
            at = 16 * j
            send_ref[j, 0:22, :] = ext[0, at + 1 : at + 23, :]
            send_ref[j, 22:44, :] = ext[1, at + 1 : at + 23, :]
            line = jnp.zeros((1, LANE), jnp.float32)
            halves = [line, line]
            if j in (0, 7):
                for i in range(3):
                    factors = row_lo[EDGE + 5 + i : EDGE + 6 + i, :LANE] if j == 0 else row_hi[EDGE + i : EDGE + 1 + i, :LANE]
                    at = 32 * (i if j == 0 else 3 + i)
                    halves[at // LANE] = halves[at // LANE] + (pltpu.roll(factors, at % LANE, 1) if at % LANE else factors)
            send_ref[j, 44:45, :] = jnp.concatenate(halves, 1)
            send_ref[j, 45:48, :] = jnp.zeros((3, COLS), jnp.float32)
    for k in range(LEVELS):
        tracers_out(k).wait()


def advect(first, tracers, velocity, ocean, row_even, row_odd, col_even, col_odd, extra):
    ins = [HBM] * 3 + [ANY] * 4
    operands = [tracers, velocity, ocean, row_even, row_odd, col_even, col_odd]
    out_specs = [HBM]
    out_shape = [f32(TRACERS, LEVELS, ROWS, COLS)]
    block = pltpu.VMEM((ROWS, COLS), jnp.float32)
    narrow = pltpu.VMEM((ROWS, LANE), jnp.float32)
    scratch = [
        pltpu.VMEM((LEVELS, 2, ROWS, COLS), jnp.float32),
        pltpu.VMEM((LEVELS, 2, ROWS, COLS), jnp.float32),
        pltpu.VMEM((LEVELS, 2, ROWS, COLS), jnp.float32),
        pltpu.VMEM((ROWS, COLS), jnp.int32),
        pltpu.VMEM((2, MESSAGE, COLS), jnp.float32),
        pltpu.VMEM((2, ROWS, LANE), jnp.float32),
        block,
        block,
        narrow,
        pltpu.VMEM((LEVELS, 3, ROWS, LANE), jnp.float32),
        pltpu.SemaphoreType.DMA((3, LEVELS)),
        pltpu.SemaphoreType.DMA((8,)),
    ]
    aliases = {}
    if first == 0:
        ins = ins + [HBM]
        operands = operands + [extra]
        out_specs.append(VMEM)
        out_shape.append(f32(8, 48, COLS))
        scratch += [
            block,
            block,
            pltpu.VMEM((8, COLS), jnp.float32),
            pltpu.VMEM((2, ROWS + 8, COLS), jnp.float32),
            pltpu.VMEM((16, COLS), jnp.float32),
        ]
    else:
        aliases = {len(operands): 0}
        ins = ins + [HBM]
        operands = operands + [extra]
    return pl.pallas_call(
        functools.partial(advect_kernel, first),
        in_specs=ins,
        out_specs=out_specs,
        out_shape=out_shape,
        scratch_shapes=scratch,
        input_output_aliases=aliases,
        compiler_params=pltpu.CompilerParams(vmem_limit_bytes=(LIMA if first == 0 else LIMB) * 2**20),
        cost_estimate=pl.CostEstimate(flops=24_000_000, bytes_accessed=9_400_000, transcendentals=0),
        name="advect_forcing" if first == 0 else "advect_rest",
    )(*operands)


def insert_kernel(parcels_hbm, tops_hbm, out_ref, tops, sems):
    copies = [pltpu.make_async_copy(tops_hbm, tops, sems.at[0]), pltpu.make_async_copy(parcels_hbm, out_ref, sems.at[1])]
    for copy in copies:
        copy.start()
    for copy in copies:
        copy.wait()
    most = jnp.max(tops[...], axis=0)[0:1, :]
    for j in range(8):
        out_ref[j, 45:46, :LANE] = most


def insert(parcels, tops):
    return pl.pallas_call(
        insert_kernel,
        in_specs=[ANY] * 2,
        out_specs=VMEM,
        out_shape=f32(8, 48, COLS),
        scratch_shapes=[pltpu.VMEM((16, 8, LANE), jnp.float32), pltpu.SemaphoreType.DMA((2,))],
        compiler_params=pltpu.CompilerParams(vmem_limit_bytes=LIMC * 2**20),
        cost_estimate=pl.CostEstimate(flops=1000, bytes_accessed=900_000, transcendentals=0),
        name="insert_maximum",
    )(parcels, tops)


NEAR = ((0, 1, 0.5), (1, 0, 0.5), (1, 1, 0.125), (1, -1, 0.125))
PADDED = WIDE + LANE


def moved(x, rows, cols):
    if cols:
        x = pltpu.roll(x, (-cols) % x.shape[1], 1)
    if rows:
        x = pltpu.roll(x, (-rows) % x.shape[0], 0)
    return x


def solve_kernel(got_ref, out_ref, h_ref, resid_ref, direction_ref, answer_ref, weight):
    for ref in (h_ref, resid_ref):
        for row in (0, EXT - 1):
            ref[row : row + 1, :] = jnp.zeros((1, PADDED), jnp.float32)
        ref[:, WIDE:] = jnp.zeros((EXT, LANE), jnp.float32)
    for j in range(8):
        cols = pl.ds(j * COLS, COLS)
        resid_ref[1:23, cols] = got_ref[j, 0:22, :]
        h_ref[1:23, cols] = got_ref[j, 22:44, :]
    lane, tile = lanes((8, LANE)), sublanes((8, LANE))
    group, row = lanes((8, COLS)), sublanes((8, COLS))
    used = (row >= 1) & (row <= 6) & (group >= 32 * (row - 1)) & (group <= 32 * (row - 1) + LEVELS)
    for j in range(7):
        pairs = got_ref[j, 44:45, :] * pltpu.roll(got_ref[j + 1, 44:45, :], COLS - 16, 1)
        flux = jnp.sum(jnp.where(used, pairs, 0.0), axis=1, keepdims=True)
        for rows, there in ((pl.ds(0, 8), tile < 4), (pl.ds(16, 8), tile >= 4)):
            last = pl.ds((j + 1) * COLS - LANE, LANE)
            after = pl.ds((j + 1) * COLS, LANE)
            resid_ref[rows, last] = resid_ref[rows, last] - jnp.where(there & (lane == LANE - 1), flux, 0.0)
            resid_ref[rows, after] = resid_ref[rows, after] + jnp.where(there & (lane == 0), flux, 0.0)
    most = got_ref[0, 45:46, 0:1]
    for j in range(1, 8):
        most = jnp.maximum(most, got_ref[j, 45:46, 0:1])
    lam_max = 0.5 + 10.0 * most
    theta = (lam_max + 0.5) / 2.0
    delta = (lam_max - 0.5) / 2.0
    sigma = theta / delta
    h = h_ref[...]
    sides = {c: moved(h, 0, c) for c in (-1, 0, 1)}
    for n, (a, b, w) in enumerate(NEAR):
        weight[n] = w * (h + moved(sides[b], a, 0))
    direction_ref[...] = resid_ref[...] / theta
    answer_ref[...] = direction_ref[...]

    def step(_, rho):
        direction = direction_ref[...]
        east, west = moved(direction, 0, 1), moved(direction, 0, -1)
        right = weight[0] * (direction - east)
        down = weight[1] * (direction - moved(direction, 1, 0))
        right_down = weight[2] * (direction - moved(east, 1, 0))
        left_down = weight[3] * (direction - moved(west, 1, 0))
        applied = (0.5 * direction + (right - moved(right, 0, -1))) + ((down + right_down) + left_down)
        applied = applied - moved(down + (moved(right_down, 0, -1) + moved(left_down, 0, 1)), -1, 0)
        resid = jnp.where(h_ref[...] > 0.0, resid_ref[...] - applied, 0.0)
        resid_ref[...] = resid
        rho_next = 1.0 / (2.0 * sigma - rho)
        direction = rho_next * rho * direction + (2.0 * rho_next / delta) * resid
        direction_ref[...] = direction
        answer_ref[...] = answer_ref[...] + direction
        return rho_next

    lax.fori_loop(0, ITERS, step, 1.0 / sigma)
    out_ref[...] = answer_ref[4:20, :WIDE]


def solve(got):
    wide = pltpu.VMEM((EXT, PADDED), jnp.float32)
    return pl.pallas_call(
        solve_kernel,
        in_specs=[VMEM],
        out_specs=VMEM,
        out_shape=f32(16, WIDE),
        scratch_shapes=[wide, wide, wide, wide, pltpu.VMEM((4, EXT, PADDED), jnp.float32)],
        compiler_params=pltpu.CompilerParams(vmem_limit_bytes=60 * 2**20),
        cost_estimate=pl.CostEstimate(flops=6_000_000, bytes_accessed=600_000, transcendentals=0),
        name="chebyshev",
    )(got)


def exchange(x, axis, odd):
    count = lax.axis_size(axis)
    pairs = []
    for i in range(odd, count - 1, 2):
        pairs += [(i, i + 1), (i + 1, i)]
    return lax.ppermute(x, axis, pairs)


def shards(tracers, velocity, ocean, thickness, depth):
    row_even, row_odd, col_even, col_odd, top = pack(thickness, tracers, velocity, ocean, depth)
    halos = (exchange(row_even, "bx", 0), exchange(row_odd, "bx", 1), exchange(col_even, "by", 0), exchange(col_odd, "by", 1))
    tops = lax.all_to_all(top, "bx", split_axis=0, concat_axis=0, tiled=True)
    part, parcels = advect(0, tracers, velocity, ocean, *halos, depth)
    got = lax.all_to_all(insert(parcels, tops), "by", split_axis=0, concat_axis=0, tiled=True)
    new_tracers = advect(2, tracers, velocity, ocean, *halos, part)[0]
    return new_tracers, solve(got)


def solution(mesh):
    return jax.shard_map(
        shards,
        mesh=mesh,
        in_specs=(
            P(None, None, "bx", "by"),
            P(None, None, "bx", "by"),
            P("bx", "by"),
            P(),
            P("bx", "by"),
        ),
        out_specs=(P(None, None, "bx", "by"), P(("bx", "by"), None)),
        check_vma=False,
    )
```

```python
import functools

import jax
import jax.numpy as jnp
from jax import lax
from jax.experimental import pallas as pl
from jax.experimental.pallas import tpu as pltpu
from jax.sharding import PartitionSpec as P

ITERS = 3
TRACERS = 4
LEVELS = 12
ROWS = 128
COLS = 256
TILES = ROWS // 8
LANE = 128
WIDE = 8 * COLS
EXT = 24
CHUNK = 32
TALL = 16
LIMA, LIMB = 48, 48

SPEED, WET, THICK, PART, COEF, EDGE, MESSAGE = 48, 60, 61, 64, 68, 72, 80
ANY = pl.BlockSpec(memory_space=pl.ANY)
HBM = pl.BlockSpec(memory_space=pltpu.HBM)
VMEM = pl.BlockSpec(memory_space=pltpu.VMEM)


def f32(*shape):
    return jax.ShapeDtypeStruct(shape, jnp.float32)


def lanes(shape):
    return lax.broadcasted_iota(jnp.int32, shape, len(shape) - 1)


def sublanes(shape):
    return lax.broadcasted_iota(jnp.int32, shape, len(shape) - 2)


def coefficient(depth, wet):
    return depth * (0.1 + 0.9 * wet)


def positive(x):
    return jnp.maximum(x, 0.0)


def negative(x):
    return jnp.minimum(x, 0.0)


def edge_forcing(q, u, v, wet, thick):
    shape = (8, COLS)
    row, col = sublanes(shape), lanes(shape)
    total = jnp.zeros(shape, jnp.float32)
    flux_x = jnp.zeros(shape, jnp.float32)
    flux_y = jnp.zeros(shape, jnp.float32)
    for k in range(LEVELS):
        depth = thick[k]
        total = total + depth * q[k]
        flux_x = flux_x + depth * (positive(u[k]) * q[k] + negative(u[k]) * pltpu.roll(q[k], 7, 0))
        flux_y = flux_y + depth * (positive(v[k]) * q[k] + negative(v[k]) * pltpu.roll(q[k], COLS - 1, 1))
    flux_x = flux_x * jnp.where(row == 7, 0.0, wet * pltpu.roll(wet, 7, 0))
    flux_y = flux_y * jnp.where(col == COLS - 1, 0.0, wet * pltpu.roll(wet, COLS - 1, 1))
    return wet * (total - (flux_x - pltpu.roll(flux_x, 1, 0)) - (flux_y - pltpu.roll(flux_y, 1, 1)))


def edge_terms(q, v, wet, thick):
    lane = lanes((8, LANE))
    last, first = wet[:, LANE:], wet[:, :LANE]
    upwind = jnp.zeros((8, LANE), jnp.float32)
    terms = jnp.where(lane == 28, pltpu.roll(first, 28, 1), 0.0)
    for k in range(LEVELS):
        depth = thick[k]
        speed = v[k][:, LANE:]
        upwind = upwind + depth * positive(speed) * q[k][:, LANE:]
        terms = jnp.where(lane == k, pltpu.roll(depth * negative(speed) * last, k + 1, 1), terms)
        terms = jnp.where(lane == 16 + k, pltpu.roll(q[k][:, :LANE] * first, 16 + k, 1), terms)
    return jnp.where(lane == LEVELS, pltpu.roll(upwind * last, LEVELS + 1, 1), terms)


def pack_kernel(thick_hbm, t_hbm, v_hbm, ocean_hbm, depth_hbm, row_even, row_odd, col_even, col_odd, top,
                t_ref, u_top, u_low, v_top, v_low, v_last, ocean_ref, depth_ref, thick, row_both, col_both, sems):
    odd_x, odd_y = lax.axis_index("bx") % 2, lax.axis_index("by") % 2
    row_hi, row_lo = row_both.at[0], row_both.at[1]
    col_hi, col_lo = col_both.at[0], col_both.at[1]

    def chunk_copy(c):
        rows = pl.ds(pl.multiple_of(c * CHUNK, CHUNK), CHUNK)
        return pltpu.make_async_copy(t_hbm.at[:, :, rows, :], t_ref.at[:, :, rows, :], sems.at[c])

    chunks = ROWS // CHUNK
    small = [
        pltpu.make_async_copy(ocean_hbm, ocean_ref, sems.at[chunks]),
        pltpu.make_async_copy(depth_hbm, depth_ref, sems.at[chunks + 1]),
        pltpu.make_async_copy(v_hbm.at[1, :, :, LANE:], v_last, sems.at[chunks + 2]),
        pltpu.make_async_copy(thick_hbm, thick, sems.at[chunks + 7]),
    ]
    tiles = [
        pltpu.make_async_copy(v_hbm.at[0, :, 0:8, :], u_top, sems.at[chunks + 3]),
        pltpu.make_async_copy(v_hbm.at[0, :, ROWS - 8 :, :], u_low, sems.at[chunks + 4]),
        pltpu.make_async_copy(v_hbm.at[1, :, 0:8, :], v_top, sems.at[chunks + 5]),
        pltpu.make_async_copy(v_hbm.at[1, :, ROWS - 8 :, :], v_low, sems.at[chunks + 6]),
    ]
    for copy in small:
        copy.start()
    for c in range(chunks):
        chunk_copy(c).start()
    for copy in tiles:
        copy.start()
    for copy in small:
        copy.wait()
    wet = ocean_ref[...].astype(jnp.float32)
    coef = coefficient(depth_ref[...], wet)
    most = jnp.max(jnp.max(coef, axis=0, keepdims=True), axis=1, keepdims=True)
    top[...] = jnp.broadcast_to(most[None], top.shape)
    thick_lanes = jnp.zeros((1, COLS), jnp.float32)
    for k in range(LEVELS):
        thick_lanes = jnp.where(lanes((1, COLS)) == k, thick[k], thick_lanes)

    def gather(c, _):
        chunk_copy(c).wait()
        lane = lanes((CHUNK, LANE))
        rows = pl.ds(pl.multiple_of(c * CHUNK, CHUNK), CHUNK)
        ocean = ocean_ref[rows, :].astype(jnp.float32)
        hi = jnp.where(lane == 2 * WET, pltpu.roll(ocean[:, LANE:], (2 * WET + 1) % LANE, 1), 0.0)
        lo = jnp.where(lane == 2 * WET - 1, pltpu.roll(ocean[:, :LANE], 2 * WET - 1, 1), 0.0)
        for k in range(LEVELS):
            for t in range(TRACERS):
                s = t * LEVELS + k
                hi = jnp.where(lane == 2 * s, pltpu.roll(t_ref[t, k, rows, LANE:], 2 * s + 1, 1), hi)
                place = (2 * s - 1) % LANE
                lo = jnp.where(lane == place, pltpu.roll(t_ref[t, k, rows, :LANE], place, 1), lo)
            s = SPEED + k
            hi = jnp.where(lane == 2 * s, pltpu.roll(v_last[k, rows, :], 2 * s + 1, 1), hi)
        col_hi[rows, :] = hi
        col_lo[rows, :] = lo
        return 0

    lax.fori_loop(0, chunks, gather, 0)
    for copy in tiles:
        copy.wait()
    for t in range(TRACERS):
        for k in range(LEVELS):
            s = t * LEVELS + k
            row_hi[s : s + 1, :] = t_ref[t, k, ROWS - 1 : ROWS, :]
            row_lo[s : s + 1, :] = t_ref[t, k, 0:1, :]
    for k in range(LEVELS):
        row_hi[SPEED + k : SPEED + k + 1, :] = u_low[k, 7:8, :]
    row_lo[SPEED:WET, :] = jnp.zeros((WET - SPEED, COLS), jnp.float32)
    for row, message, u, v, keep in ((0, row_lo, u_top, v_top, 0), (ROWS - 8, row_hi, u_low, v_low, 4)):
        rows = slice(row, row + 8)
        here = ocean_ref[rows, :].astype(jnp.float32)
        q = [0.2 * t_ref[0, k, rows, :] - 0.8 * t_ref[1, k, rows, :] for k in range(LEVELS)]
        speed_x = [u[k] for k in range(LEVELS)]
        speed_y = [v[k] for k in range(LEVELS)]
        message[WET:THICK, :] = here[7:8, :] if keep else here[0:1, :]
        message[THICK:PART, :] = jnp.broadcast_to(thick_lanes, (PART - THICK, COLS))
        message[PART:COEF, :] = edge_forcing(q, speed_x, speed_y, here, thick)[keep : keep + 4, :]
        message[COEF:EDGE, :] = coefficient(depth_ref[rows, :], here)[keep : keep + 4, :]
        message[EDGE:MESSAGE, :LANE] = edge_terms(q, speed_y, here, thick)
        message[EDGE:MESSAGE, LANE:] = jnp.zeros((8, LANE), jnp.float32)
    row_even[...] = row_both[odd_x]
    row_odd[...] = row_both[1 - odd_x]
    col_even[...] = col_both[odd_y]
    col_odd[...] = col_both[1 - odd_y]


def pack(thickness, tracers, velocity, ocean, depth):
    tile = (LEVELS, 8, COLS)
    return pl.pallas_call(
        pack_kernel,
        in_specs=[HBM] * 5,
        out_specs=[VMEM] * 5,
        out_shape=[f32(MESSAGE, COLS), f32(MESSAGE, COLS), f32(ROWS, LANE), f32(ROWS, LANE), f32(16, 8, LANE)],
        scratch_shapes=[
            pltpu.VMEM((TRACERS, LEVELS, ROWS, COLS), jnp.float32),
            pltpu.VMEM(tile, jnp.float32),
            pltpu.VMEM(tile, jnp.float32),
            pltpu.VMEM(tile, jnp.float32),
            pltpu.VMEM(tile, jnp.float32),
            pltpu.VMEM((LEVELS, ROWS, LANE), jnp.float32),
            pltpu.VMEM((ROWS, COLS), jnp.int32),
            pltpu.VMEM((ROWS, COLS), jnp.float32),
            pltpu.SMEM((LEVELS,), jnp.float32),
            pltpu.VMEM((2, MESSAGE, COLS), jnp.float32),
            pltpu.VMEM((2, ROWS, LANE), jnp.float32),
            pltpu.SemaphoreType.DMA((ROWS // CHUNK + 8,)),
        ],
        compiler_params=pltpu.CompilerParams(vmem_limit_bytes=60 * 2**20),
        cost_estimate=pl.CostEstimate(flops=4_000_000, bytes_accessed=7_400_000, transcendentals=0),
        name="pack_edges",
    )(thickness, tracers, velocity, ocean, depth)


def ahead_y(x, edge):
    last = lanes((x.shape[0], LANE)) == LANE - 1
    a, b = pltpu.roll(x[:, :LANE], LANE - 1, 1), pltpu.roll(x[:, LANE:], LANE - 1, 1)
    return jnp.concatenate([jnp.where(last, b, a), jnp.where(last, edge, b)], 1)


def behind_y(x, edge):
    first = lanes((x.shape[0], LANE)) == 0
    a, b = pltpu.roll(x[:, :LANE], 1, 1), pltpu.roll(x[:, LANE:], 1, 1)
    return jnp.concatenate([jnp.where(first, edge, a), jnp.where(first, a, b)], 1)


def above(load, edge, r, tall=8):
    if (r + 1) * tall < ROWS:
        return load(tall * r + 1)
    return jnp.where(sublanes((tall, COLS)) == tall - 1, edge, pltpu.roll(load(tall * r), tall - 1, 0))


def upwind(speed, here, ahead):
    return speed * jnp.where(speed > 0.0, here, ahead)


def advect_kernel(first, *refs):
    if first == 0:
        (t_hbm, v_hbm, ocean_hbm, row_even, row_odd, col_even, col_odd, depth_hbm, out_hbm, send_ref,
         t_ref, v_ref, out_ref, ocean_ref, rows_in, cols_in, w_x, w_y, before_y, edges, sems, small_sems,
         depth_ref, total, flux, ext, thick) = refs
    else:
        (t_hbm, v_hbm, ocean_hbm, row_even, row_odd, col_even, col_odd, _, out_hbm,
         t_ref, v_ref, out_ref, ocean_ref, rows_in, cols_in, w_x, w_y, before_y, edges, sems, small_sems) = refs
    odd_x, odd_y = lax.axis_index("bx") % 2, lax.axis_index("by") % 2
    row_lo, row_hi = rows_in.at[0], rows_in.at[1]
    small = [
        (ocean_hbm, ocean_ref),
        (row_even, rows_in.at[1 - odd_x]),
        (row_odd, rows_in.at[odd_x]),
        (col_even, cols_in.at[1 - odd_y]),
        (col_odd, cols_in.at[odd_y]),
    ]
    if first == 0:
        small += [(depth_hbm, depth_ref)]
    small = [pltpu.make_async_copy(a, b, small_sems.at[i]) for i, (a, b) in enumerate(small)]

    def tracers_in(k):
        return pltpu.make_async_copy(t_hbm.at[first : first + 2, k], t_ref.at[k], sems.at[0, k])

    def velocity_in(k):
        return pltpu.make_async_copy(v_hbm.at[:, k], v_ref.at[k], sems.at[1, k])

    def tracers_out(k):
        return pltpu.make_async_copy(out_ref.at[k], out_hbm.at[first : first + 2, k], sems.at[2, k])

    for copy in small:
        copy.start()
    for k in range(LEVELS):
        tracers_in(k).start()
        velocity_in(k).start()
    for copy in small:
        copy.wait()
    even = lanes((8, LANE)) % 2 == 0
    load_wet = lambda at: ocean_ref[at : at + 8, :].astype(jnp.float32)
    for r in range(TILES):
        rows = pl.ds(8 * r, 8)
        edge = jnp.where(even, cols_in[0, rows, :], cols_in[1, rows, :])
        for k in range(LEVELS):
            for i, slot in enumerate((first * LEVELS + k, (first + 1) * LEVELS + k, SPEED + k)):
                edges[k, i, rows, :] = pltpu.roll(edge, (LANE - 2 * slot) % LANE, 1)
        here = load_wet(8 * r)
        wet_edge = pltpu.roll(edge, LANE - 2 * WET, 1)
        w_x[rows, :] = here * above(load_wet, row_hi[WET : WET + 1, :], r)
        w_y[rows, :] = here * ahead_y(here, wet_edge)
        before_y[rows, :] = here[:, :LANE] * wet_edge
        if first == 0:
            total[rows, :] = jnp.zeros((8, COLS), jnp.float32)
    w_before = load_wet(0)[0:1, :] * row_lo[WET : WET + 1, :]
    if first == 0:
        flux[...] = jnp.zeros((8, COLS), jnp.float32)
        line = rows_in[1 - odd_x, THICK : THICK + 1, :]
        for k in range(LEVELS):
            thick[k : k + 1, :] = jnp.broadcast_to(line[:, k : k + 1], (1, COLS))

    def level(k, _):
        tracers_in(k).wait()
        velocity_in(k).wait()
        u_before = row_lo[pl.ds(SPEED + k, 1), :] * w_before
        into_x = [upwind(u_before, row_lo[pl.ds((first + t) * LEVELS + k, 1), :], t_ref[k, t, 0:1, :]) for t in range(2)]
        carry, out_x = list(into_x), [None, None]
        if first == 0:
            depth = thick[pl.ds(k, 1), :]
        for r in range(ROWS // TALL):
            rows = pl.ds(TALL * r, TALL)
            u = v_ref[k, 0, rows, :] * w_x[rows, :]
            v = v_ref[k, 1, rows, :] * w_y[rows, :]
            v_before = edges[k, 2, rows, :] * before_y[rows, :]
            new = []
            for t in range(2):
                load = lambda at: t_ref[k, t, at : at + TALL, :]
                slot = (first + t) * LEVELS + k
                c = load(TALL * r)
                c_edge = edges[k, t, rows, :]
                here_x = upwind(u, c, above(load, row_hi[pl.ds(slot, 1), :], r, TALL))
                turned = pltpu.roll(here_x, 1, 0)
                past_x = jnp.where(sublanes((TALL, COLS)) == 0, carry[t], turned)
                carry[t] = turned[0:1, :]
                if r == ROWS // TALL - 1:
                    out_x[t] = here_x[TALL - 1 :, :]
                here_y = upwind(v, c, ahead_y(c, c_edge))
                past_y = behind_y(here_y, upwind(v_before, c_edge, c[:, :LANE]))
                value = (c - (here_x - past_x)) - (here_y - past_y)
                out_ref[k, t, rows, :] = value
                new.append(value)
            if first == 0:
                total[rows, :] = total[rows, :] + depth * (0.2 * new[0] - 0.8 * new[1])
        if first == 0:
            flux[0:1, :] = flux[0:1, :] + depth * (0.2 * into_x[0] - 0.8 * into_x[1])
            flux[1:2, :] = flux[1:2, :] + depth * (0.2 * out_x[0] - 0.8 * out_x[1])
        tracers_out(k).start()
        return 0

    lax.fori_loop(0, LEVELS, level, 0)

    if first == 0:
        row = sublanes((4, COLS))
        ext[0, 0:4, :] = row_lo[PART:COEF, :] - jnp.where(row == 3, flux[0:1, :], 0.0)
        ext[0, ROWS + 4 :, :] = row_hi[PART:COEF, :] + jnp.where(row == 0, flux[1:2, :], 0.0)
        ext[1, 0:4, :] = row_lo[COEF:EDGE, :]
        ext[1, ROWS + 4 :, :] = row_hi[COEF:EDGE, :]
        for r in range(TILES):
            rows = pl.ds(8 * r, 8)
            here = load_wet(8 * r)
            ext[0, 8 * r + 4 : 8 * r + 12, :] = total[rows, :] * here
            ext[1, 8 * r + 4 : 8 * r + 12, :] = coefficient(depth_ref[rows, :], here)
        for j in range(8):
            at = 16 * j
            send_ref[j, 0:22, :] = ext[0, at + 1 : at + 23, :]
            send_ref[j, 22:44, :] = ext[1, at + 1 : at + 23, :]
            line = jnp.zeros((1, LANE), jnp.float32)
            halves = [line, line]
            if j in (0, 7):
                for i in range(3):
                    factors = row_lo[EDGE + 5 + i : EDGE + 6 + i, :LANE] if j == 0 else row_hi[EDGE + i : EDGE + 1 + i, :LANE]
                    at = 32 * (i if j == 0 else 3 + i)
                    halves[at // LANE] = halves[at // LANE] + (pltpu.roll(factors, at % LANE, 1) if at % LANE else factors)
            send_ref[j, 44:45, :] = jnp.concatenate(halves, 1)
            send_ref[j, 45:48, :] = jnp.zeros((3, COLS), jnp.float32)
    for k in range(LEVELS):
        tracers_out(k).wait()


def advect(first, tracers, velocity, ocean, row_even, row_odd, col_even, col_odd, extra):
    ins = [HBM] * 3 + [ANY] * 4
    operands = [tracers, velocity, ocean, row_even, row_odd, col_even, col_odd]
    out_specs = [HBM]
    out_shape = [f32(TRACERS, LEVELS, ROWS, COLS)]
    block = pltpu.VMEM((ROWS, COLS), jnp.float32)
    narrow = pltpu.VMEM((ROWS, LANE), jnp.float32)
    scratch = [
        pltpu.VMEM((LEVELS, 2, ROWS, COLS), jnp.float32),
        pltpu.VMEM((LEVELS, 2, ROWS, COLS), jnp.float32),
        pltpu.VMEM((LEVELS, 2, ROWS, COLS), jnp.float32),
        pltpu.VMEM((ROWS, COLS), jnp.int32),
        pltpu.VMEM((2, MESSAGE, COLS), jnp.float32),
        pltpu.VMEM((2, ROWS, LANE), jnp.float32),
        block,
        block,
        narrow,
        pltpu.VMEM((LEVELS, 3, ROWS, LANE), jnp.float32),
        pltpu.SemaphoreType.DMA((3, LEVELS)),
        pltpu.SemaphoreType.DMA((8,)),
    ]
    aliases = {}
    if first == 0:
        ins = ins + [HBM]
        operands = operands + [extra]
        out_specs.append(VMEM)
        out_shape.append(f32(8, 48, COLS))
        scratch += [
            block,
            block,
            pltpu.VMEM((8, COLS), jnp.float32),
            pltpu.VMEM((2, ROWS + 8, COLS), jnp.float32),
            pltpu.VMEM((16, COLS), jnp.float32),
        ]
    else:
        aliases = {len(operands): 0}
        ins = ins + [HBM]
        operands = operands + [extra]
    return pl.pallas_call(
        functools.partial(advect_kernel, first),
        in_specs=ins,
        out_specs=out_specs,
        out_shape=out_shape,
        scratch_shapes=scratch,
        input_output_aliases=aliases,
        compiler_params=pltpu.CompilerParams(vmem_limit_bytes=(LIMA if first == 0 else LIMB) * 2**20),
        cost_estimate=pl.CostEstimate(flops=24_000_000, bytes_accessed=9_400_000, transcendentals=0),
        name="advect_forcing" if first == 0 else "advect_rest",
    )(*operands)


def insert_kernel(_, tops, out_hbm, most, sem):
    most[...] = jnp.broadcast_to(jnp.max(tops[...], axis=0)[0:1, :][None], most.shape)
    copy = pltpu.make_async_copy(most, out_hbm.at[:, 45:46, :LANE], sem.at[0])
    copy.start()
    copy.wait()


def insert(parcels, tops):
    return pl.pallas_call(
        insert_kernel,
        in_specs=[HBM, VMEM],
        out_specs=HBM,
        out_shape=f32(8, 48, COLS),
        scratch_shapes=[pltpu.VMEM((8, 1, LANE), jnp.float32), pltpu.SemaphoreType.DMA((1,))],
        input_output_aliases={0: 0},
        compiler_params=pltpu.CompilerParams(vmem_limit_bytes=60 * 2**20),
        cost_estimate=pl.CostEstimate(flops=1000, bytes_accessed=100_000, transcendentals=0),
        name="insert_maximum",
    )(parcels, tops)


NEAR = ((0, 1, 0.5), (1, 0, 0.5), (1, 1, 0.125), (1, -1, 0.125))
PADDED = WIDE + LANE


def moved(x, rows, cols):
    if cols:
        x = pltpu.roll(x, (-cols) % x.shape[1], 1)
    if rows:
        x = pltpu.roll(x, (-rows) % x.shape[0], 0)
    return x


def solve_kernel(got_ref, out_ref, h_ref, resid_ref, direction_ref, answer_ref, weight):
    for ref in (h_ref, resid_ref):
        for row in (0, EXT - 1):
            ref[row : row + 1, :] = jnp.zeros((1, PADDED), jnp.float32)
        ref[:, WIDE:] = jnp.zeros((EXT, LANE), jnp.float32)
    for j in range(8):
        cols = pl.ds(j * COLS, COLS)
        resid_ref[1:23, cols] = got_ref[j, 0:22, :]
        h_ref[1:23, cols] = got_ref[j, 22:44, :]
    lane, tile = lanes((8, LANE)), sublanes((8, LANE))
    group, row = lanes((8, COLS)), sublanes((8, COLS))
    used = (row >= 1) & (row <= 6) & (group >= 32 * (row - 1)) & (group <= 32 * (row - 1) + LEVELS)
    for j in range(7):
        pairs = got_ref[j, 44:45, :] * pltpu.roll(got_ref[j + 1, 44:45, :], COLS - 16, 1)
        flux = jnp.sum(jnp.where(used, pairs, 0.0), axis=1, keepdims=True)
        for rows, there in ((pl.ds(0, 8), tile < 4), (pl.ds(16, 8), tile >= 4)):
            last = pl.ds((j + 1) * COLS - LANE, LANE)
            after = pl.ds((j + 1) * COLS, LANE)
            resid_ref[rows, last] = resid_ref[rows, last] - jnp.where(there & (lane == LANE - 1), flux, 0.0)
            resid_ref[rows, after] = resid_ref[rows, after] + jnp.where(there & (lane == 0), flux, 0.0)
    most = got_ref[0, 45:46, 0:1]
    for j in range(1, 8):
        most = jnp.maximum(most, got_ref[j, 45:46, 0:1])
    lam_max = 0.5 + 10.0 * most
    theta = (lam_max + 0.5) / 2.0
    delta = (lam_max - 0.5) / 2.0
    sigma = theta / delta
    h = h_ref[...]
    sides = {c: moved(h, 0, c) for c in (-1, 0, 1)}
    for n, (a, b, w) in enumerate(NEAR):
        weight[n] = w * (h + moved(sides[b], a, 0))
    direction_ref[...] = resid_ref[...] / theta
    answer_ref[...] = direction_ref[...]

    def step(_, rho):
        direction = direction_ref[...]
        east, west = moved(direction, 0, 1), moved(direction, 0, -1)
        right = weight[0] * (direction - east)
        down = weight[1] * (direction - moved(direction, 1, 0))
        right_down = weight[2] * (direction - moved(east, 1, 0))
        left_down = weight[3] * (direction - moved(west, 1, 0))
        applied = (0.5 * direction + (right - moved(right, 0, -1))) + ((down + right_down) + left_down)
        applied = applied - moved(down + (moved(right_down, 0, -1) + moved(left_down, 0, 1)), -1, 0)
        resid = jnp.where(h_ref[...] > 0.0, resid_ref[...] - applied, 0.0)
        resid_ref[...] = resid
        rho_next = 1.0 / (2.0 * sigma - rho)
        direction = rho_next * rho * direction + (2.0 * rho_next / delta) * resid
        direction_ref[...] = direction
        answer_ref[...] = answer_ref[...] + direction
        return rho_next

    lax.fori_loop(0, ITERS, step, 1.0 / sigma)
    out_ref[...] = answer_ref[4:20, :WIDE]


def solve(got):
    wide = pltpu.VMEM((EXT, PADDED), jnp.float32)
    return pl.pallas_call(
        solve_kernel,
        in_specs=[VMEM],
        out_specs=VMEM,
        out_shape=f32(16, WIDE),
        scratch_shapes=[wide, wide, wide, wide, pltpu.VMEM((4, EXT, PADDED), jnp.float32)],
        compiler_params=pltpu.CompilerParams(vmem_limit_bytes=60 * 2**20),
        cost_estimate=pl.CostEstimate(flops=6_000_000, bytes_accessed=600_000, transcendentals=0),
        name="chebyshev",
    )(got)


def exchange(x, axis, odd):
    count = lax.axis_size(axis)
    pairs = []
    for i in range(odd, count - 1, 2):
        pairs += [(i, i + 1), (i + 1, i)]
    return lax.ppermute(x, axis, pairs)


def shards(tracers, velocity, ocean, thickness, depth):
    row_even, row_odd, col_even, col_odd, top = pack(thickness, tracers, velocity, ocean, depth)
    halos = (exchange(row_even, "bx", 0), exchange(row_odd, "bx", 1), exchange(col_even, "by", 0), exchange(col_odd, "by", 1))
    tops = lax.all_to_all(top, "bx", split_axis=0, concat_axis=0, tiled=True)
    part, parcels = advect(0, tracers, velocity, ocean, *halos, depth)
    got = lax.all_to_all(insert(parcels, tops), "by", split_axis=0, concat_axis=0, tiled=True)
    new_tracers = advect(2, tracers, velocity, ocean, *halos, part)[0]
    return new_tracers, solve(got)


def solution(mesh):
    return jax.shard_map(
        shards,
        mesh=mesh,
        in_specs=(
            P(None, None, "bx", "by"),
            P(None, None, "bx", "by"),
            P("bx", "by"),
            P(),
            P("bx", "by"),
        ),
        out_specs=(P(None, None, "bx", "by"), P(("bx", "by"), None)),
        check_vma=False,
    )
```

```python
import functools

import jax
import jax.numpy as jnp
from jax import lax
from jax.experimental import pallas as pl
from jax.experimental.pallas import tpu as pltpu
from jax.sharding import PartitionSpec as P

ITERS = 3
TRACERS = 4
LEVELS = 12
ROWS = 128
COLS = 256
TILES = ROWS // 8
LANE = 128
WIDE = 8 * COLS
EXT = 24
CHUNK = 32
TALL = 16
LIMA, LIMB = 48, 48

SPEED, WET, THICK, PART, COEF, EDGE, MESSAGE = 48, 60, 61, 64, 68, 72, 80
ANY = pl.BlockSpec(memory_space=pl.ANY)
HBM = pl.BlockSpec(memory_space=pltpu.HBM)
VMEM = pl.BlockSpec(memory_space=pltpu.VMEM)


def f32(*shape):
    return jax.ShapeDtypeStruct(shape, jnp.float32)


def lanes(shape):
    return lax.broadcasted_iota(jnp.int32, shape, len(shape) - 1)


def sublanes(shape):
    return lax.broadcasted_iota(jnp.int32, shape, len(shape) - 2)


def coefficient(depth, wet):
    return depth * (0.1 + 0.9 * wet)


def positive(x):
    return jnp.maximum(x, 0.0)


def negative(x):
    return jnp.minimum(x, 0.0)


def edge_forcing(q, u, v, wet, thick):
    shape = (8, COLS)
    row, col = sublanes(shape), lanes(shape)
    total = jnp.zeros(shape, jnp.float32)
    flux_x = jnp.zeros(shape, jnp.float32)
    flux_y = jnp.zeros(shape, jnp.float32)
    for k in range(LEVELS):
        depth = thick[k]
        total = total + depth * q[k]
        flux_x = flux_x + depth * (positive(u[k]) * q[k] + negative(u[k]) * pltpu.roll(q[k], 7, 0))
        flux_y = flux_y + depth * (positive(v[k]) * q[k] + negative(v[k]) * pltpu.roll(q[k], COLS - 1, 1))
    flux_x = flux_x * jnp.where(row == 7, 0.0, wet * pltpu.roll(wet, 7, 0))
    flux_y = flux_y * jnp.where(col == COLS - 1, 0.0, wet * pltpu.roll(wet, COLS - 1, 1))
    return wet * (total - (flux_x - pltpu.roll(flux_x, 1, 0)) - (flux_y - pltpu.roll(flux_y, 1, 1)))


def edge_terms(q, v, wet, thick):
    lane = lanes((8, LANE))
    last, first = wet[:, LANE:], wet[:, :LANE]
    upwind = jnp.zeros((8, LANE), jnp.float32)
    terms = jnp.where(lane == 28, pltpu.roll(first, 28, 1), 0.0)
    for k in range(LEVELS):
        depth = thick[k]
        speed = v[k][:, LANE:]
        upwind = upwind + depth * positive(speed) * q[k][:, LANE:]
        terms = jnp.where(lane == k, pltpu.roll(depth * negative(speed) * last, k + 1, 1), terms)
        terms = jnp.where(lane == 16 + k, pltpu.roll(q[k][:, :LANE] * first, 16 + k, 1), terms)
    return jnp.where(lane == LEVELS, pltpu.roll(upwind * last, LEVELS + 1, 1), terms)


def pack_kernel(thick_hbm, t_hbm, v_hbm, ocean_hbm, depth_hbm, row_even, row_odd, col_even, col_odd, top,
                t_ref, u_top, u_low, v_top, v_low, v_last, ocean_ref, depth_ref, thick, row_both, col_both, sems):
    odd_x, odd_y = lax.axis_index("bx") % 2, lax.axis_index("by") % 2
    row_hi, row_lo = row_both.at[0], row_both.at[1]
    col_hi, col_lo = col_both.at[0], col_both.at[1]

    def chunk_copy(c):
        rows = pl.ds(pl.multiple_of(c * CHUNK, CHUNK), CHUNK)
        return pltpu.make_async_copy(t_hbm.at[:, :, rows, :], t_ref.at[:, :, rows, :], sems.at[c])

    chunks = ROWS // CHUNK
    small = [
        pltpu.make_async_copy(ocean_hbm, ocean_ref, sems.at[chunks]),
        pltpu.make_async_copy(depth_hbm, depth_ref, sems.at[chunks + 1]),
        pltpu.make_async_copy(v_hbm.at[1, :, :, LANE:], v_last, sems.at[chunks + 2]),
        pltpu.make_async_copy(thick_hbm, thick, sems.at[chunks + 7]),
    ]
    tiles = [
        pltpu.make_async_copy(v_hbm.at[0, :, 0:8, :], u_top, sems.at[chunks + 3]),
        pltpu.make_async_copy(v_hbm.at[0, :, ROWS - 8 :, :], u_low, sems.at[chunks + 4]),
        pltpu.make_async_copy(v_hbm.at[1, :, 0:8, :], v_top, sems.at[chunks + 5]),
        pltpu.make_async_copy(v_hbm.at[1, :, ROWS - 8 :, :], v_low, sems.at[chunks + 6]),
    ]
    for copy in small:
        copy.start()
    for c in range(chunks):
        chunk_copy(c).start()
    for copy in tiles:
        copy.start()
    for copy in small:
        copy.wait()
    wet = ocean_ref[...].astype(jnp.float32)
    coef = coefficient(depth_ref[...], wet)
    most = jnp.max(jnp.max(coef, axis=0, keepdims=True), axis=1, keepdims=True)
    top[...] = jnp.broadcast_to(most[None], top.shape)
    thick_lanes = jnp.zeros((1, COLS), jnp.float32)
    for k in range(LEVELS):
        thick_lanes = jnp.where(lanes((1, COLS)) == k, thick[k], thick_lanes)

    def gather(c, _):
        chunk_copy(c).wait()
        lane = lanes((CHUNK, LANE))
        rows = pl.ds(pl.multiple_of(c * CHUNK, CHUNK), CHUNK)
        ocean = ocean_ref[rows, :].astype(jnp.float32)
        hi = jnp.where(lane == 2 * WET, pltpu.roll(ocean[:, LANE:], (2 * WET + 1) % LANE, 1), 0.0)
        lo = jnp.where(lane == 2 * WET - 1, pltpu.roll(ocean[:, :LANE], 2 * WET - 1, 1), 0.0)
        for k in range(LEVELS):
            for t in range(TRACERS):
                s = t * LEVELS + k
                hi = jnp.where(lane == 2 * s, pltpu.roll(t_ref[t, k, rows, LANE:], 2 * s + 1, 1), hi)
                place = (2 * s - 1) % LANE
                lo = jnp.where(lane == place, pltpu.roll(t_ref[t, k, rows, :LANE], place, 1), lo)
            s = SPEED + k
            hi = jnp.where(lane == 2 * s, pltpu.roll(v_last[k, rows, :], 2 * s + 1, 1), hi)
        col_hi[rows, :] = hi
        col_lo[rows, :] = lo
        return 0

    lax.fori_loop(0, chunks, gather, 0)
    for copy in tiles:
        copy.wait()
    for t in range(TRACERS):
        for k in range(LEVELS):
            s = t * LEVELS + k
            row_hi[s : s + 1, :] = t_ref[t, k, ROWS - 1 : ROWS, :]
            row_lo[s : s + 1, :] = t_ref[t, k, 0:1, :]
    for k in range(LEVELS):
        row_hi[SPEED + k : SPEED + k + 1, :] = u_low[k, 7:8, :]
    row_lo[SPEED:WET, :] = jnp.zeros((WET - SPEED, COLS), jnp.float32)
    for row, message, u, v, keep in ((0, row_lo, u_top, v_top, 0), (ROWS - 8, row_hi, u_low, v_low, 4)):
        rows = slice(row, row + 8)
        here = ocean_ref[rows, :].astype(jnp.float32)
        q = [0.2 * t_ref[0, k, rows, :] - 0.8 * t_ref[1, k, rows, :] for k in range(LEVELS)]
        speed_x = [u[k] for k in range(LEVELS)]
        speed_y = [v[k] for k in range(LEVELS)]
        message[WET:THICK, :] = here[7:8, :] if keep else here[0:1, :]
        message[THICK:PART, :] = jnp.broadcast_to(thick_lanes, (PART - THICK, COLS))
        message[PART:COEF, :] = edge_forcing(q, speed_x, speed_y, here, thick)[keep : keep + 4, :]
        message[COEF:EDGE, :] = coefficient(depth_ref[rows, :], here)[keep : keep + 4, :]
        message[EDGE:MESSAGE, :LANE] = edge_terms(q, speed_y, here, thick)
        message[EDGE:MESSAGE, LANE:] = jnp.zeros((8, LANE), jnp.float32)
    row_even[...] = row_both[odd_x]
    row_odd[...] = row_both[1 - odd_x]
    col_even[...] = col_both[odd_y]
    col_odd[...] = col_both[1 - odd_y]


def pack(thickness, tracers, velocity, ocean, depth):
    tile = (LEVELS, 8, COLS)
    return pl.pallas_call(
        pack_kernel,
        in_specs=[HBM] * 5,
        out_specs=[VMEM] * 5,
        out_shape=[f32(MESSAGE, COLS), f32(MESSAGE, COLS), f32(ROWS, LANE), f32(ROWS, LANE), f32(16, 8, LANE)],
        scratch_shapes=[
            pltpu.VMEM((TRACERS, LEVELS, ROWS, COLS), jnp.float32),
            pltpu.VMEM(tile, jnp.float32),
            pltpu.VMEM(tile, jnp.float32),
            pltpu.VMEM(tile, jnp.float32),
            pltpu.VMEM(tile, jnp.float32),
            pltpu.VMEM((LEVELS, ROWS, LANE), jnp.float32),
            pltpu.VMEM((ROWS, COLS), jnp.int32),
            pltpu.VMEM((ROWS, COLS), jnp.float32),
            pltpu.SMEM((LEVELS,), jnp.float32),
            pltpu.VMEM((2, MESSAGE, COLS), jnp.float32),
            pltpu.VMEM((2, ROWS, LANE), jnp.float32),
            pltpu.SemaphoreType.DMA((ROWS // CHUNK + 8,)),
        ],
        compiler_params=pltpu.CompilerParams(vmem_limit_bytes=60 * 2**20),
        cost_estimate=pl.CostEstimate(flops=4_000_000, bytes_accessed=7_400_000, transcendentals=0),
        name="pack_edges",
    )(thickness, tracers, velocity, ocean, depth)


def ahead_y(x, edge):
    last = lanes((x.shape[0], LANE)) == LANE - 1
    a, b = pltpu.roll(x[:, :LANE], LANE - 1, 1), pltpu.roll(x[:, LANE:], LANE - 1, 1)
    return jnp.concatenate([jnp.where(last, b, a), jnp.where(last, edge, b)], 1)


def behind_y(x, edge):
    first = lanes((x.shape[0], LANE)) == 0
    a, b = pltpu.roll(x[:, :LANE], 1, 1), pltpu.roll(x[:, LANE:], 1, 1)
    return jnp.concatenate([jnp.where(first, edge, a), jnp.where(first, a, b)], 1)


def above(load, edge, r, tall=8):
    if (r + 1) * tall < ROWS:
        return load(tall * r + 1)
    return jnp.where(sublanes((tall, COLS)) == tall - 1, edge, pltpu.roll(load(tall * r), tall - 1, 0))


def upwind(speed, here, ahead):
    return speed * jnp.where(speed > 0.0, here, ahead)


def advect_kernel(first, *refs):
    if first == 0:
        (t_hbm, v_hbm, ocean_hbm, row_even, row_odd, col_even, col_odd, depth_hbm, out_hbm, send_ref,
         t_ref, v_ref, out_ref, ocean_ref, rows_in, cols_in, w_x, w_y, before_y, edges, sems, small_sems,
         depth_ref, total, flux, ext, thick) = refs
    else:
        (t_hbm, v_hbm, ocean_hbm, row_even, row_odd, col_even, col_odd, _, out_hbm,
         t_ref, v_ref, out_ref, ocean_ref, rows_in, cols_in, w_x, w_y, before_y, edges, sems, small_sems) = refs
    odd_x, odd_y = lax.axis_index("bx") % 2, lax.axis_index("by") % 2
    row_lo, row_hi = rows_in.at[0], rows_in.at[1]
    small = [
        (ocean_hbm, ocean_ref),
        (row_even, rows_in.at[1 - odd_x]),
        (row_odd, rows_in.at[odd_x]),
        (col_even, cols_in.at[1 - odd_y]),
        (col_odd, cols_in.at[odd_y]),
    ]
    if first == 0:
        small += [(depth_hbm, depth_ref)]
    small = [pltpu.make_async_copy(a, b, small_sems.at[i]) for i, (a, b) in enumerate(small)]

    def tracers_in(k):
        return pltpu.make_async_copy(t_hbm.at[first : first + 2, k], t_ref.at[k], sems.at[0, k])

    def velocity_in(k):
        return pltpu.make_async_copy(v_hbm.at[:, k], v_ref.at[k], sems.at[1, k])

    def tracers_out(k):
        return pltpu.make_async_copy(out_ref.at[k], out_hbm.at[first : first + 2, k], sems.at[2, k])

    for copy in small:
        copy.start()
    for k in range(LEVELS):
        tracers_in(k).start()
        velocity_in(k).start()
    for copy in small:
        copy.wait()
    even = lanes((8, LANE)) % 2 == 0
    load_wet = lambda at: ocean_ref[at : at + 8, :].astype(jnp.float32)
    for r in range(TILES):
        rows = pl.ds(8 * r, 8)
        edge = jnp.where(even, cols_in[0, rows, :], cols_in[1, rows, :])
        for k in range(LEVELS):
            for i, slot in enumerate((first * LEVELS + k, (first + 1) * LEVELS + k, SPEED + k)):
                edges[k, i, rows, :] = pltpu.roll(edge, (LANE - 2 * slot) % LANE, 1)
        here = load_wet(8 * r)
        wet_edge = pltpu.roll(edge, LANE - 2 * WET, 1)
        w_x[rows, :] = here * above(load_wet, row_hi[WET : WET + 1, :], r)
        w_y[rows, :] = here * ahead_y(here, wet_edge)
        before_y[rows, :] = here[:, :LANE] * wet_edge
        if first == 0:
            total[rows, :] = jnp.zeros((8, COLS), jnp.float32)
    w_before = load_wet(0)[0:1, :] * row_lo[WET : WET + 1, :]
    if first == 0:
        flux[...] = jnp.zeros((8, COLS), jnp.float32)
        line = rows_in[1 - odd_x, THICK : THICK + 1, :]
        for k in range(LEVELS):
            thick[k : k + 1, :] = jnp.broadcast_to(line[:, k : k + 1], (1, COLS))

    def level(k, _):
        tracers_in(k).wait()
        velocity_in(k).wait()
        u_before = row_lo[pl.ds(SPEED + k, 1), :] * w_before
        into_x = [upwind(u_before, row_lo[pl.ds((first + t) * LEVELS + k, 1), :], t_ref[k, t, 0:1, :]) for t in range(2)]
        carry, out_x = list(into_x), [None, None]
        if first == 0:
            depth = thick[pl.ds(k, 1), :]
        for r in range(ROWS // TALL):
            rows = pl.ds(TALL * r, TALL)
            u = v_ref[k, 0, rows, :] * w_x[rows, :]
            v = v_ref[k, 1, rows, :] * w_y[rows, :]
            v_before = edges[k, 2, rows, :] * before_y[rows, :]
            new = []
            for t in range(2):
                load = lambda at: t_ref[k, t, at : at + TALL, :]
                slot = (first + t) * LEVELS + k
                c = load(TALL * r)
                c_edge = edges[k, t, rows, :]
                here_x = upwind(u, c, above(load, row_hi[pl.ds(slot, 1), :], r, TALL))
                turned = pltpu.roll(here_x, 1, 0)
                past_x = jnp.where(sublanes((TALL, COLS)) == 0, carry[t], turned)
                carry[t] = turned[0:1, :]
                if r == ROWS // TALL - 1:
                    out_x[t] = here_x[TALL - 1 :, :]
                here_y = upwind(v, c, ahead_y(c, c_edge))
                past_y = behind_y(here_y, upwind(v_before, c_edge, c[:, :LANE]))
                value = (c - (here_x - past_x)) - (here_y - past_y)
                out_ref[k, t, rows, :] = value
                new.append(value)
            if first == 0:
                total[rows, :] = total[rows, :] + depth * (0.2 * new[0] - 0.8 * new[1])
        if first == 0:
            flux[0:1, :] = flux[0:1, :] + depth * (0.2 * into_x[0] - 0.8 * into_x[1])
            flux[1:2, :] = flux[1:2, :] + depth * (0.2 * out_x[0] - 0.8 * out_x[1])
        tracers_out(k).start()
        return 0

    lax.fori_loop(0, LEVELS, level, 0)

    if first == 0:
        row = sublanes((4, COLS))
        ext[0, 0:4, :] = row_lo[PART:COEF, :] - jnp.where(row == 3, flux[0:1, :], 0.0)
        ext[0, ROWS + 4 :, :] = row_hi[PART:COEF, :] + jnp.where(row == 0, flux[1:2, :], 0.0)
        ext[1, 0:4, :] = row_lo[COEF:EDGE, :]
        ext[1, ROWS + 4 :, :] = row_hi[COEF:EDGE, :]
        for r in range(TILES):
            rows = pl.ds(8 * r, 8)
            here = load_wet(8 * r)
            ext[0, 8 * r + 4 : 8 * r + 12, :] = total[rows, :] * here
            ext[1, 8 * r + 4 : 8 * r + 12, :] = coefficient(depth_ref[rows, :], here)
        for j in range(8):
            at = 16 * j
            send_ref[j, 0:22, :] = ext[0, at + 1 : at + 23, :]
            send_ref[j, 22:44, :] = ext[1, at + 1 : at + 23, :]
            line = jnp.zeros((1, LANE), jnp.float32)
            halves = [line, line]
            if j in (0, 7):
                for i in range(3):
                    factors = row_lo[EDGE + 5 + i : EDGE + 6 + i, :LANE] if j == 0 else row_hi[EDGE + i : EDGE + 1 + i, :LANE]
                    at = 32 * (i if j == 0 else 3 + i)
                    halves[at // LANE] = halves[at // LANE] + (pltpu.roll(factors, at % LANE, 1) if at % LANE else factors)
            send_ref[j, 44:45, :] = jnp.concatenate(halves, 1)
            send_ref[j, 45:48, :] = jnp.zeros((3, COLS), jnp.float32)
    for k in range(LEVELS):
        tracers_out(k).wait()


def advect(first, tracers, velocity, ocean, row_even, row_odd, col_even, col_odd, extra):
    ins = [HBM] * 3 + [ANY] * 4
    operands = [tracers, velocity, ocean, row_even, row_odd, col_even, col_odd]
    out_specs = [HBM]
    out_shape = [f32(TRACERS, LEVELS, ROWS, COLS)]
    block = pltpu.VMEM((ROWS, COLS), jnp.float32)
    narrow = pltpu.VMEM((ROWS, LANE), jnp.float32)
    scratch = [
        pltpu.VMEM((LEVELS, 2, ROWS, COLS), jnp.float32),
        pltpu.VMEM((LEVELS, 2, ROWS, COLS), jnp.float32),
        pltpu.VMEM((LEVELS, 2, ROWS, COLS), jnp.float32),
        pltpu.VMEM((ROWS, COLS), jnp.int32),
        pltpu.VMEM((2, MESSAGE, COLS), jnp.float32),
        pltpu.VMEM((2, ROWS, LANE), jnp.float32),
        block,
        block,
        narrow,
        pltpu.VMEM((LEVELS, 3, ROWS, LANE), jnp.float32),
        pltpu.SemaphoreType.DMA((3, LEVELS)),
        pltpu.SemaphoreType.DMA((8,)),
    ]
    aliases = {}
    if first == 0:
        ins = ins + [HBM]
        operands = operands + [extra]
        out_specs.append(VMEM)
        out_shape.append(f32(8, 48, COLS))
        scratch += [
            block,
            block,
            pltpu.VMEM((8, COLS), jnp.float32),
            pltpu.VMEM((2, ROWS + 8, COLS), jnp.float32),
            pltpu.VMEM((16, COLS), jnp.float32),
        ]
    else:
        aliases = {len(operands): 0}
        ins = ins + [HBM]
        operands = operands + [extra]
    return pl.pallas_call(
        functools.partial(advect_kernel, first),
        in_specs=ins,
        out_specs=out_specs,
        out_shape=out_shape,
        scratch_shapes=scratch,
        input_output_aliases=aliases,
        compiler_params=pltpu.CompilerParams(vmem_limit_bytes=(LIMA if first == 0 else LIMB) * 2**20),
        cost_estimate=pl.CostEstimate(flops=24_000_000, bytes_accessed=9_400_000, transcendentals=0),
        name="advect_forcing" if first == 0 else "advect_rest",
    )(*operands)


def insert_kernel(_, tops, out_hbm, most, sem):
    most[...] = jnp.broadcast_to(jnp.max(tops[...], axis=0)[0:1, :][None], most.shape)
    copy = pltpu.make_async_copy(most, out_hbm.at[:, 45:46, :LANE], sem.at[0])
    copy.start()
    copy.wait()


def insert(parcels, tops):
    return pl.pallas_call(
        insert_kernel,
        in_specs=[HBM, VMEM],
        out_specs=HBM,
        out_shape=f32(8, 48, COLS),
        scratch_shapes=[pltpu.VMEM((8, 1, LANE), jnp.float32), pltpu.SemaphoreType.DMA((1,))],
        input_output_aliases={0: 0},
        compiler_params=pltpu.CompilerParams(vmem_limit_bytes=60 * 2**20),
        cost_estimate=pl.CostEstimate(flops=1000, bytes_accessed=100_000, transcendentals=0),
        name="insert_maximum",
    )(parcels, tops)


NEAR = ((1, 0, 0.5), (-1, 0, 0.5), (0, 1, 0.5), (0, -1, 0.5), (1, 1, 0.125), (1, -1, 0.125), (-1, 1, 0.125), (-1, -1, 0.125))
PADDED = WIDE + LANE


def solve_kernel(got_ref, out_ref, h_ref, resid_ref, answer_ref, weight, buffers):
    here = slice(8, 8 + EXT)

    def spread():
        field = buffers[0, here, :]
        buffers[1, here, :] = pltpu.roll(field, PADDED - 1, 1)
        buffers[2, here, :] = pltpu.roll(field, 1, 1)

    def near(rows, cols, block):
        return buffers[{0: 0, 1: 1, -1: 2}[cols], 8 + rows : 8 + rows + EXT, block]

    def block_at(c):
        return pl.ds(c * COLS, COLS)

    for n in range(3):
        for rows in (slice(0, 16), slice(EXT, 16 + EXT)):
            buffers[n, rows, :] = jnp.zeros((16, PADDED), jnp.float32)
    buffers[0, 16:EXT, WIDE:] = jnp.zeros((EXT - 16, LANE), jnp.float32)
    for row in (0, EXT - 1):
        resid_ref[row : row + 1, :] = jnp.zeros((1, WIDE), jnp.float32)
    for j in range(8):
        cols = pl.ds(j * COLS, COLS)
        resid_ref[1:23, cols] = got_ref[j, 0:22, :]
        buffers[0, 9:31, cols] = got_ref[j, 22:44, :]
    lane, tile = lanes((8, LANE)), sublanes((8, LANE))
    group, row = lanes((8, COLS)), sublanes((8, COLS))
    used = (row >= 1) & (row <= 6) & (group >= 32 * (row - 1)) & (group <= 32 * (row - 1) + LEVELS)
    for j in range(7):
        pairs = got_ref[j, 44:45, :] * pltpu.roll(got_ref[j + 1, 44:45, :], COLS - 16, 1)
        flux = jnp.sum(jnp.where(used, pairs, 0.0), axis=1, keepdims=True)
        for rows, there in ((pl.ds(0, 8), tile < 4), (pl.ds(16, 8), tile >= 4)):
            last = pl.ds((j + 1) * COLS - LANE, LANE)
            after = pl.ds((j + 1) * COLS, LANE)
            resid_ref[rows, last] = resid_ref[rows, last] - jnp.where(there & (lane == LANE - 1), flux, 0.0)
            resid_ref[rows, after] = resid_ref[rows, after] + jnp.where(there & (lane == 0), flux, 0.0)
    most = got_ref[0, 45:46, 0:1]
    for j in range(1, 8):
        most = jnp.maximum(most, got_ref[j, 45:46, 0:1])
    lam_max = 0.5 + 10.0 * most
    theta = (lam_max + 0.5) / 2.0
    delta = (lam_max - 0.5) / 2.0
    sigma = theta / delta
    spread()

    def weigh(c, _):
        block = block_at(c)
        h = near(0, 0, block)
        h_ref[:, block] = h
        for n, (a, b, w) in enumerate(NEAR):
            weight[n, :, block] = w * (h + near(a, b, block))
        return 0

    for c in range(WIDE // COLS):
        weigh(c, 0)
    direction = resid_ref[...] / theta
    buffers[0, here, :WIDE] = direction
    answer_ref[...] = direction

    def step(_, rho):
        spread()
        rho_next = 1.0 / (2.0 * sigma - rho)
        keep, add = rho_next * rho, 2.0 * rho_next / delta

        def update(c, _):
            block = block_at(c)
            direction = near(0, 0, block)
            applied = 0.5 * direction
            for n, (a, b, _) in enumerate(NEAR):
                applied = applied + weight[n, :, block] * (direction - near(a, b, block))
            resid = jnp.where(h_ref[:, block] > 0.0, resid_ref[:, block] - applied, 0.0)
            resid_ref[:, block] = resid
            direction = keep * direction + add * resid
            buffers[0, here, block] = direction
            answer_ref[:, block] = answer_ref[:, block] + direction
            return 0

        for c in range(WIDE // COLS):
            update(c, 0)
        return rho_next

    lax.fori_loop(0, ITERS, step, 1.0 / sigma)
    out_ref[...] = answer_ref[4:20, :]


def solve(got):
    wide = pltpu.VMEM((EXT, WIDE), jnp.float32)
    return pl.pallas_call(
        solve_kernel,
        in_specs=[VMEM],
        out_specs=VMEM,
        out_shape=f32(16, WIDE),
        scratch_shapes=[
            wide,
            wide,
            wide,
            pltpu.VMEM((8, EXT, WIDE), jnp.float32),
            pltpu.VMEM((3, EXT + 16, PADDED), jnp.float32),
        ],
        compiler_params=pltpu.CompilerParams(vmem_limit_bytes=60 * 2**20),
        cost_estimate=pl.CostEstimate(flops=6_000_000, bytes_accessed=600_000, transcendentals=0),
        name="chebyshev",
    )(got)


def exchange(x, axis, odd):
    count = lax.axis_size(axis)
    pairs = []
    for i in range(odd, count - 1, 2):
        pairs += [(i, i + 1), (i + 1, i)]
    return lax.ppermute(x, axis, pairs)


def shards(tracers, velocity, ocean, thickness, depth):
    row_even, row_odd, col_even, col_odd, top = pack(thickness, tracers, velocity, ocean, depth)
    from_row_odd, from_col_odd = exchange(row_odd, "bx", 1), exchange(col_odd, "by", 1)
    halos = (exchange(row_even, "bx", 0), from_row_odd, exchange(col_even, "by", 0), from_col_odd)
    tops = lax.all_to_all(top, "bx", split_axis=0, concat_axis=0, tiled=True)
    part, parcels = advect(0, tracers, velocity, ocean, *halos, depth)
    got = lax.all_to_all(insert(parcels, tops), "by", split_axis=0, concat_axis=0, tiled=True)
    new_tracers = advect(2, tracers, velocity, ocean, *halos, part)[0]
    return new_tracers, solve(got)


def solution(mesh):
    return jax.shard_map(
        shards,
        mesh=mesh,
        in_specs=(
            P(None, None, "bx", "by"),
            P(None, None, "bx", "by"),
            P("bx", "by"),
            P(),
            P("bx", "by"),
        ),
        out_specs=(P(None, None, "bx", "by"), P(("bx", "by"), None)),
        check_vma=False,
    )
```

```python
import functools

import jax
import jax.numpy as jnp
from jax import lax
from jax.experimental import pallas as pl
from jax.experimental.pallas import tpu as pltpu
from jax.sharding import PartitionSpec as P

ITERS = 3
TRACERS = 4
LEVELS = 12
ROWS = 128
COLS = 256
TILES = ROWS // 8
LANE = 128
WIDE = 8 * COLS
EXT = 24
CHUNK = 32
TALL = 16
LIMA, LIMB = 48, 48

SPEED, WET, THICK, PART, COEF, EDGE, MESSAGE = 48, 60, 61, 64, 68, 72, 80
ANY = pl.BlockSpec(memory_space=pl.ANY)
HBM = pl.BlockSpec(memory_space=pltpu.HBM)
VMEM = pl.BlockSpec(memory_space=pltpu.VMEM)


def f32(*shape):
    return jax.ShapeDtypeStruct(shape, jnp.float32)


def lanes(shape):
    return lax.broadcasted_iota(jnp.int32, shape, len(shape) - 1)


def sublanes(shape):
    return lax.broadcasted_iota(jnp.int32, shape, len(shape) - 2)


def coefficient(depth, wet):
    return depth * (0.1 + 0.9 * wet)


def positive(x):
    return jnp.maximum(x, 0.0)


def negative(x):
    return jnp.minimum(x, 0.0)


def edge_forcing(q, u, v, wet, thick):
    shape = (8, COLS)
    row, col = sublanes(shape), lanes(shape)
    total = jnp.zeros(shape, jnp.float32)
    flux_x = jnp.zeros(shape, jnp.float32)
    flux_y = jnp.zeros(shape, jnp.float32)
    for k in range(LEVELS):
        depth = thick[k]
        total = total + depth * q[k]
        flux_x = flux_x + depth * (positive(u[k]) * q[k] + negative(u[k]) * pltpu.roll(q[k], 7, 0))
        flux_y = flux_y + depth * (positive(v[k]) * q[k] + negative(v[k]) * pltpu.roll(q[k], COLS - 1, 1))
    flux_x = flux_x * jnp.where(row == 7, 0.0, wet * pltpu.roll(wet, 7, 0))
    flux_y = flux_y * jnp.where(col == COLS - 1, 0.0, wet * pltpu.roll(wet, COLS - 1, 1))
    return wet * (total - (flux_x - pltpu.roll(flux_x, 1, 0)) - (flux_y - pltpu.roll(flux_y, 1, 1)))


def edge_terms(q, v, wet, thick):
    lane = lanes((8, LANE))
    last, first = wet[:, LANE:], wet[:, :LANE]
    upwind = jnp.zeros((8, LANE), jnp.float32)
    terms = jnp.where(lane == 28, pltpu.roll(first, 28, 1), 0.0)
    for k in range(LEVELS):
        depth = thick[k]
        speed = v[k][:, LANE:]
        upwind = upwind + depth * positive(speed) * q[k][:, LANE:]
        terms = jnp.where(lane == k, pltpu.roll(depth * negative(speed) * last, k + 1, 1), terms)
        terms = jnp.where(lane == 16 + k, pltpu.roll(q[k][:, :LANE] * first, 16 + k, 1), terms)
    return jnp.where(lane == LEVELS, pltpu.roll(upwind * last, LEVELS + 1, 1), terms)


def pack_kernel(thick_hbm, t_hbm, v_hbm, ocean_hbm, depth_hbm, row_odd, col_odd, row_even, col_even, top,
                t_ref, u_top, u_low, v_top, v_low, v_last, ocean_ref, depth_ref, thick, row_both, col_both, sems):
    odd_x, odd_y = lax.axis_index("bx") % 2, lax.axis_index("by") % 2
    row_hi, row_lo = row_both.at[0], row_both.at[1]
    col_hi, col_lo = col_both.at[0], col_both.at[1]

    def chunk_copy(c):
        rows = pl.ds(pl.multiple_of(c * CHUNK, CHUNK), CHUNK)
        return pltpu.make_async_copy(t_hbm.at[:, :, rows, :], t_ref.at[:, :, rows, :], sems.at[c])

    chunks = ROWS // CHUNK
    small = [
        pltpu.make_async_copy(ocean_hbm, ocean_ref, sems.at[chunks]),
        pltpu.make_async_copy(depth_hbm, depth_ref, sems.at[chunks + 1]),
        pltpu.make_async_copy(v_hbm.at[1, :, :, LANE:], v_last, sems.at[chunks + 2]),
        pltpu.make_async_copy(thick_hbm, thick, sems.at[chunks + 7]),
    ]
    tiles = [
        pltpu.make_async_copy(v_hbm.at[0, :, 0:8, :], u_top, sems.at[chunks + 3]),
        pltpu.make_async_copy(v_hbm.at[0, :, ROWS - 8 :, :], u_low, sems.at[chunks + 4]),
        pltpu.make_async_copy(v_hbm.at[1, :, 0:8, :], v_top, sems.at[chunks + 5]),
        pltpu.make_async_copy(v_hbm.at[1, :, ROWS - 8 :, :], v_low, sems.at[chunks + 6]),
    ]
    for copy in small:
        copy.start()
    for c in range(chunks):
        chunk_copy(c).start()
    for copy in tiles:
        copy.start()
    for copy in small:
        copy.wait()
    wet = ocean_ref[...].astype(jnp.float32)
    coef = coefficient(depth_ref[...], wet)
    most = jnp.max(jnp.max(coef, axis=0, keepdims=True), axis=1, keepdims=True)
    top[...] = jnp.broadcast_to(most[None], top.shape)
    thick_lanes = jnp.zeros((1, COLS), jnp.float32)
    for k in range(LEVELS):
        thick_lanes = jnp.where(lanes((1, COLS)) == k, thick[k], thick_lanes)

    def gather(c, _):
        chunk_copy(c).wait()
        lane = lanes((CHUNK, LANE))
        rows = pl.ds(pl.multiple_of(c * CHUNK, CHUNK), CHUNK)
        ocean = ocean_ref[rows, :].astype(jnp.float32)
        hi = jnp.where(lane == 2 * WET, pltpu.roll(ocean[:, LANE:], (2 * WET + 1) % LANE, 1), 0.0)
        lo = jnp.where(lane == 2 * WET - 1, pltpu.roll(ocean[:, :LANE], 2 * WET - 1, 1), 0.0)
        for k in range(LEVELS):
            for t in range(TRACERS):
                s = t * LEVELS + k
                hi = jnp.where(lane == 2 * s, pltpu.roll(t_ref[t, k, rows, LANE:], 2 * s + 1, 1), hi)
                place = (2 * s - 1) % LANE
                lo = jnp.where(lane == place, pltpu.roll(t_ref[t, k, rows, :LANE], place, 1), lo)
            s = SPEED + k
            hi = jnp.where(lane == 2 * s, pltpu.roll(v_last[k, rows, :], 2 * s + 1, 1), hi)
        col_hi[rows, :] = hi
        col_lo[rows, :] = lo
        return 0

    lax.fori_loop(0, chunks, gather, 0)
    for copy in tiles:
        copy.wait()
    for t in range(TRACERS):
        for k in range(LEVELS):
            s = t * LEVELS + k
            row_hi[s : s + 1, :] = t_ref[t, k, ROWS - 1 : ROWS, :]
            row_lo[s : s + 1, :] = t_ref[t, k, 0:1, :]
    for k in range(LEVELS):
        row_hi[SPEED + k : SPEED + k + 1, :] = u_low[k, 7:8, :]
    row_lo[SPEED:WET, :] = jnp.zeros((WET - SPEED, COLS), jnp.float32)
    for row, message, u, v, keep in ((0, row_lo, u_top, v_top, 0), (ROWS - 8, row_hi, u_low, v_low, 4)):
        rows = slice(row, row + 8)
        here = ocean_ref[rows, :].astype(jnp.float32)
        q = [0.2 * t_ref[0, k, rows, :] - 0.8 * t_ref[1, k, rows, :] for k in range(LEVELS)]
        speed_x = [u[k] for k in range(LEVELS)]
        speed_y = [v[k] for k in range(LEVELS)]
        message[WET:THICK, :] = here[7:8, :] if keep else here[0:1, :]
        message[THICK:PART, :] = jnp.broadcast_to(thick_lanes, (PART - THICK, COLS))
        message[PART:COEF, :] = edge_forcing(q, speed_x, speed_y, here, thick)[keep : keep + 4, :]
        message[COEF:EDGE, :] = coefficient(depth_ref[rows, :], here)[keep : keep + 4, :]
        message[EDGE:MESSAGE, :LANE] = edge_terms(q, speed_y, here, thick)
        message[EDGE:MESSAGE, LANE:] = jnp.zeros((8, LANE), jnp.float32)
    row_even[...] = row_both[odd_x]
    row_odd[...] = row_both[1 - odd_x]
    col_even[...] = col_both[odd_y]
    col_odd[...] = col_both[1 - odd_y]


def pack(thickness, tracers, velocity, ocean, depth):
    tile = (LEVELS, 8, COLS)
    return pl.pallas_call(
        pack_kernel,
        in_specs=[HBM] * 5,
        out_specs=[VMEM] * 5,
        out_shape=[f32(MESSAGE, COLS), f32(ROWS, LANE), f32(MESSAGE, COLS), f32(ROWS, LANE), f32(16, 8, LANE)],
        scratch_shapes=[
            pltpu.VMEM((TRACERS, LEVELS, ROWS, COLS), jnp.float32),
            pltpu.VMEM(tile, jnp.float32),
            pltpu.VMEM(tile, jnp.float32),
            pltpu.VMEM(tile, jnp.float32),
            pltpu.VMEM(tile, jnp.float32),
            pltpu.VMEM((LEVELS, ROWS, LANE), jnp.float32),
            pltpu.VMEM((ROWS, COLS), jnp.int32),
            pltpu.VMEM((ROWS, COLS), jnp.float32),
            pltpu.SMEM((LEVELS,), jnp.float32),
            pltpu.VMEM((2, MESSAGE, COLS), jnp.float32),
            pltpu.VMEM((2, ROWS, LANE), jnp.float32),
            pltpu.SemaphoreType.DMA((ROWS // CHUNK + 8,)),
        ],
        compiler_params=pltpu.CompilerParams(vmem_limit_bytes=60 * 2**20),
        cost_estimate=pl.CostEstimate(flops=4_000_000, bytes_accessed=7_400_000, transcendentals=0),
        name="pack_edges",
    )(thickness, tracers, velocity, ocean, depth)


def ahead_y(x, edge):
    last = lanes((x.shape[0], LANE)) == LANE - 1
    a, b = pltpu.roll(x[:, :LANE], LANE - 1, 1), pltpu.roll(x[:, LANE:], LANE - 1, 1)
    return jnp.concatenate([jnp.where(last, b, a), jnp.where(last, edge, b)], 1)


def behind_y(x, edge):
    first = lanes((x.shape[0], LANE)) == 0
    a, b = pltpu.roll(x[:, :LANE], 1, 1), pltpu.roll(x[:, LANE:], 1, 1)
    return jnp.concatenate([jnp.where(first, edge, a), jnp.where(first, a, b)], 1)


def above(load, edge, r, tall=8):
    if (r + 1) * tall < ROWS:
        return load(tall * r + 1)
    return jnp.where(sublanes((tall, COLS)) == tall - 1, edge, pltpu.roll(load(tall * r), tall - 1, 0))


def upwind(speed, here, ahead):
    return speed * jnp.where(speed > 0.0, here, ahead)


def advect_kernel(first, *refs):
    if first == 0:
        (t_hbm, v_hbm, ocean_hbm, row_odd, col_odd, row_even, col_even, depth_hbm, out_hbm, send_ref,
         t_ref, v_ref, out_ref, ocean_ref, rows_in, cols_in, w_x, w_y, before_y, edges, sems, small_sems,
         depth_ref, total, flux, ext, thick) = refs
    else:
        (t_hbm, v_hbm, ocean_hbm, row_odd, col_odd, row_even, col_even, _, out_hbm,
         t_ref, v_ref, out_ref, ocean_ref, rows_in, cols_in, w_x, w_y, before_y, edges, sems, small_sems) = refs
    odd_x, odd_y = lax.axis_index("bx") % 2, lax.axis_index("by") % 2
    row_lo, row_hi = rows_in.at[0], rows_in.at[1]
    small = [
        (ocean_hbm, ocean_ref),
        (row_even, rows_in.at[1 - odd_x]),
        (row_odd, rows_in.at[odd_x]),
        (col_even, cols_in.at[1 - odd_y]),
        (col_odd, cols_in.at[odd_y]),
    ]
    if first == 0:
        small += [(depth_hbm, depth_ref)]
    small = [pltpu.make_async_copy(a, b, small_sems.at[i]) for i, (a, b) in enumerate(small)]

    def tracers_in(k):
        return pltpu.make_async_copy(t_hbm.at[first : first + 2, k], t_ref.at[k], sems.at[0, k])

    def velocity_in(k):
        return pltpu.make_async_copy(v_hbm.at[:, k], v_ref.at[k], sems.at[1, k])

    def tracers_out(k):
        return pltpu.make_async_copy(out_ref.at[k], out_hbm.at[first : first + 2, k], sems.at[2, k])

    for copy in small:
        copy.start()
    for k in range(LEVELS):
        tracers_in(k).start()
        velocity_in(k).start()
    for copy in small:
        copy.wait()
    even = lanes((8, LANE)) % 2 == 0
    load_wet = lambda at: ocean_ref[at : at + 8, :].astype(jnp.float32)
    for r in range(TILES):
        rows = pl.ds(8 * r, 8)
        edge = jnp.where(even, cols_in[0, rows, :], cols_in[1, rows, :])
        for k in range(LEVELS):
            for i, slot in enumerate((first * LEVELS + k, (first + 1) * LEVELS + k, SPEED + k)):
                edges[k, i, rows, :] = pltpu.roll(edge, (LANE - 2 * slot) % LANE, 1)
        here = load_wet(8 * r)
        wet_edge = pltpu.roll(edge, LANE - 2 * WET, 1)
        w_x[rows, :] = here * above(load_wet, row_hi[WET : WET + 1, :], r)
        w_y[rows, :] = here * ahead_y(here, wet_edge)
        before_y[rows, :] = here[:, :LANE] * wet_edge
        if first == 0:
            total[rows, :] = jnp.zeros((8, COLS), jnp.float32)
    w_before = load_wet(0)[0:1, :] * row_lo[WET : WET + 1, :]
    if first == 0:
        flux[...] = jnp.zeros((8, COLS), jnp.float32)
        line = rows_in[1 - odd_x, THICK : THICK + 1, :]
        for k in range(LEVELS):
            thick[k : k + 1, :] = jnp.broadcast_to(line[:, k : k + 1], (1, COLS))

    def level(k, _):
        tracers_in(k).wait()
        velocity_in(k).wait()
        u_before = row_lo[pl.ds(SPEED + k, 1), :] * w_before
        into_x = [upwind(u_before, row_lo[pl.ds((first + t) * LEVELS + k, 1), :], t_ref[k, t, 0:1, :]) for t in range(2)]
        carry, out_x = list(into_x), [None, None]
        if first == 0:
            depth = thick[pl.ds(k, 1), :]
        for r in range(ROWS // TALL):
            rows = pl.ds(TALL * r, TALL)
            u = v_ref[k, 0, rows, :] * w_x[rows, :]
            v = v_ref[k, 1, rows, :] * w_y[rows, :]
            v_before = edges[k, 2, rows, :] * before_y[rows, :]
            new = []
            for t in range(2):
                load = lambda at: t_ref[k, t, at : at + TALL, :]
                slot = (first + t) * LEVELS + k
                c = load(TALL * r)
                c_edge = edges[k, t, rows, :]
                here_x = upwind(u, c, above(load, row_hi[pl.ds(slot, 1), :], r, TALL))
                turned = pltpu.roll(here_x, 1, 0)
                past_x = jnp.where(sublanes((TALL, COLS)) == 0, carry[t], turned)
                carry[t] = turned[0:1, :]
                if r == ROWS // TALL - 1:
                    out_x[t] = here_x[TALL - 1 :, :]
                here_y = upwind(v, c, ahead_y(c, c_edge))
                past_y = behind_y(here_y, upwind(v_before, c_edge, c[:, :LANE]))
                value = (c - (here_x - past_x)) - (here_y - past_y)
                out_ref[k, t, rows, :] = value
                new.append(value)
            if first == 0:
                total[rows, :] = total[rows, :] + depth * (0.2 * new[0] - 0.8 * new[1])
        if first == 0:
            flux[0:1, :] = flux[0:1, :] + depth * (0.2 * into_x[0] - 0.8 * into_x[1])
            flux[1:2, :] = flux[1:2, :] + depth * (0.2 * out_x[0] - 0.8 * out_x[1])
        tracers_out(k).start()
        return 0

    lax.fori_loop(0, LEVELS, level, 0)

    if first == 0:
        row = sublanes((4, COLS))
        ext[0, 0:4, :] = row_lo[PART:COEF, :] - jnp.where(row == 3, flux[0:1, :], 0.0)
        ext[0, ROWS + 4 :, :] = row_hi[PART:COEF, :] + jnp.where(row == 0, flux[1:2, :], 0.0)
        ext[1, 0:4, :] = row_lo[COEF:EDGE, :]
        ext[1, ROWS + 4 :, :] = row_hi[COEF:EDGE, :]
        for r in range(TILES):
            rows = pl.ds(8 * r, 8)
            here = load_wet(8 * r)
            ext[0, 8 * r + 4 : 8 * r + 12, :] = total[rows, :] * here
            ext[1, 8 * r + 4 : 8 * r + 12, :] = coefficient(depth_ref[rows, :], here)
        for j in range(8):
            at = 16 * j
            send_ref[j, 0:22, :] = ext[0, at + 1 : at + 23, :]
            send_ref[j, 22:44, :] = ext[1, at + 1 : at + 23, :]
            line = jnp.zeros((1, LANE), jnp.float32)
            halves = [line, line]
            if j in (0, 7):
                for i in range(3):
                    factors = row_lo[EDGE + 5 + i : EDGE + 6 + i, :LANE] if j == 0 else row_hi[EDGE + i : EDGE + 1 + i, :LANE]
                    at = 32 * (i if j == 0 else 3 + i)
                    halves[at // LANE] = halves[at // LANE] + (pltpu.roll(factors, at % LANE, 1) if at % LANE else factors)
            send_ref[j, 44:45, :] = jnp.concatenate(halves, 1)
            send_ref[j, 45:48, :] = jnp.zeros((3, COLS), jnp.float32)
    for k in range(LEVELS):
        tracers_out(k).wait()


def advect(first, tracers, velocity, ocean, row_odd, col_odd, row_even, col_even, extra):
    ins = [HBM] * 3 + [ANY] * 4
    operands = [tracers, velocity, ocean, row_odd, col_odd, row_even, col_even]
    out_specs = [HBM]
    out_shape = [f32(TRACERS, LEVELS, ROWS, COLS)]
    block = pltpu.VMEM((ROWS, COLS), jnp.float32)
    narrow = pltpu.VMEM((ROWS, LANE), jnp.float32)
    scratch = [
        pltpu.VMEM((LEVELS, 2, ROWS, COLS), jnp.float32),
        pltpu.VMEM((LEVELS, 2, ROWS, COLS), jnp.float32),
        pltpu.VMEM((LEVELS, 2, ROWS, COLS), jnp.float32),
        pltpu.VMEM((ROWS, COLS), jnp.int32),
        pltpu.VMEM((2, MESSAGE, COLS), jnp.float32),
        pltpu.VMEM((2, ROWS, LANE), jnp.float32),
        block,
        block,
        narrow,
        pltpu.VMEM((LEVELS, 3, ROWS, LANE), jnp.float32),
        pltpu.SemaphoreType.DMA((3, LEVELS)),
        pltpu.SemaphoreType.DMA((8,)),
    ]
    aliases = {}
    if first == 0:
        ins = ins + [HBM]
        operands = operands + [extra]
        out_specs.append(VMEM)
        out_shape.append(f32(8, 48, COLS))
        scratch += [
            block,
            block,
            pltpu.VMEM((8, COLS), jnp.float32),
            pltpu.VMEM((2, ROWS + 8, COLS), jnp.float32),
            pltpu.VMEM((16, COLS), jnp.float32),
        ]
    else:
        aliases = {len(operands): 0}
        ins = ins + [HBM]
        operands = operands + [extra]
    return pl.pallas_call(
        functools.partial(advect_kernel, first),
        in_specs=ins,
        out_specs=out_specs,
        out_shape=out_shape,
        scratch_shapes=scratch,
        input_output_aliases=aliases,
        compiler_params=pltpu.CompilerParams(vmem_limit_bytes=(LIMA if first == 0 else LIMB) * 2**20),
        cost_estimate=pl.CostEstimate(flops=24_000_000, bytes_accessed=9_400_000, transcendentals=0),
        name="advect_forcing" if first == 0 else "advect_rest",
    )(*operands)


def insert_kernel(_, tops, out_hbm, most, sem):
    most[...] = jnp.broadcast_to(jnp.max(tops[...], axis=0)[0:1, :][None], most.shape)
    copy = pltpu.make_async_copy(most, out_hbm.at[:, 45:46, :LANE], sem.at[0])
    copy.start()
    copy.wait()


def insert(parcels, tops):
    return pl.pallas_call(
        insert_kernel,
        in_specs=[HBM, VMEM],
        out_specs=HBM,
        out_shape=f32(8, 48, COLS),
        scratch_shapes=[pltpu.VMEM((8, 1, LANE), jnp.float32), pltpu.SemaphoreType.DMA((1,))],
        input_output_aliases={0: 0},
        compiler_params=pltpu.CompilerParams(vmem_limit_bytes=60 * 2**20),
        cost_estimate=pl.CostEstimate(flops=1000, bytes_accessed=100_000, transcendentals=0),
        name="insert_maximum",
    )(parcels, tops)


NEAR = ((1, 0, 0.5), (-1, 0, 0.5), (0, 1, 0.5), (0, -1, 0.5), (1, 1, 0.125), (1, -1, 0.125), (-1, 1, 0.125), (-1, -1, 0.125))
PADDED = WIDE + LANE


def solve_kernel(got_ref, out_ref, h_ref, resid_ref, answer_ref, weight, buffers):
    here = slice(8, 8 + EXT)

    def spread():
        field = buffers[0, here, :]
        buffers[1, here, :] = pltpu.roll(field, PADDED - 1, 1)
        buffers[2, here, :] = pltpu.roll(field, 1, 1)

    def near(rows, cols, block):
        return buffers[{0: 0, 1: 1, -1: 2}[cols], 8 + rows : 8 + rows + EXT, block]

    def block_at(c):
        return pl.ds(c * COLS, COLS)

    for n in range(3):
        for rows in (slice(0, 16), slice(EXT, 16 + EXT)):
            buffers[n, rows, :] = jnp.zeros((16, PADDED), jnp.float32)
    buffers[0, 16:EXT, WIDE:] = jnp.zeros((EXT - 16, LANE), jnp.float32)
    for row in (0, EXT - 1):
        resid_ref[row : row + 1, :] = jnp.zeros((1, WIDE), jnp.float32)
    for j in range(8):
        cols = pl.ds(j * COLS, COLS)
        resid_ref[1:23, cols] = got_ref[j, 0:22, :]
        buffers[0, 9:31, cols] = got_ref[j, 22:44, :]
    lane, tile = lanes((8, LANE)), sublanes((8, LANE))
    group, row = lanes((8, COLS)), sublanes((8, COLS))
    used = (row >= 1) & (row <= 6) & (group >= 32 * (row - 1)) & (group <= 32 * (row - 1) + LEVELS)
    for j in range(7):
        pairs = got_ref[j, 44:45, :] * pltpu.roll(got_ref[j + 1, 44:45, :], COLS - 16, 1)
        flux = jnp.sum(jnp.where(used, pairs, 0.0), axis=1, keepdims=True)
        for rows, there in ((pl.ds(0, 8), tile < 4), (pl.ds(16, 8), tile >= 4)):
            last = pl.ds((j + 1) * COLS - LANE, LANE)
            after = pl.ds((j + 1) * COLS, LANE)
            resid_ref[rows, last] = resid_ref[rows, last] - jnp.where(there & (lane == LANE - 1), flux, 0.0)
            resid_ref[rows, after] = resid_ref[rows, after] + jnp.where(there & (lane == 0), flux, 0.0)
    most = got_ref[0, 45:46, 0:1]
    for j in range(1, 8):
        most = jnp.maximum(most, got_ref[j, 45:46, 0:1])
    lam_max = 0.5 + 10.0 * most
    theta = (lam_max + 0.5) / 2.0
    delta = (lam_max - 0.5) / 2.0
    sigma = theta / delta
    spread()

    def weigh(c, _):
        block = block_at(c)
        h = near(0, 0, block)
        h_ref[:, block] = h
        for n, (a, b, w) in enumerate(NEAR):
            weight[n, :, block] = w * (h + near(a, b, block))
        return 0

    for c in range(WIDE // COLS):
        weigh(c, 0)
    direction = resid_ref[...] / theta
    buffers[0, here, :WIDE] = direction
    answer_ref[...] = direction

    def step(_, rho):
        spread()
        rho_next = 1.0 / (2.0 * sigma - rho)
        keep, add = rho_next * rho, 2.0 * rho_next / delta

        def update(c, _):
            block = block_at(c)
            direction = near(0, 0, block)
            applied = 0.5 * direction
            for n, (a, b, _) in enumerate(NEAR):
                applied = applied + weight[n, :, block] * (direction - near(a, b, block))
            resid = jnp.where(h_ref[:, block] > 0.0, resid_ref[:, block] - applied, 0.0)
            resid_ref[:, block] = resid
            direction = keep * direction + add * resid
            buffers[0, here, block] = direction
            answer_ref[:, block] = answer_ref[:, block] + direction
            return 0

        for c in range(WIDE // COLS):
            update(c, 0)
        return rho_next

    lax.fori_loop(0, ITERS, step, 1.0 / sigma)
    out_ref[...] = answer_ref[4:20, :]


def solve(got):
    wide = pltpu.VMEM((EXT, WIDE), jnp.float32)
    return pl.pallas_call(
        solve_kernel,
        in_specs=[VMEM],
        out_specs=VMEM,
        out_shape=f32(16, WIDE),
        scratch_shapes=[
            wide,
            wide,
            wide,
            pltpu.VMEM((8, EXT, WIDE), jnp.float32),
            pltpu.VMEM((3, EXT + 16, PADDED), jnp.float32),
        ],
        compiler_params=pltpu.CompilerParams(vmem_limit_bytes=60 * 2**20),
        cost_estimate=pl.CostEstimate(flops=6_000_000, bytes_accessed=600_000, transcendentals=0),
        name="chebyshev",
    )(got)


def exchange(x, axis, odd):
    count = lax.axis_size(axis)
    pairs = []
    for i in range(odd, count - 1, 2):
        pairs += [(i, i + 1), (i + 1, i)]
    return lax.ppermute(x, axis, pairs)


def shards(tracers, velocity, ocean, thickness, depth):
    row_odd, col_odd, row_even, col_even, top = pack(thickness, tracers, velocity, ocean, depth)
    halos = (exchange(row_odd, "bx", 1), exchange(col_odd, "by", 1), exchange(row_even, "bx", 0), exchange(col_even, "by", 0))
    tops = lax.all_to_all(top, "bx", split_axis=0, concat_axis=0, tiled=True)
    part, parcels = advect(0, tracers, velocity, ocean, *halos, depth)
    got = lax.all_to_all(insert(parcels, tops), "by", split_axis=0, concat_axis=0, tiled=True)
    new_tracers = advect(2, tracers, velocity, ocean, *halos, part)[0]
    return new_tracers, solve(got)


def solution(mesh):
    return jax.shard_map(
        shards,
        mesh=mesh,
        in_specs=(
            P(None, None, "bx", "by"),
            P(None, None, "bx", "by"),
            P("bx", "by"),
            P(),
            P("bx", "by"),
        ),
        out_specs=(P(None, None, "bx", "by"), P(("bx", "by"), None)),
        check_vma=False,
    )
```

```python
import functools

import jax
import jax.numpy as jnp
from jax import lax
from jax.experimental import pallas as pl
from jax.experimental.pallas import tpu as pltpu
from jax.sharding import PartitionSpec as P

ITERS = 3
TRACERS = 4
LEVELS = 12
ROWS = 128
COLS = 256
TILES = ROWS // 8
LANE = 128
WIDE = 8 * COLS
EXT = 24
CHUNK = 32
TALL = 16
LIMA, LIMB = 852, 768

SPEED, WET, THICK, PART, COEF, EDGE, MESSAGE = 48, 60, 61, 64, 68, 72, 80
ANY = pl.BlockSpec(memory_space=pl.ANY)
HBM = pl.BlockSpec(memory_space=pltpu.HBM)
VMEM = pl.BlockSpec(memory_space=pltpu.VMEM)


def f32(*shape):
    return jax.ShapeDtypeStruct(shape, jnp.float32)


def lanes(shape):
    return lax.broadcasted_iota(jnp.int32, shape, len(shape) - 1)


def sublanes(shape):
    return lax.broadcasted_iota(jnp.int32, shape, len(shape) - 2)


def coefficient(depth, wet):
    return depth * (0.1 + 0.9 * wet)


def positive(x):
    return jnp.maximum(x, 0.0)


def negative(x):
    return jnp.minimum(x, 0.0)


def edge_forcing(q, u, v, wet, thick):
    shape = (8, COLS)
    row, col = sublanes(shape), lanes(shape)
    total = jnp.zeros(shape, jnp.float32)
    flux_x = jnp.zeros(shape, jnp.float32)
    flux_y = jnp.zeros(shape, jnp.float32)
    for k in range(LEVELS):
        depth = thick[k]
        total = total + depth * q[k]
        flux_x = flux_x + depth * (positive(u[k]) * q[k] + negative(u[k]) * pltpu.roll(q[k], 7, 0))
        flux_y = flux_y + depth * (positive(v[k]) * q[k] + negative(v[k]) * pltpu.roll(q[k], COLS - 1, 1))
    flux_x = flux_x * jnp.where(row == 7, 0.0, wet * pltpu.roll(wet, 7, 0))
    flux_y = flux_y * jnp.where(col == COLS - 1, 0.0, wet * pltpu.roll(wet, COLS - 1, 1))
    return wet * (total - (flux_x - pltpu.roll(flux_x, 1, 0)) - (flux_y - pltpu.roll(flux_y, 1, 1)))


def edge_terms(q, v, wet, thick):
    lane = lanes((8, LANE))
    last, first = wet[:, LANE:], wet[:, :LANE]
    upwind = jnp.zeros((8, LANE), jnp.float32)
    terms = jnp.where(lane == 28, pltpu.roll(first, 28, 1), 0.0)
    for k in range(LEVELS):
        depth = thick[k]
        speed = v[k][:, LANE:]
        upwind = upwind + depth * positive(speed) * q[k][:, LANE:]
        terms = jnp.where(lane == k, pltpu.roll(depth * negative(speed) * last, k + 1, 1), terms)
        terms = jnp.where(lane == 16 + k, pltpu.roll(q[k][:, :LANE] * first, 16 + k, 1), terms)
    return jnp.where(lane == LEVELS, pltpu.roll(upwind * last, LEVELS + 1, 1), terms)


def pack_kernel(thick_hbm, t_hbm, v_hbm, ocean_hbm, depth_hbm, row_even, row_odd, col_even, col_odd, top,
                t_ref, u_top, u_low, v_top, v_low, v_last, ocean_ref, depth_ref, thick, row_both, col_both, sems):
    odd_x, odd_y = lax.axis_index("bx") % 2, lax.axis_index("by") % 2
    row_hi, row_lo = row_both.at[0], row_both.at[1]
    col_hi, col_lo = col_both.at[0], col_both.at[1]

    def chunk_copy(c):
        rows = pl.ds(pl.multiple_of(c * CHUNK, CHUNK), CHUNK)
        return pltpu.make_async_copy(t_hbm.at[:, :, rows, :], t_ref.at[:, :, rows, :], sems.at[c])

    chunks = ROWS // CHUNK
    small = [
        pltpu.make_async_copy(ocean_hbm, ocean_ref, sems.at[chunks]),
        pltpu.make_async_copy(depth_hbm, depth_ref, sems.at[chunks + 1]),
        pltpu.make_async_copy(v_hbm.at[1, :, :, LANE:], v_last, sems.at[chunks + 2]),
        pltpu.make_async_copy(thick_hbm, thick, sems.at[chunks + 7]),
    ]
    tiles = [
        pltpu.make_async_copy(v_hbm.at[0, :, 0:8, :], u_top, sems.at[chunks + 3]),
        pltpu.make_async_copy(v_hbm.at[0, :, ROWS - 8 :, :], u_low, sems.at[chunks + 4]),
        pltpu.make_async_copy(v_hbm.at[1, :, 0:8, :], v_top, sems.at[chunks + 5]),
        pltpu.make_async_copy(v_hbm.at[1, :, ROWS - 8 :, :], v_low, sems.at[chunks + 6]),
    ]
    for copy in small:
        copy.start()
    for c in range(chunks):
        chunk_copy(c).start()
    for copy in tiles:
        copy.start()
    for copy in small:
        copy.wait()
    wet = ocean_ref[...].astype(jnp.float32)
    coef = coefficient(depth_ref[...], wet)
    most = jnp.max(jnp.max(coef, axis=0, keepdims=True), axis=1, keepdims=True)
    top[...] = jnp.broadcast_to(most[None], top.shape)
    thick_lanes = jnp.zeros((1, COLS), jnp.float32)
    for k in range(LEVELS):
        thick_lanes = jnp.where(lanes((1, COLS)) == k, thick[k], thick_lanes)

    def gather(c, _):
        chunk_copy(c).wait()
        lane = lanes((CHUNK, LANE))
        rows = pl.ds(pl.multiple_of(c * CHUNK, CHUNK), CHUNK)
        ocean = ocean_ref[rows, :].astype(jnp.float32)
        hi = jnp.where(lane == 2 * WET, pltpu.roll(ocean[:, LANE:], (2 * WET + 1) % LANE, 1), 0.0)
        lo = jnp.where(lane == 2 * WET - 1, pltpu.roll(ocean[:, :LANE], 2 * WET - 1, 1), 0.0)
        for k in range(LEVELS):
            for t in range(TRACERS):
                s = t * LEVELS + k
                hi = jnp.where(lane == 2 * s, pltpu.roll(t_ref[t, k, rows, LANE:], 2 * s + 1, 1), hi)
                place = (2 * s - 1) % LANE
                lo = jnp.where(lane == place, pltpu.roll(t_ref[t, k, rows, :LANE], place, 1), lo)
            s = SPEED + k
            hi = jnp.where(lane == 2 * s, pltpu.roll(v_last[k, rows, :], 2 * s + 1, 1), hi)
        col_hi[rows, :] = hi
        col_lo[rows, :] = lo
        return 0

    lax.fori_loop(0, chunks, gather, 0)
    for copy in tiles:
        copy.wait()
    for t in range(TRACERS):
        for k in range(LEVELS):
            s = t * LEVELS + k
            row_hi[s : s + 1, :] = t_ref[t, k, ROWS - 1 : ROWS, :]
            row_lo[s : s + 1, :] = t_ref[t, k, 0:1, :]
    for k in range(LEVELS):
        row_hi[SPEED + k : SPEED + k + 1, :] = u_low[k, 7:8, :]
    row_lo[SPEED:WET, :] = jnp.zeros((WET - SPEED, COLS), jnp.float32)
    for row, message, u, v, keep in ((0, row_lo, u_top, v_top, 0), (ROWS - 8, row_hi, u_low, v_low, 4)):
        rows = slice(row, row + 8)
        here = ocean_ref[rows, :].astype(jnp.float32)
        q = [0.2 * t_ref[0, k, rows, :] - 0.8 * t_ref[1, k, rows, :] for k in range(LEVELS)]
        speed_x = [u[k] for k in range(LEVELS)]
        speed_y = [v[k] for k in range(LEVELS)]
        message[WET:THICK, :] = here[7:8, :] if keep else here[0:1, :]
        message[THICK:PART, :] = jnp.broadcast_to(thick_lanes, (PART - THICK, COLS))
        message[PART:COEF, :] = edge_forcing(q, speed_x, speed_y, here, thick)[keep : keep + 4, :]
        message[COEF:EDGE, :] = coefficient(depth_ref[rows, :], here)[keep : keep + 4, :]
        message[EDGE:MESSAGE, :LANE] = edge_terms(q, speed_y, here, thick)
        message[EDGE:MESSAGE, LANE:] = jnp.zeros((8, LANE), jnp.float32)
    row_even[...] = row_both[odd_x]
    row_odd[...] = row_both[1 - odd_x]
    col_even[...] = col_both[odd_y]
    col_odd[...] = col_both[1 - odd_y]


def pack(thickness, tracers, velocity, ocean, depth):
    tile = (LEVELS, 8, COLS)
    return pl.pallas_call(
        pack_kernel,
        in_specs=[HBM] * 5,
        out_specs=[VMEM] * 5,
        out_shape=[f32(MESSAGE, COLS), f32(MESSAGE, COLS), f32(ROWS, LANE), f32(ROWS, LANE), f32(16, 8, LANE)],
        scratch_shapes=[
            pltpu.VMEM((TRACERS, LEVELS, ROWS, COLS), jnp.float32),
            pltpu.VMEM(tile, jnp.float32),
            pltpu.VMEM(tile, jnp.float32),
            pltpu.VMEM(tile, jnp.float32),
            pltpu.VMEM(tile, jnp.float32),
            pltpu.VMEM((LEVELS, ROWS, LANE), jnp.float32),
            pltpu.VMEM((ROWS, COLS), jnp.int32),
            pltpu.VMEM((ROWS, COLS), jnp.float32),
            pltpu.SMEM((LEVELS,), jnp.float32),
            pltpu.VMEM((2, MESSAGE, COLS), jnp.float32),
            pltpu.VMEM((2, ROWS, LANE), jnp.float32),
            pltpu.SemaphoreType.DMA((ROWS // CHUNK + 8,)),
        ],
        compiler_params=pltpu.CompilerParams(vmem_limit_bytes=60 * 2**20),
        cost_estimate=pl.CostEstimate(flops=4_000_000, bytes_accessed=7_400_000, transcendentals=0),
        name="pack_edges",
    )(thickness, tracers, velocity, ocean, depth)


def ahead_y(x, edge):
    last = lanes((x.shape[0], LANE)) == LANE - 1
    a, b = pltpu.roll(x[:, :LANE], LANE - 1, 1), pltpu.roll(x[:, LANE:], LANE - 1, 1)
    return jnp.concatenate([jnp.where(last, b, a), jnp.where(last, edge, b)], 1)


def behind_y(x, edge):
    first = lanes((x.shape[0], LANE)) == 0
    a, b = pltpu.roll(x[:, :LANE], 1, 1), pltpu.roll(x[:, LANE:], 1, 1)
    return jnp.concatenate([jnp.where(first, edge, a), jnp.where(first, a, b)], 1)


def above(load, edge, r, tall=8):
    if (r + 1) * tall < ROWS:
        return load(tall * r + 1)
    return jnp.where(sublanes((tall, COLS)) == tall - 1, edge, pltpu.roll(load(tall * r), tall - 1, 0))


def upwind(speed, here, ahead):
    return speed * jnp.where(speed > 0.0, here, ahead)


def advect_kernel(first, *refs):
    if first == 0:
        (t_hbm, v_hbm, ocean_hbm, row_even, row_odd, col_even, col_odd, depth_hbm, out_hbm, send_ref,
         t_ref, v_ref, out_ref, ocean_ref, rows_in, cols_in, w_x, w_y, before_y, edges, sems, small_sems,
         depth_ref, total, flux, ext, thick) = refs
    else:
        (t_hbm, v_hbm, ocean_hbm, row_even, row_odd, col_even, col_odd, _, out_hbm,
         t_ref, v_ref, out_ref, ocean_ref, rows_in, cols_in, w_x, w_y, before_y, edges, sems, small_sems) = refs
    odd_x, odd_y = lax.axis_index("bx") % 2, lax.axis_index("by") % 2
    row_lo, row_hi = rows_in.at[0], rows_in.at[1]
    small = [
        (ocean_hbm, ocean_ref),
        (row_even, rows_in.at[1 - odd_x]),
        (row_odd, rows_in.at[odd_x]),
        (col_even, cols_in.at[1 - odd_y]),
        (col_odd, cols_in.at[odd_y]),
    ]
    if first == 0:
        small += [(depth_hbm, depth_ref)]
    small = [pltpu.make_async_copy(a, b, small_sems.at[i]) for i, (a, b) in enumerate(small)]

    def tracers_in(k):
        return pltpu.make_async_copy(t_hbm.at[first : first + 2, k], t_ref.at[k], sems.at[0, k])

    def velocity_in(k):
        return pltpu.make_async_copy(v_hbm.at[:, k], v_ref.at[k], sems.at[1, k])

    def tracers_out(k):
        return pltpu.make_async_copy(out_ref.at[k], out_hbm.at[first : first + 2, k], sems.at[2, k])

    for copy in small:
        copy.start()
    for k in range(LEVELS):
        tracers_in(k).start()
        velocity_in(k).start()
    for copy in small:
        copy.wait()
    even = lanes((8, LANE)) % 2 == 0
    load_wet = lambda at: ocean_ref[at : at + 8, :].astype(jnp.float32)
    for r in range(TILES):
        rows = pl.ds(8 * r, 8)
        edge = jnp.where(even, cols_in[0, rows, :], cols_in[1, rows, :])
        for k in range(LEVELS):
            for i, slot in enumerate((first * LEVELS + k, (first + 1) * LEVELS + k, SPEED + k)):
                edges[k, i, rows, :] = pltpu.roll(edge, (LANE - 2 * slot) % LANE, 1)
        here = load_wet(8 * r)
        wet_edge = pltpu.roll(edge, LANE - 2 * WET, 1)
        w_x[rows, :] = here * above(load_wet, row_hi[WET : WET + 1, :], r)
        w_y[rows, :] = here * ahead_y(here, wet_edge)
        before_y[rows, :] = here[:, :LANE] * wet_edge
        if first == 0:
            total[rows, :] = jnp.zeros((8, COLS), jnp.float32)
    w_before = load_wet(0)[0:1, :] * row_lo[WET : WET + 1, :]
    if first == 0:
        flux[...] = jnp.zeros((8, COLS), jnp.float32)
        line = rows_in[1 - odd_x, THICK : THICK + 1, :]
        for k in range(LEVELS):
            thick[k : k + 1, :] = jnp.broadcast_to(line[:, k : k + 1], (1, COLS))

    def level(k, _):
        tracers_in(k).wait()
        velocity_in(k).wait()
        u_before = row_lo[pl.ds(SPEED + k, 1), :] * w_before
        into_x = [upwind(u_before, row_lo[pl.ds((first + t) * LEVELS + k, 1), :], t_ref[k, t, 0:1, :]) for t in range(2)]
        carry, out_x = list(into_x), [None, None]
        if first == 0:
            depth = thick[pl.ds(k, 1), :]
        for r in range(ROWS // TALL):
            rows = pl.ds(TALL * r, TALL)
            u = v_ref[k, 0, rows, :] * w_x[rows, :]
            v = v_ref[k, 1, rows, :] * w_y[rows, :]
            v_before = edges[k, 2, rows, :] * before_y[rows, :]
            new = []
            for t in range(2):
                load = lambda at: t_ref[k, t, at : at + TALL, :]
                slot = (first + t) * LEVELS + k
                c = load(TALL * r)
                c_edge = edges[k, t, rows, :]
                here_x = upwind(u, c, above(load, row_hi[pl.ds(slot, 1), :], r, TALL))
                turned = pltpu.roll(here_x, 1, 0)
                past_x = jnp.where(sublanes((TALL, COLS)) == 0, carry[t], turned)
                carry[t] = turned[0:1, :]
                if r == ROWS // TALL - 1:
                    out_x[t] = here_x[TALL - 1 :, :]
                here_y = upwind(v, c, ahead_y(c, c_edge))
                past_y = behind_y(here_y, upwind(v_before, c_edge, c[:, :LANE]))
                value = (c - (here_x - past_x)) - (here_y - past_y)
                out_ref[k, t, rows, :] = value
                new.append(value)
            if first == 0:
                total[rows, :] = total[rows, :] + depth * (0.2 * new[0] - 0.8 * new[1])
        if first == 0:
            flux[0:1, :] = flux[0:1, :] + depth * (0.2 * into_x[0] - 0.8 * into_x[1])
            flux[1:2, :] = flux[1:2, :] + depth * (0.2 * out_x[0] - 0.8 * out_x[1])
        tracers_out(k).start()
        return 0

    lax.fori_loop(0, LEVELS, level, 0)

    if first == 0:
        row = sublanes((4, COLS))
        ext[0, 0:4, :] = row_lo[PART:COEF, :] - jnp.where(row == 3, flux[0:1, :], 0.0)
        ext[0, ROWS + 4 :, :] = row_hi[PART:COEF, :] + jnp.where(row == 0, flux[1:2, :], 0.0)
        ext[1, 0:4, :] = row_lo[COEF:EDGE, :]
        ext[1, ROWS + 4 :, :] = row_hi[COEF:EDGE, :]
        for r in range(TILES):
            rows = pl.ds(8 * r, 8)
            here = load_wet(8 * r)
            ext[0, 8 * r + 4 : 8 * r + 12, :] = total[rows, :] * here
            ext[1, 8 * r + 4 : 8 * r + 12, :] = coefficient(depth_ref[rows, :], here)
        for j in range(8):
            at = 16 * j
            send_ref[j, 0:22, :] = ext[0, at + 1 : at + 23, :]
            send_ref[j, 22:44, :] = ext[1, at + 1 : at + 23, :]
            line = jnp.zeros((1, LANE), jnp.float32)
            halves = [line, line]
            if j in (0, 7):
                for i in range(3):
                    factors = row_lo[EDGE + 5 + i : EDGE + 6 + i, :LANE] if j == 0 else row_hi[EDGE + i : EDGE + 1 + i, :LANE]
                    at = 32 * (i if j == 0 else 3 + i)
                    halves[at // LANE] = halves[at // LANE] + (pltpu.roll(factors, at % LANE, 1) if at % LANE else factors)
            send_ref[j, 44:45, :] = jnp.concatenate(halves, 1)
            send_ref[j, 45:48, :] = jnp.zeros((3, COLS), jnp.float32)
    for k in range(LEVELS):
        tracers_out(k).wait()


def advect(first, tracers, velocity, ocean, row_even, row_odd, col_even, col_odd, extra):
    ins = [HBM] * 3 + [ANY] * 4
    operands = [tracers, velocity, ocean, row_even, row_odd, col_even, col_odd]
    out_specs = [HBM]
    out_shape = [f32(TRACERS, LEVELS, ROWS, COLS)]
    block = pltpu.VMEM((ROWS, COLS), jnp.float32)
    narrow = pltpu.VMEM((ROWS, LANE), jnp.float32)
    scratch = [
        pltpu.VMEM((LEVELS, 2, ROWS, COLS), jnp.float32),
        pltpu.VMEM((LEVELS, 2, ROWS, COLS), jnp.float32),
        pltpu.VMEM((LEVELS, 2, ROWS, COLS), jnp.float32),
        pltpu.VMEM((ROWS, COLS), jnp.int32),
        pltpu.VMEM((2, MESSAGE, COLS), jnp.float32),
        pltpu.VMEM((2, ROWS, LANE), jnp.float32),
        block,
        block,
        narrow,
        pltpu.VMEM((LEVELS, 3, ROWS, LANE), jnp.float32),
        pltpu.SemaphoreType.DMA((3, LEVELS)),
        pltpu.SemaphoreType.DMA((8,)),
    ]
    aliases = {}
    if first == 0:
        ins = ins + [HBM]
        operands = operands + [extra]
        out_specs.append(VMEM)
        out_shape.append(f32(8, 48, COLS))
        scratch += [
            block,
            block,
            pltpu.VMEM((8, COLS), jnp.float32),
            pltpu.VMEM((2, ROWS + 8, COLS), jnp.float32),
            pltpu.VMEM((16, COLS), jnp.float32),
        ]
    else:
        aliases = {len(operands): 0}
        ins = ins + [HBM]
        operands = operands + [extra]
    return pl.pallas_call(
        functools.partial(advect_kernel, first),
        in_specs=ins,
        out_specs=out_specs,
        out_shape=out_shape,
        scratch_shapes=scratch,
        input_output_aliases=aliases,
        compiler_params=pltpu.CompilerParams(vmem_limit_bytes=(LIMA if first == 0 else LIMB) * 2**16),
        cost_estimate=pl.CostEstimate(flops=24_000_000, bytes_accessed=9_400_000, transcendentals=0),
        name="advect_forcing" if first == 0 else "advect_rest",
    )(*operands)


def insert_kernel(_, tops, out_hbm, most, sem):
    most[...] = jnp.broadcast_to(jnp.max(tops[...], axis=0)[0:1, :][None], most.shape)
    copy = pltpu.make_async_copy(most, out_hbm.at[:, 45:46, :LANE], sem.at[0])
    copy.start()
    copy.wait()


def insert(parcels, tops):
    return pl.pallas_call(
        insert_kernel,
        in_specs=[HBM, VMEM],
        out_specs=HBM,
        out_shape=f32(8, 48, COLS),
        scratch_shapes=[pltpu.VMEM((8, 1, LANE), jnp.float32), pltpu.SemaphoreType.DMA((1,))],
        input_output_aliases={0: 0},
        compiler_params=pltpu.CompilerParams(vmem_limit_bytes=60 * 2**20),
        cost_estimate=pl.CostEstimate(flops=1000, bytes_accessed=100_000, transcendentals=0),
        name="insert_maximum",
    )(parcels, tops)


NEAR = ((1, 0, 0.5), (-1, 0, 0.5), (0, 1, 0.5), (0, -1, 0.5), (1, 1, 0.125), (1, -1, 0.125), (-1, 1, 0.125), (-1, -1, 0.125))
PADDED = WIDE + LANE


def solve_kernel(got_ref, out_ref, h_ref, resid_ref, answer_ref, weight, buffers):
    here = slice(8, 8 + EXT)

    def spread():
        field = buffers[0, here, :]
        buffers[1, here, :] = pltpu.roll(field, PADDED - 1, 1)
        buffers[2, here, :] = pltpu.roll(field, 1, 1)

    def near(rows, cols, block):
        return buffers[{0: 0, 1: 1, -1: 2}[cols], 8 + rows : 8 + rows + EXT, block]

    def block_at(c):
        return pl.ds(c * COLS, COLS)

    for n in range(3):
        for rows in (slice(0, 16), slice(EXT, 16 + EXT)):
            buffers[n, rows, :] = jnp.zeros((16, PADDED), jnp.float32)
    buffers[0, 16:EXT, WIDE:] = jnp.zeros((EXT - 16, LANE), jnp.float32)
    for row in (0, EXT - 1):
        resid_ref[row : row + 1, :] = jnp.zeros((1, WIDE), jnp.float32)
    for j in range(8):
        cols = pl.ds(j * COLS, COLS)
        resid_ref[1:23, cols] = got_ref[j, 0:22, :]
        buffers[0, 9:31, cols] = got_ref[j, 22:44, :]
    lane, tile = lanes((8, LANE)), sublanes((8, LANE))
    group, row = lanes((8, COLS)), sublanes((8, COLS))
    used = (row >= 1) & (row <= 6) & (group >= 32 * (row - 1)) & (group <= 32 * (row - 1) + LEVELS)
    for j in range(7):
        pairs = got_ref[j, 44:45, :] * pltpu.roll(got_ref[j + 1, 44:45, :], COLS - 16, 1)
        flux = jnp.sum(jnp.where(used, pairs, 0.0), axis=1, keepdims=True)
        for rows, there in ((pl.ds(0, 8), tile < 4), (pl.ds(16, 8), tile >= 4)):
            last = pl.ds((j + 1) * COLS - LANE, LANE)
            after = pl.ds((j + 1) * COLS, LANE)
            resid_ref[rows, last] = resid_ref[rows, last] - jnp.where(there & (lane == LANE - 1), flux, 0.0)
            resid_ref[rows, after] = resid_ref[rows, after] + jnp.where(there & (lane == 0), flux, 0.0)
    most = got_ref[0, 45:46, 0:1]
    for j in range(1, 8):
        most = jnp.maximum(most, got_ref[j, 45:46, 0:1])
    lam_max = 0.5 + 10.0 * most
    theta = (lam_max + 0.5) / 2.0
    delta = (lam_max - 0.5) / 2.0
    sigma = theta / delta
    spread()

    def weigh(c, _):
        block = block_at(c)
        h = near(0, 0, block)
        h_ref[:, block] = h
        for n, (a, b, w) in enumerate(NEAR):
            weight[n, :, block] = w * (h + near(a, b, block))
        return 0

    for c in range(WIDE // COLS):
        weigh(c, 0)
    direction = resid_ref[...] / theta
    buffers[0, here, :WIDE] = direction
    answer_ref[...] = direction

    def step(_, rho):
        spread()
        rho_next = 1.0 / (2.0 * sigma - rho)
        keep, add = rho_next * rho, 2.0 * rho_next / delta

        def update(c, _):
            block = block_at(c)
            direction = near(0, 0, block)
            applied = 0.5 * direction
            for n, (a, b, _) in enumerate(NEAR):
                applied = applied + weight[n, :, block] * (direction - near(a, b, block))
            resid = jnp.where(h_ref[:, block] > 0.0, resid_ref[:, block] - applied, 0.0)
            resid_ref[:, block] = resid
            direction = keep * direction + add * resid
            buffers[0, here, block] = direction
            answer_ref[:, block] = answer_ref[:, block] + direction
            return 0

        for c in range(WIDE // COLS):
            update(c, 0)
        return rho_next

    lax.fori_loop(0, ITERS, step, 1.0 / sigma)
    out_ref[...] = answer_ref[4:20, :]


def solve(got):
    wide = pltpu.VMEM((EXT, WIDE), jnp.float32)
    return pl.pallas_call(
        solve_kernel,
        in_specs=[VMEM],
        out_specs=VMEM,
        out_shape=f32(16, WIDE),
        scratch_shapes=[
            wide,
            wide,
            wide,
            pltpu.VMEM((8, EXT, WIDE), jnp.float32),
            pltpu.VMEM((3, EXT + 16, PADDED), jnp.float32),
        ],
        compiler_params=pltpu.CompilerParams(vmem_limit_bytes=60 * 2**20),
        cost_estimate=pl.CostEstimate(flops=6_000_000, bytes_accessed=600_000, transcendentals=0),
        name="chebyshev",
    )(got)


def exchange(x, axis, odd):
    count = lax.axis_size(axis)
    pairs = []
    for i in range(odd, count - 1, 2):
        pairs += [(i, i + 1), (i + 1, i)]
    return lax.ppermute(x, axis, pairs)


def shards(tracers, velocity, ocean, thickness, depth):
    row_even, row_odd, col_even, col_odd, top = pack(thickness, tracers, velocity, ocean, depth)
    from_row_odd, from_col_odd = exchange(row_odd, "bx", 1), exchange(col_odd, "by", 1)
    halos = (exchange(row_even, "bx", 0), from_row_odd, exchange(col_even, "by", 0), from_col_odd)
    tops = lax.all_to_all(top, "bx", split_axis=0, concat_axis=0, tiled=True)
    part, parcels = advect(0, tracers, velocity, ocean, *halos, depth)
    got = lax.all_to_all(insert(parcels, tops), "by", split_axis=0, concat_axis=0, tiled=True)
    new_tracers = advect(2, tracers, velocity, ocean, *halos, part)[0]
    return new_tracers, solve(got)


def solution(mesh):
    return jax.shard_map(
        shards,
        mesh=mesh,
        in_specs=(
            P(None, None, "bx", "by"),
            P(None, None, "bx", "by"),
            P("bx", "by"),
            P(),
            P("bx", "by"),
        ),
        out_specs=(P(None, None, "bx", "by"), P(("bx", "by"), None)),
        check_vma=False,
    )
```

```python
import functools

import jax
import jax.numpy as jnp
from jax import lax
from jax.experimental import pallas as pl
from jax.experimental.pallas import tpu as pltpu
from jax.sharding import PartitionSpec as P

ITERS = 3
TRACERS = 4
LEVELS = 12
ROWS = 128
COLS = 256
TILES = ROWS // 8
LANE = 128
WIDE = 8 * COLS
EXT = 24
CHUNK = 32
TALL = 16
LIMA, LIMB = 48, 48

SPEED, WET, THICK, PART, COEF, EDGE, MESSAGE = 48, 60, 61, 64, 68, 72, 80
ANY = pl.BlockSpec(memory_space=pl.ANY)
HBM = pl.BlockSpec(memory_space=pltpu.HBM)
VMEM = pl.BlockSpec(memory_space=pltpu.VMEM)


def f32(*shape):
    return jax.ShapeDtypeStruct(shape, jnp.float32)


def lanes(shape):
    return lax.broadcasted_iota(jnp.int32, shape, len(shape) - 1)


def sublanes(shape):
    return lax.broadcasted_iota(jnp.int32, shape, len(shape) - 2)


def coefficient(depth, wet):
    return depth * (0.1 + 0.9 * wet)


def positive(x):
    return jnp.maximum(x, 0.0)


def negative(x):
    return jnp.minimum(x, 0.0)


def edge_forcing(q, u, v, wet, thick):
    shape = (8, COLS)
    row, col = sublanes(shape), lanes(shape)
    total = jnp.zeros(shape, jnp.float32)
    flux_x = jnp.zeros(shape, jnp.float32)
    flux_y = jnp.zeros(shape, jnp.float32)
    for k in range(LEVELS):
        depth = thick[k]
        total = total + depth * q[k]
        flux_x = flux_x + depth * (positive(u[k]) * q[k] + negative(u[k]) * pltpu.roll(q[k], 7, 0))
        flux_y = flux_y + depth * (positive(v[k]) * q[k] + negative(v[k]) * pltpu.roll(q[k], COLS - 1, 1))
    flux_x = flux_x * jnp.where(row == 7, 0.0, wet * pltpu.roll(wet, 7, 0))
    flux_y = flux_y * jnp.where(col == COLS - 1, 0.0, wet * pltpu.roll(wet, COLS - 1, 1))
    return wet * (total - (flux_x - pltpu.roll(flux_x, 1, 0)) - (flux_y - pltpu.roll(flux_y, 1, 1)))


def edge_terms(q, v, wet, thick):
    lane = lanes((8, LANE))
    last, first = wet[:, LANE:], wet[:, :LANE]
    upwind = jnp.zeros((8, LANE), jnp.float32)
    terms = jnp.where(lane == 28, pltpu.roll(first, 28, 1), 0.0)
    for k in range(LEVELS):
        depth = thick[k]
        speed = v[k][:, LANE:]
        upwind = upwind + depth * positive(speed) * q[k][:, LANE:]
        terms = jnp.where(lane == k, pltpu.roll(depth * negative(speed) * last, k + 1, 1), terms)
        terms = jnp.where(lane == 16 + k, pltpu.roll(q[k][:, :LANE] * first, 16 + k, 1), terms)
    return jnp.where(lane == LEVELS, pltpu.roll(upwind * last, LEVELS + 1, 1), terms)


def pack_kernel(thick_hbm, t_hbm, v_hbm, ocean_hbm, depth_hbm, row_even, row_odd, col_even, col_odd, top,
                t_ref, u_top, u_low, v_top, v_low, v_last, ocean_ref, depth_ref, thick, row_both, col_both, sems):
    odd_x, odd_y = lax.axis_index("bx") % 2, lax.axis_index("by") % 2
    row_hi, row_lo = row_both.at[0], row_both.at[1]
    col_hi, col_lo = col_both.at[0], col_both.at[1]

    def chunk_copy(c):
        rows = pl.ds(pl.multiple_of(c * CHUNK, CHUNK), CHUNK)
        return pltpu.make_async_copy(t_hbm.at[:, :, rows, :], t_ref.at[:, :, rows, :], sems.at[c])

    chunks = ROWS // CHUNK
    small = [
        pltpu.make_async_copy(ocean_hbm, ocean_ref, sems.at[chunks]),
        pltpu.make_async_copy(depth_hbm, depth_ref, sems.at[chunks + 1]),
        pltpu.make_async_copy(v_hbm.at[1, :, :, LANE:], v_last, sems.at[chunks + 2]),
        pltpu.make_async_copy(thick_hbm, thick, sems.at[chunks + 7]),
    ]
    tiles = [
        pltpu.make_async_copy(v_hbm.at[0, :, 0:8, :], u_top, sems.at[chunks + 3]),
        pltpu.make_async_copy(v_hbm.at[0, :, ROWS - 8 :, :], u_low, sems.at[chunks + 4]),
        pltpu.make_async_copy(v_hbm.at[1, :, 0:8, :], v_top, sems.at[chunks + 5]),
        pltpu.make_async_copy(v_hbm.at[1, :, ROWS - 8 :, :], v_low, sems.at[chunks + 6]),
    ]
    for copy in small:
        copy.start()
    for c in range(chunks):
        chunk_copy(c).start()
    for copy in tiles:
        copy.start()
    for copy in small:
        copy.wait()
    wet = ocean_ref[...].astype(jnp.float32)
    coef = coefficient(depth_ref[...], wet)
    most = jnp.max(jnp.max(coef, axis=0, keepdims=True), axis=1, keepdims=True)
    top[...] = jnp.broadcast_to(most[None], top.shape)
    thick_lanes = jnp.zeros((1, COLS), jnp.float32)
    for k in range(LEVELS):
        thick_lanes = jnp.where(lanes((1, COLS)) == k, thick[k], thick_lanes)

    def gather(c, _):
        chunk_copy(c).wait()
        lane = lanes((CHUNK, LANE))
        rows = pl.ds(pl.multiple_of(c * CHUNK, CHUNK), CHUNK)
        ocean = ocean_ref[rows, :].astype(jnp.float32)
        hi = jnp.where(lane == 2 * WET, pltpu.roll(ocean[:, LANE:], (2 * WET + 1) % LANE, 1), 0.0)
        lo = jnp.where(lane == 2 * WET - 1, pltpu.roll(ocean[:, :LANE], 2 * WET - 1, 1), 0.0)
        for k in range(LEVELS):
            for t in range(TRACERS):
                s = t * LEVELS + k
                hi = jnp.where(lane == 2 * s, pltpu.roll(t_ref[t, k, rows, LANE:], 2 * s + 1, 1), hi)
                place = (2 * s - 1) % LANE
                lo = jnp.where(lane == place, pltpu.roll(t_ref[t, k, rows, :LANE], place, 1), lo)
            s = SPEED + k
            hi = jnp.where(lane == 2 * s, pltpu.roll(v_last[k, rows, :], 2 * s + 1, 1), hi)
        col_hi[rows, :] = hi
        col_lo[rows, :] = lo
        return 0

    lax.fori_loop(0, chunks, gather, 0)
    for copy in tiles:
        copy.wait()
    for t in range(TRACERS):
        for k in range(LEVELS):
            s = t * LEVELS + k
            row_hi[s : s + 1, :] = t_ref[t, k, ROWS - 1 : ROWS, :]
            row_lo[s : s + 1, :] = t_ref[t, k, 0:1, :]
    for k in range(LEVELS):
        row_hi[SPEED + k : SPEED + k + 1, :] = u_low[k, 7:8, :]
    row_lo[SPEED:WET, :] = jnp.zeros((WET - SPEED, COLS), jnp.float32)
    for row, message, u, v, keep in ((0, row_lo, u_top, v_top, 0), (ROWS - 8, row_hi, u_low, v_low, 4)):
        rows = slice(row, row + 8)
        here = ocean_ref[rows, :].astype(jnp.float32)
        q = [0.2 * t_ref[0, k, rows, :] - 0.8 * t_ref[1, k, rows, :] for k in range(LEVELS)]
        speed_x = [u[k] for k in range(LEVELS)]
        speed_y = [v[k] for k in range(LEVELS)]
        message[WET:THICK, :] = here[7:8, :] if keep else here[0:1, :]
        message[THICK:PART, :] = jnp.broadcast_to(thick_lanes, (PART - THICK, COLS))
        message[PART:COEF, :] = edge_forcing(q, speed_x, speed_y, here, thick)[keep : keep + 4, :]
        message[COEF:EDGE, :] = coefficient(depth_ref[rows, :], here)[keep : keep + 4, :]
        message[EDGE:MESSAGE, :LANE] = edge_terms(q, speed_y, here, thick)
        message[EDGE:MESSAGE, LANE:] = jnp.zeros((8, LANE), jnp.float32)
    row_even[...] = row_both[odd_x]
    row_odd[...] = row_both[1 - odd_x]
    col_even[...] = col_both[odd_y]
    col_odd[...] = col_both[1 - odd_y]


def pack(thickness, tracers, velocity, ocean, depth):
    tile = (LEVELS, 8, COLS)
    return pl.pallas_call(
        pack_kernel,
        in_specs=[HBM] * 5,
        out_specs=[VMEM] * 5,
        out_shape=[f32(MESSAGE, COLS), f32(MESSAGE, COLS), f32(ROWS, LANE), f32(ROWS, LANE), f32(16, 1, LANE)],
        scratch_shapes=[
            pltpu.VMEM((TRACERS, LEVELS, ROWS, COLS), jnp.float32),
            pltpu.VMEM(tile, jnp.float32),
            pltpu.VMEM(tile, jnp.float32),
            pltpu.VMEM(tile, jnp.float32),
            pltpu.VMEM(tile, jnp.float32),
            pltpu.VMEM((LEVELS, ROWS, LANE), jnp.float32),
            pltpu.VMEM((ROWS, COLS), jnp.int32),
            pltpu.VMEM((ROWS, COLS), jnp.float32),
            pltpu.SMEM((LEVELS,), jnp.float32),
            pltpu.VMEM((2, MESSAGE, COLS), jnp.float32),
            pltpu.VMEM((2, ROWS, LANE), jnp.float32),
            pltpu.SemaphoreType.DMA((ROWS // CHUNK + 8,)),
        ],
        compiler_params=pltpu.CompilerParams(vmem_limit_bytes=60 * 2**20),
        cost_estimate=pl.CostEstimate(flops=4_000_000, bytes_accessed=7_400_000, transcendentals=0),
        name="pack_edges",
    )(thickness, tracers, velocity, ocean, depth)


def ahead_y(x, edge):
    last = lanes((x.shape[0], LANE)) == LANE - 1
    a, b = pltpu.roll(x[:, :LANE], LANE - 1, 1), pltpu.roll(x[:, LANE:], LANE - 1, 1)
    return jnp.concatenate([jnp.where(last, b, a), jnp.where(last, edge, b)], 1)


def behind_y(x, edge):
    first = lanes((x.shape[0], LANE)) == 0
    a, b = pltpu.roll(x[:, :LANE], 1, 1), pltpu.roll(x[:, LANE:], 1, 1)
    return jnp.concatenate([jnp.where(first, edge, a), jnp.where(first, a, b)], 1)


def above(load, edge, r, tall=8):
    if (r + 1) * tall < ROWS:
        return load(tall * r + 1)
    return jnp.where(sublanes((tall, COLS)) == tall - 1, edge, pltpu.roll(load(tall * r), tall - 1, 0))


def upwind(speed, here, ahead):
    return speed * jnp.where(speed > 0.0, here, ahead)


def advect_kernel(first, *refs):
    if first == 0:
        (t_hbm, v_hbm, ocean_hbm, row_even, row_odd, col_even, col_odd, depth_hbm, out_hbm, send_ref,
         t_ref, v_ref, out_ref, ocean_ref, rows_in, cols_in, w_x, w_y, before_y, edges, sems, small_sems,
         depth_ref, total, flux, ext, thick) = refs
    else:
        (t_hbm, v_hbm, ocean_hbm, row_even, row_odd, col_even, col_odd, _, out_hbm,
         t_ref, v_ref, out_ref, ocean_ref, rows_in, cols_in, w_x, w_y, before_y, edges, sems, small_sems) = refs
    odd_x, odd_y = lax.axis_index("bx") % 2, lax.axis_index("by") % 2
    row_lo, row_hi = rows_in.at[0], rows_in.at[1]
    small = [
        (ocean_hbm, ocean_ref),
        (row_even, rows_in.at[1 - odd_x]),
        (row_odd, rows_in.at[odd_x]),
        (col_even, cols_in.at[1 - odd_y]),
        (col_odd, cols_in.at[odd_y]),
    ]
    if first == 0:
        small += [(depth_hbm, depth_ref)]
    small = [pltpu.make_async_copy(a, b, small_sems.at[i]) for i, (a, b) in enumerate(small)]

    def tracers_in(k):
        return pltpu.make_async_copy(t_hbm.at[first : first + 2, k], t_ref.at[k], sems.at[0, k])

    def velocity_in(k):
        return pltpu.make_async_copy(v_hbm.at[:, k], v_ref.at[k], sems.at[1, k])

    def tracers_out(k):
        return pltpu.make_async_copy(out_ref.at[k], out_hbm.at[first : first + 2, k], sems.at[2, k])

    for copy in small:
        copy.start()
    for k in range(LEVELS):
        tracers_in(k).start()
        velocity_in(k).start()
    for copy in small:
        copy.wait()
    even = lanes((8, LANE)) % 2 == 0
    load_wet = lambda at: ocean_ref[at : at + 8, :].astype(jnp.float32)
    for r in range(TILES):
        rows = pl.ds(8 * r, 8)
        edge = jnp.where(even, cols_in[0, rows, :], cols_in[1, rows, :])
        for k in range(LEVELS):
            for i, slot in enumerate((first * LEVELS + k, (first + 1) * LEVELS + k, SPEED + k)):
                edges[k, i, rows, :] = pltpu.roll(edge, (LANE - 2 * slot) % LANE, 1)
        here = load_wet(8 * r)
        wet_edge = pltpu.roll(edge, LANE - 2 * WET, 1)
        w_x[rows, :] = here * above(load_wet, row_hi[WET : WET + 1, :], r)
        w_y[rows, :] = here * ahead_y(here, wet_edge)
        before_y[rows, :] = here[:, :LANE] * wet_edge
        if first == 0:
            total[rows, :] = jnp.zeros((8, COLS), jnp.float32)
    w_before = load_wet(0)[0:1, :] * row_lo[WET : WET + 1, :]
    if first == 0:
        flux[...] = jnp.zeros((8, COLS), jnp.float32)
        line = rows_in[1 - odd_x, THICK : THICK + 1, :]
        for k in range(LEVELS):
            thick[k : k + 1, :] = jnp.broadcast_to(line[:, k : k + 1], (1, COLS))

    def level(k, _):
        tracers_in(k).wait()
        velocity_in(k).wait()
        u_before = row_lo[pl.ds(SPEED + k, 1), :] * w_before
        into_x = [upwind(u_before, row_lo[pl.ds((first + t) * LEVELS + k, 1), :], t_ref[k, t, 0:1, :]) for t in range(2)]
        carry, out_x = list(into_x), [None, None]
        if first == 0:
            depth = thick[pl.ds(k, 1), :]
        for r in range(ROWS // TALL):
            rows = pl.ds(TALL * r, TALL)
            u = v_ref[k, 0, rows, :] * w_x[rows, :]
            v = v_ref[k, 1, rows, :] * w_y[rows, :]
            v_before = edges[k, 2, rows, :] * before_y[rows, :]
            new = []
            for t in range(2):
                load = lambda at: t_ref[k, t, at : at + TALL, :]
                slot = (first + t) * LEVELS + k
                c = load(TALL * r)
                c_edge = edges[k, t, rows, :]
                here_x = upwind(u, c, above(load, row_hi[pl.ds(slot, 1), :], r, TALL))
                turned = pltpu.roll(here_x, 1, 0)
                past_x = jnp.where(sublanes((TALL, COLS)) == 0, carry[t], turned)
                carry[t] = turned[0:1, :]
                if r == ROWS // TALL - 1:
                    out_x[t] = here_x[TALL - 1 :, :]
                here_y = upwind(v, c, ahead_y(c, c_edge))
                past_y = behind_y(here_y, upwind(v_before, c_edge, c[:, :LANE]))
                value = (c - (here_x - past_x)) - (here_y - past_y)
                out_ref[k, t, rows, :] = value
                new.append(value)
            if first == 0:
                total[rows, :] = total[rows, :] + depth * (0.2 * new[0] - 0.8 * new[1])
        if first == 0:
            flux[0:1, :] = flux[0:1, :] + depth * (0.2 * into_x[0] - 0.8 * into_x[1])
            flux[1:2, :] = flux[1:2, :] + depth * (0.2 * out_x[0] - 0.8 * out_x[1])
        tracers_out(k).start()
        return 0

    lax.fori_loop(0, LEVELS, level, 0)

    if first == 0:
        row = sublanes((4, COLS))
        ext[0, 0:4, :] = row_lo[PART:COEF, :] - jnp.where(row == 3, flux[0:1, :], 0.0)
        ext[0, ROWS + 4 :, :] = row_hi[PART:COEF, :] + jnp.where(row == 0, flux[1:2, :], 0.0)
        ext[1, 0:4, :] = row_lo[COEF:EDGE, :]
        ext[1, ROWS + 4 :, :] = row_hi[COEF:EDGE, :]
        for r in range(TILES):
            rows = pl.ds(8 * r, 8)
            here = load_wet(8 * r)
            ext[0, 8 * r + 4 : 8 * r + 12, :] = total[rows, :] * here
            ext[1, 8 * r + 4 : 8 * r + 12, :] = coefficient(depth_ref[rows, :], here)
        for j in range(8):
            at = 16 * j
            send_ref[j, 0:22, :] = ext[0, at + 1 : at + 23, :]
            send_ref[j, 22:44, :] = ext[1, at + 1 : at + 23, :]
            line = jnp.zeros((1, LANE), jnp.float32)
            halves = [line, line]
            if j in (0, 7):
                for i in range(3):
                    factors = row_lo[EDGE + 5 + i : EDGE + 6 + i, :LANE] if j == 0 else row_hi[EDGE + i : EDGE + 1 + i, :LANE]
                    at = 32 * (i if j == 0 else 3 + i)
                    halves[at // LANE] = halves[at // LANE] + (pltpu.roll(factors, at % LANE, 1) if at % LANE else factors)
            send_ref[j, 44:45, :] = jnp.concatenate(halves, 1)
            send_ref[j, 45:48, :] = jnp.zeros((3, COLS), jnp.float32)
    for k in range(LEVELS):
        tracers_out(k).wait()


def advect(first, tracers, velocity, ocean, row_even, row_odd, col_even, col_odd, extra):
    ins = [HBM] * 3 + [ANY] * 4
    operands = [tracers, velocity, ocean, row_even, row_odd, col_even, col_odd]
    out_specs = [HBM]
    out_shape = [f32(TRACERS, LEVELS, ROWS, COLS)]
    block = pltpu.VMEM((ROWS, COLS), jnp.float32)
    narrow = pltpu.VMEM((ROWS, LANE), jnp.float32)
    scratch = [
        pltpu.VMEM((LEVELS, 2, ROWS, COLS), jnp.float32),
        pltpu.VMEM((LEVELS, 2, ROWS, COLS), jnp.float32),
        pltpu.VMEM((LEVELS, 2, ROWS, COLS), jnp.float32),
        pltpu.VMEM((ROWS, COLS), jnp.int32),
        pltpu.VMEM((2, MESSAGE, COLS), jnp.float32),
        pltpu.VMEM((2, ROWS, LANE), jnp.float32),
        block,
        block,
        narrow,
        pltpu.VMEM((LEVELS, 3, ROWS, LANE), jnp.float32),
        pltpu.SemaphoreType.DMA((3, LEVELS)),
        pltpu.SemaphoreType.DMA((8,)),
    ]
    aliases = {}
    if first == 0:
        ins = ins + [HBM]
        operands = operands + [extra]
        out_specs.append(VMEM)
        out_shape.append(f32(8, 48, COLS))
        scratch += [
            block,
            block,
            pltpu.VMEM((8, COLS), jnp.float32),
            pltpu.VMEM((2, ROWS + 8, COLS), jnp.float32),
            pltpu.VMEM((16, COLS), jnp.float32),
        ]
    else:
        aliases = {len(operands): 0}
        ins = ins + [HBM]
        operands = operands + [extra]
    return pl.pallas_call(
        functools.partial(advect_kernel, first),
        in_specs=ins,
        out_specs=out_specs,
        out_shape=out_shape,
        scratch_shapes=scratch,
        input_output_aliases=aliases,
        compiler_params=pltpu.CompilerParams(vmem_limit_bytes=(LIMA if first == 0 else LIMB) * 2**20),
        cost_estimate=pl.CostEstimate(flops=24_000_000, bytes_accessed=9_400_000, transcendentals=0),
        name="advect_forcing" if first == 0 else "advect_rest",
    )(*operands)


def insert_kernel(_, tops, out_hbm, most, sem):
    most[...] = jnp.broadcast_to(jnp.max(tops[...], axis=0)[0:1, :][None], most.shape)
    copy = pltpu.make_async_copy(most, out_hbm.at[:, 45:46, :LANE], sem.at[0])
    copy.start()
    copy.wait()


def insert(parcels, tops):
    return pl.pallas_call(
        insert_kernel,
        in_specs=[HBM, VMEM],
        out_specs=HBM,
        out_shape=f32(8, 48, COLS),
        scratch_shapes=[pltpu.VMEM((8, 1, LANE), jnp.float32), pltpu.SemaphoreType.DMA((1,))],
        input_output_aliases={0: 0},
        compiler_params=pltpu.CompilerParams(vmem_limit_bytes=60 * 2**20),
        cost_estimate=pl.CostEstimate(flops=1000, bytes_accessed=100_000, transcendentals=0),
        name="insert_maximum",
    )(parcels, tops)


NEAR = ((1, 0, 0.5), (-1, 0, 0.5), (0, 1, 0.5), (0, -1, 0.5), (1, 1, 0.125), (1, -1, 0.125), (-1, 1, 0.125), (-1, -1, 0.125))
PADDED = WIDE + LANE


def solve_kernel(got_ref, out_ref, h_ref, resid_ref, answer_ref, weight, buffers):
    here = slice(8, 8 + EXT)

    def spread():
        field = buffers[0, here, :]
        buffers[1, here, :] = pltpu.roll(field, PADDED - 1, 1)
        buffers[2, here, :] = pltpu.roll(field, 1, 1)

    def near(rows, cols, block):
        return buffers[{0: 0, 1: 1, -1: 2}[cols], 8 + rows : 8 + rows + EXT, block]

    def block_at(c):
        return pl.ds(c * COLS, COLS)

    for n in range(3):
        for rows in (slice(0, 16), slice(EXT, 16 + EXT)):
            buffers[n, rows, :] = jnp.zeros((16, PADDED), jnp.float32)
    buffers[0, 16:EXT, WIDE:] = jnp.zeros((EXT - 16, LANE), jnp.float32)
    for row in (0, EXT - 1):
        resid_ref[row : row + 1, :] = jnp.zeros((1, WIDE), jnp.float32)
    for j in range(8):
        cols = pl.ds(j * COLS, COLS)
        resid_ref[1:23, cols] = got_ref[j, 0:22, :]
        buffers[0, 9:31, cols] = got_ref[j, 22:44, :]
    lane, tile = lanes((8, LANE)), sublanes((8, LANE))
    group, row = lanes((8, COLS)), sublanes((8, COLS))
    used = (row >= 1) & (row <= 6) & (group >= 32 * (row - 1)) & (group <= 32 * (row - 1) + LEVELS)
    for j in range(7):
        pairs = got_ref[j, 44:45, :] * pltpu.roll(got_ref[j + 1, 44:45, :], COLS - 16, 1)
        flux = jnp.sum(jnp.where(used, pairs, 0.0), axis=1, keepdims=True)
        for rows, there in ((pl.ds(0, 8), tile < 4), (pl.ds(16, 8), tile >= 4)):
            last = pl.ds((j + 1) * COLS - LANE, LANE)
            after = pl.ds((j + 1) * COLS, LANE)
            resid_ref[rows, last] = resid_ref[rows, last] - jnp.where(there & (lane == LANE - 1), flux, 0.0)
            resid_ref[rows, after] = resid_ref[rows, after] + jnp.where(there & (lane == 0), flux, 0.0)
    most = got_ref[0, 45:46, 0:1]
    for j in range(1, 8):
        most = jnp.maximum(most, got_ref[j, 45:46, 0:1])
    lam_max = 0.5 + 10.0 * most
    theta = (lam_max + 0.5) / 2.0
    delta = (lam_max - 0.5) / 2.0
    sigma = theta / delta
    spread()

    def weigh(c, _):
        block = block_at(c)
        h = near(0, 0, block)
        h_ref[:, block] = h
        for n, (a, b, w) in enumerate(NEAR):
            weight[n, :, block] = w * (h + near(a, b, block))
        return 0

    for c in range(WIDE // COLS):
        weigh(c, 0)
    direction = resid_ref[...] / theta
    buffers[0, here, :WIDE] = direction
    answer_ref[...] = direction

    def step(_, rho):
        spread()
        rho_next = 1.0 / (2.0 * sigma - rho)
        keep, add = rho_next * rho, 2.0 * rho_next / delta

        def update(c, _):
            block = block_at(c)
            direction = near(0, 0, block)
            applied = 0.5 * direction
            for n, (a, b, _) in enumerate(NEAR):
                applied = applied + weight[n, :, block] * (direction - near(a, b, block))
            resid = jnp.where(h_ref[:, block] > 0.0, resid_ref[:, block] - applied, 0.0)
            resid_ref[:, block] = resid
            direction = keep * direction + add * resid
            buffers[0, here, block] = direction
            answer_ref[:, block] = answer_ref[:, block] + direction
            return 0

        for c in range(WIDE // COLS):
            update(c, 0)
        return rho_next

    lax.fori_loop(0, ITERS, step, 1.0 / sigma)
    out_ref[...] = answer_ref[4:20, :]


def solve(got):
    wide = pltpu.VMEM((EXT, WIDE), jnp.float32)
    return pl.pallas_call(
        solve_kernel,
        in_specs=[VMEM],
        out_specs=VMEM,
        out_shape=f32(16, WIDE),
        scratch_shapes=[
            wide,
            wide,
            wide,
            pltpu.VMEM((8, EXT, WIDE), jnp.float32),
            pltpu.VMEM((3, EXT + 16, PADDED), jnp.float32),
        ],
        compiler_params=pltpu.CompilerParams(vmem_limit_bytes=60 * 2**20),
        cost_estimate=pl.CostEstimate(flops=6_000_000, bytes_accessed=600_000, transcendentals=0),
        name="chebyshev",
    )(got)


def exchange(x, axis, odd):
    count = lax.axis_size(axis)
    pairs = []
    for i in range(odd, count - 1, 2):
        pairs += [(i, i + 1), (i + 1, i)]
    return lax.ppermute(x, axis, pairs)


def shards(tracers, velocity, ocean, thickness, depth):
    row_even, row_odd, col_even, col_odd, top = pack(thickness, tracers, velocity, ocean, depth)
    from_row_odd, from_col_odd = exchange(row_odd, "bx", 1), exchange(col_odd, "by", 1)
    halos = (exchange(row_even, "bx", 0), from_row_odd, exchange(col_even, "by", 0), from_col_odd)
    tops = lax.all_to_all(top, "bx", split_axis=0, concat_axis=0, tiled=True)
    part, parcels = advect(0, tracers, velocity, ocean, *halos, depth)
    got = lax.all_to_all(insert(parcels, tops), "by", split_axis=0, concat_axis=0, tiled=True)
    new_tracers = advect(2, tracers, velocity, ocean, *halos, part)[0]
    return new_tracers, solve(got)


def solution(mesh):
    return jax.shard_map(
        shards,
        mesh=mesh,
        in_specs=(
            P(None, None, "bx", "by"),
            P(None, None, "bx", "by"),
            P("bx", "by"),
            P(),
            P("bx", "by"),
        ),
        out_specs=(P(None, None, "bx", "by"), P(("bx", "by"), None)),
        check_vma=False,
    )
```
